32 devices in a mesh: img: 8 (over z, x), band: 4 (over y, core).
Axes of the slice: x: 2, y: 2, z: 4, core: 2. Of those that a mesh axis runs over, the one named last changes fastest.
Arguments:
- image: bfloat16 [32, 16, 14, 256], P('img', 'band'), may hold values from -6 to 6
- conv_weight: bfloat16 [2304, 256], replicated, may hold values from -0.125 to 0.125
- gn_gain: float32 [256], replicated, may hold values from 0.5 to 1.5
- gn_bias: float32 [256], replicated, may hold values from -3 to 3
- embed_weight: bfloat16 [256, 768], replicated, may hold values from -0.5 to 0.5
- embed_bias: float32 [768], replicated, may hold values from -2 to 2
- ln1_gain: float32 [768], replicated, may hold values from 0.5 to 1.5
- ln1_bias: float32 [768], replicated, may hold values from -2 to 2
- qkv_weight: bfloat16 [768, 2304], replicated, may hold values from -0.21875 to 0.21875
- query_bias: float32 [768], replicated, may hold values from -2 to 2
- value_bias: float32 [768], replicated, may hold values from -2 to 2
- out_weight: bfloat16 [768, 768], replicated, may hold values from -0.875 to 0.875
- out_bias: float32 [768], replicated, may hold values from -2 to 2
- ln2_gain: float32 [768], replicated, may hold values from 0.5 to 1.5
- ln2_bias: float32 [768], replicated, may hold values from -2 to 2
- up_weight: bfloat16 [768, 3072], replicated, may hold values from -0.21875 to 0.21875
- up_bias: float32 [3072], replicated, may hold values from -3 to 3
- down_weight: bfloat16 [3072, 768], replicated, may hold values from -0.21875 to 0.21875
- down_bias: float32 [768], replicated, may hold values from -2 to 2
- text_embed: bfloat16 [32, 32, 768], P(('img', 'band')), may hold values from -6 to 6
- text_len: int32 [32], P(('img', 'band')), may hold values from 1 to 32, 640 in all
- cotangent: bfloat16 [32, 228, 768], P(('img', 'band')), may hold values from -14 to 14
Outputs:
- encoded: bfloat16 [32, 228, 768], P(('img', 'band'))
- image_grad: float32 [32, 16, 14, 256], P('img', 'band')
- text_grad: float32 [32, 32, 768], P(('img', 'band'))
- grad_conv_weight: float32 [2304, 256], P('img', 'band')
- grad_gn_gain: float32 [256], P('img')
- grad_gn_bias: float32 [256], P('img')
- grad_embed_weight: float32 [256, 768], P('img', 'band')
- grad_embed_bias: float32 [768], P('img')
- grad_ln1_gain: float32 [768], P('img')
- grad_ln1_bias: float32 [768], P('img')
- grad_qkv_weight: float32 [768, 2304], P('img', 'band')
- grad_query_bias: float32 [768], P('img')
- grad_value_bias: float32 [768], P('img')
- grad_out_weight: float32 [768, 768], P('band', 'img')
- grad_out_bias: float32 [768], P('img')
- grad_ln2_gain: float32 [768], P('img')
- grad_ln2_bias: float32 [768], P('img')
- grad_up_weight: float32 [768, 3072], P('img', 'band')
- grad_up_bias: float32 [3072], P('img')
- grad_down_weight: float32 [3072, 768], P('band', 'img')
- grad_down_bias: float32 [768], P('img')
The draws below stay inside these ranges and needn't reach their ends.
Inputs may be any that keep to these rules, and one draw needn't show every extreme that they name: `text_len`: live text slots of each example; the largest is 32 in every draw.
All inputs are finite; a program needn't handle non-finite values. No bound on the sum of `text_len` on one device may be relied on, other than what follows from the above.
Results may differ from the reference program's by a relative error of at most 0.013.
Values may be sent and summed in bfloat16 or wider, within the bound.
A program may use at most 128 MiB of HBM per device.

```python
import math
import jax
import jax.numpy as jnp
import numpy as np
from jax import lax

D = 768
HEADS = 12
HD = 64
FF = 3072
CH = 256
GROUPS = 32
GRID = 14
TEXT = 32
IMG_DEV = 4
PATCHES = 196
SEQ = 228
PAD_ROWS = 16
IMAGES = 32


def draw_cotangent(key, part):
    noise_key = jax.random.fold_in(key, 11)
    common_key = jax.random.fold_in(key, 23)
    noise = jnp.clip(jax.random.normal(noise_key, (IMAGES, SEQ, D), jnp.float32), -4.0, 4.0)
    lowest = 0.4
    highest = 2.0
    common = jnp.clip(jax.random.normal(common_key, (IMAGES, 1, D), jnp.float32), -4.0, 4.0)
    position = jnp.arange(SEQ)
    row_index = (position // GRID).astype(jnp.float32)
    factor = jnp.where(position < PATCHES, lowest + (highest - lowest) * row_index / (GRID - 1), 1.0)
    values = factor[None, :, None] * (0.6 * noise + 0.8 * common)
    return values.astype(jnp.bfloat16)


def block_levels(rng, shape, cuts, smallest, high):
    level = 1.0
    for axis_at, parts in cuts:
        steps = jax.random.uniform(jax.random.fold_in(jax.random.fold_in(rng, 6), axis_at), (parts,), jnp.float32, smallest / len(cuts), high / len(cuts))
        level = level * jnp.repeat(jnp.exp(steps), shape[axis_at] // parts).reshape((-1,) + (1,) * (len(shape) - 1 - axis_at))
    return level


def split_up(count, total, limit, skew):
    weights = [(1 << 20) // math.isqrt(standing ** skew) + 1 for standing in range(2, count + 1)]
    surplus, counts = total - limit - (count - 1), [1] * (count - 1)
    while surplus > 0:
        movable = [i for i in range(count - 1) if counts[i] < limit]
        pool, budget = sum([weights[i] for i in movable]), surplus
        for i in movable:
            extra = min(limit - counts[i], max(1, budget * weights[i] // pool), surplus)
            counts[i] = counts[i] + extra
            surplus = surplus - extra
    return np.array([limit] + counts)


def ragged_sizes(key, count, total, limit, lean):
    if count == 2:
        one = jax.random.randint(key, (), max(1, total - limit), min(limit, total - 1) + 1)
        return jnp.stack([one, total - one])
    sizes = jnp.asarray(split_up(count, total, limit, lean), jnp.int32)
    couples = (count - 1) // 2
    donor, receiver = sizes[1:1 + 2 * couples:2], sizes[2:2 + 2 * couples:2]
    margin = jnp.minimum(donor - 1, limit - receiver)
    shifted = jax.random.randint(jax.random.fold_in(key, 1), (couples,), 0, 1 << 20) % (margin + 1)
    sizes = sizes.at[1:1 + 2 * couples:2].set(donor - shifted).at[2:2 + 2 * couples:2].set(receiver + shifted)
    return sizes[jax.random.permutation(jax.random.fold_in(key, 2), count)]


def normal_values(rng, extent, deviation, bound, cuts=(), kind=jnp.bfloat16):
    values = jax.random.normal(rng, extent, jnp.float32) * deviation
    if len(cuts) > 0:
        values = block_levels(rng, extent, cuts, -0.22, 0.18) * values
    return jnp.clip(values, min=-bound, max=bound).astype(kind)


def setup_inputs(seed: int = 0) -> dict:
    seeds = jax.random.split(jax.random.key(seed), 23)
    return {
        "image": normal_values(seeds[0], (IMAGES, PAD_ROWS, GRID, CH), 1.0, 6.0, ((0, 8), (1, 4))),
        "conv_weight": normal_values(seeds[1], (9 * CH, CH), (9 * CH) ** -0.5, 0.125),
        "gn_gain": jnp.clip(jax.random.uniform(seeds[2], (CH,), jnp.float32, 0.5, 1.5), 0.5, 1.5),
        "gn_bias": normal_values(seeds[3], (CH,), 0.5, 3.0, (), jnp.float32),
        "embed_weight": normal_values(seeds[4], (CH, D), (CH // 2) ** -0.5, 0.5),
        "embed_bias": normal_values(seeds[5], (D,), 0.3, 2.0, (), jnp.float32),
        "ln1_gain": jnp.clip(jax.random.uniform(seeds[6], (D,), jnp.float32, 0.5, 1.5), 0.5, 1.5),
        "ln1_bias": normal_values(seeds[7], (D,), 0.3, 2.0, (), jnp.float32),
        "qkv_weight": normal_values(seeds[8], (D, 3 * D), D ** -0.5, 0.21875),
        "query_bias": normal_values(seeds[9], (D,), 0.3, 2.0, (), jnp.float32),
        "value_bias": normal_values(seeds[10], (D,), 0.3, 2.0, (), jnp.float32),
        "out_weight": normal_values(seeds[11], (D, D), (D // 16) ** -0.5, 0.875),
        "out_bias": normal_values(seeds[12], (D,), 0.3, 2.0, (), jnp.float32),
        "ln2_gain": jnp.clip(jax.random.uniform(seeds[13], (D,), jnp.float32, 0.5, 1.5), 0.5, 1.5),
        "ln2_bias": normal_values(seeds[14], (D,), 0.3, 2.0, (), jnp.float32),
        "up_weight": normal_values(seeds[15], (D, FF), D ** -0.5, 0.21875),
        "up_bias": normal_values(seeds[16], (FF,), 0.5, 3.0, (), jnp.float32),
        "down_weight": normal_values(seeds[17], (FF, D), (FF // 4) ** -0.5, 0.21875),
        "down_bias": normal_values(seeds[18], (D,), 0.3, 2.0, (), jnp.float32),
        "text_embed": normal_values(seeds[19], (IMAGES, TEXT, D), 1.0, 6.0, ((0, 32),)),
        "text_len": ragged_sizes(seeds[20], IMAGES, (5 * IMAGES * TEXT) // 8, TEXT, 2).astype(jnp.int32),
        "cotangent": draw_cotangent(jax.random.fold_in(seeds[22], 71), 0),
    }


@jax.custom_vjp
def low(v):
    return lax.optimization_barrier(v.astype(jnp.bfloat16)).astype(jnp.float32)

@jax.custom_vjp
def low_back(v):
    return v

def low_keep(v):
    return (low(v), None)

def low_pass(kept, grad):
    return (grad,)

def back_keep(v):
    return (v, None)

def back_low(kept, grad):
    return (low(grad),)
low.defvjp(low_keep, low_pass)
low_back.defvjp(back_keep, back_low)

def matmul(left, right):
    return jnp.dot(left, right, precision=lax.Precision.HIGHEST, preferred_element_type=jnp.float32)

def layer_norm(values, gain, shift):
    mean = lax.optimization_barrier(jnp.mean(values, -1, keepdims=True))
    cent = values - mean
    var = lax.optimization_barrier(jnp.mean(cent * cent, -1, keepdims=True))
    return cent * lax.rsqrt(var + 1e-06) * gain + shift

def forward(params, image, text, lens):
    conv_w, gn_g, gn_b, emb_w, emb_b, ln1_g, ln1_b, qkv_w, q_b, v_b, out_w, out_b, ln2_g, ln2_b, up_w, up_b, down_w, down_b = params
    count = image.shape[0]
    channels = conv_w.shape[1]
    wmean = lax.optimization_barrier(jnp.mean(conv_w, 0))
    wcent = conv_w - wmean
    stand = low(wcent * lax.rsqrt(lax.optimization_barrier(jnp.mean(wcent * wcent, 0)) + 1e-05))
    kernel = stand.reshape(3, 3, channels, channels)
    pixels = image[:, :GRID]
    feat = lax.conv_general_dilated(pixels, kernel, (1, 1), ((1, 1), (1, 1)), dimension_numbers=('NHWC', 'HWIO', 'NHWC'), precision=lax.Precision.HIGHEST, preferred_element_type=jnp.float32)
    feat = low_back(feat)
    per_group = channels // GROUPS
    grouped = feat.reshape(count, GRID, GRID, GROUPS, per_group)
    entries = GRID * GRID * per_group
    gmean = lax.optimization_barrier(jnp.sum(grouped, (1, 2, 4), keepdims=True)) / entries
    gvar = lax.optimization_barrier(jnp.sum(grouped * grouped, (1, 2, 4), keepdims=True)) / entries - gmean * gmean
    zhat = ((grouped - gmean) * lax.rsqrt(gvar + 1e-05)).reshape(count, GRID, GRID, channels)
    active = low_back(low(jax.nn.gelu(zhat * gn_g + gn_b, approximate=False)))
    patches = low_back(low(matmul(active.reshape(-1, channels), emb_w) + emb_b))
    stream = jnp.concatenate([patches.reshape(count, PATCHES, D), text], 1)
    hidden = low(layer_norm(stream, ln1_g, ln1_b)).reshape(-1, D)
    proj = matmul(hidden, qkv_w)
    query = low(low_back(proj[:, :D] + q_b)).reshape(count, SEQ, HEADS, HD)
    key = low(low_back(proj[:, D:2 * D])).reshape(count, SEQ, HEADS, HD)
    value = low(low_back(proj[:, 2 * D:] + v_b)).reshape(count, SEQ, HEADS, HD)
    scores = low_back(jnp.einsum('bqhd,bkhd->bhqk', query, key, precision=lax.Precision.HIGHEST) * HD ** (-0.5))
    live = jnp.arange(SEQ)[None, :] < (PATCHES + lens)[:, None]
    scores = jnp.where(live[:, None, None, :], scores, -1000000000.0)
    probs = jax.nn.softmax(scores, -1)
    mixed = jnp.einsum('bhqk,bkhd->bqhd', low(probs), value, precision=lax.Precision.HIGHEST)
    mixed = low_back(low(mixed)).reshape(-1, D)
    attn = low_back(matmul(mixed, out_w) + out_b).reshape(count, SEQ, D)
    mid = stream + attn
    hidden2 = low(layer_norm(mid, ln2_g, ln2_b)).reshape(-1, D)
    pre = low_back(matmul(hidden2, up_w) + up_b)
    act = low(jax.nn.gelu(pre, approximate=False))
    return mid + (matmul(act, down_w) + down_b).reshape(count, SEQ, D)

def reference(image, conv_weight, gn_gain, gn_bias, embed_weight, embed_bias, ln1_gain, ln1_bias, qkv_weight, query_bias, value_bias, out_weight, out_bias, ln2_gain, ln2_bias, up_weight, up_bias, down_weight, down_bias, text_embed, text_len, cotangent):
    params = tuple((p.astype(jnp.float32) for p in (conv_weight, gn_gain, gn_bias, embed_weight, embed_bias, ln1_gain, ln1_bias, qkv_weight, query_bias, value_bias, out_weight, out_bias, ln2_gain, ln2_bias, up_weight, up_bias, down_weight, down_bias)))
    batches = IMAGES // IMG_DEV
    images = image.astype(jnp.float32).reshape(batches, IMG_DEV, PAD_ROWS, GRID, CH)
    texts = text_embed.astype(jnp.float32).reshape(batches, IMG_DEV, TEXT, D)
    lens = text_len.astype(jnp.int32).reshape(batches, IMG_DEV)
    cots = cotangent.astype(jnp.float32).reshape(batches, IMG_DEV, SEQ, D)

    def one_batch(carry, pieces):
        pix, txt, lengths, cot = pieces
        out, pull = jax.vjp(lambda p, a, b: forward(p, a, b, lengths), params, pix, txt)
        gparams, gpix, gtxt = pull(cot)
        carry = jax.tree.map(lambda c, g: c + g, carry, gparams)
        return (carry, (out.astype(jnp.bfloat16), gpix, gtxt))
    zeros = jax.tree.map(jnp.zeros_like, params)
    grads, (outs, gimage, gtext) = lax.scan(one_batch, zeros, (images, texts, lens, cots))
    encoded = outs.reshape(IMAGES, SEQ, D)
    image_grad = gimage.reshape(IMAGES, PAD_ROWS, GRID, CH)
    text_grad = gtext.reshape(IMAGES, TEXT, D)
    return (encoded, image_grad, text_grad, grads[0], grads[1], grads[2], grads[3], grads[4], grads[5], grads[6], grads[7], grads[8], grads[9], grads[10], grads[11], grads[12], grads[13], grads[14], grads[15], grads[16], grads[17])
```

```python
import functools

import jax
import jax.numpy as jnp
from jax import lax
from jax.experimental import pallas as pl
from jax.experimental.pallas import tpu as pltpu
from jax.sharding import PartitionSpec as P

D = 768
HEADS = 12
HD = 64
GROUPS = 32
GRID = 14
TEXT = 32
PATCHES = 196


MESH_ID = pl.DeviceIdType.MESH
HALF = jnp.bfloat16
FULL = jnp.float32
TOK = 256


def bit_of(value, bit):
    return lax.rem(lax.div(value, bit), 2)


def flip(value, bit):
    return value + bit * (1 - 2 * bit_of(value, bit))


def partner(label):
    axis, bit = label
    img, band = lax.axis_index("img"), lax.axis_index("band")
    return (flip(img, bit), band) if axis == "img" else (img, flip(band, bit))


def my_bit(label):
    axis, bit = label
    return bit_of(lax.axis_index(axis), bit)


def bits(count):
    return [1 << k for k in range(count.bit_length() - 1)]


class Plan:
    def __init__(self, n_img, rows, width, lead, order):
        self.width = width
        split = [("img", k) for k in reversed(bits(n_img)) if (rows // n_img) * k % 16 == 0]
        self.rows = rows >> len(split)
        self.first = ([lead] if lead else []) + split
        rest = [("img", k) for k in bits(n_img) if ("img", k) not in split]
        ordered = [lab for lab in order if lab in self.first]
        self.order = ordered + rest + [lab for lab in order if lab not in self.first and lab[0] == "band"]
        self.shapes = []
        labels = list(self.first)
        for lab in self.order:
            if lab in labels:
                labels.remove(lab)
            self.shapes.append((2,) * len(labels) + (self.rows, width))
        self.shape = (2,) * len(self.first) + (self.rows, width)

    def scratch(self, kind):
        return [pltpu.VMEM(s, kind) for s in [self.shape] + self.shapes]


class Piece:
    def __init__(self, plan, refs, sems, slot):
        self.plan, self.buf, self.recv = plan, refs[0], refs[1:]
        self.sems, self.slot = sems, slot
        self.labels, self.cur = list(plan.first), refs[0]
        self.sent = []

    def _index(self, label, which):
        at = self.labels.index(label)
        return (slice(None),) * at + (which,)

    def start(self, stage):
        label = self.plan.order[stage]
        src = self.cur
        if label in self.labels:
            src = src.at[self._index(label, 1 - my_bit(label))]
        send, recv = self.sems
        copy = pltpu.make_async_remote_copy(
            src_ref=src,
            dst_ref=self.recv[stage],
            send_sem=send.at[self.slot + stage],
            recv_sem=recv.at[self.slot + stage],
            device_id=partner(label),
            device_id_type=MESH_ID,
        )
        copy.start()
        self.sent.append(copy)

    def finish(self, stage, out=None):
        label = self.plan.order[stage]
        self.sent[stage].wait_recv()
        mine = self.cur
        if label in self.labels:
            mine = mine[self._index(label, my_bit(label))]
            self.labels.remove(label)
        else:
            mine = mine[...]
        got = self.recv[stage]
        if out is None:
            got[...] = got[...] + mine
        else:
            out[...] = (got[...].astype(FULL) + mine.astype(FULL)).reshape(out.shape)
        self.cur = got

    def drain(self):
        for copy in self.sent:
            copy.wait_send()


def dot_tn(left, right):
    return lax.dot_general(left, right, (((0,), (0,)), ((), ())), preferred_element_type=FULL)


def grads_kernel(plans, vec_rows, *refs):
    (cot, act, hid2, dpre, dattn, mixed, hid, dqkv, win, dfeat, active, dpat, vec,
     o_down, o_up, o_out, o_qkv, o_conv, o_emb, o_vec) = refs[:20]
    rest = list(refs[20:])
    (r_cot, r_act, r_hid2, r_dpre, r_dattn, r_mixed, r_hid, r_dqkv, r_win, r_dfeat, r_active, r_dpat) = rest[:12]
    rest = rest[12:]
    core_send, core_recv, send_sem, recv_sem = rest[-4:]
    rest = rest[:-4]
    pieces = []
    slot = 0
    for plan in plans:
        count = 1 + len(plan.order)
        pieces.append(Piece(plan, rest[:count], (send_sem, recv_sem), slot))
        rest = rest[count:]
        slot += count - 1
    vec_recv = rest
    core = ("band", 1)
    links = [core, ("band", 2)] + [("img", k) for k in bits(lax.axis_size("img"))]
    barrier = pltpu.get_barrier_semaphore()
    for label in links:
        pl.semaphore_signal(barrier, inc=1, device_id=partner(label), device_id_type=MESH_ID)
    pl.semaphore_wait(barrier, len(links))
    c = my_bit(core)
    core_copies = {}

    def swap(name, at, src, dst):
        copy = pltpu.make_async_remote_copy(
            src_ref=src, dst_ref=dst, send_sem=core_send.at[at], recv_sem=core_recv.at[at],
            device_id=partner(core), device_id_type=MESH_ID)
        copy.start()
        core_copies.setdefault(name, []).append(copy)

    def swap_bands(name, at, src, dst):
        for y in range(2):
            swap(name, at + y, src.at[2 * y + 1 - c], dst.at[y])

    swap("down", 0, cot, r_cot)
    swap_bands("down", 1, act, r_act)
    swap("up", 3, hid2, r_hid2)
    swap_bands("up", 4, dpre, r_dpre)
    swap("qkv", 6, hid, r_hid)
    swap_bands("qkv", 7, dqkv, r_dqkv)
    swap("out", 9, dattn, r_dattn)
    swap_bands("out", 10, mixed, r_mixed)
    swap("conv", 12, win, r_win)
    swap("conv", 13, dfeat, r_dfeat)
    swap("emb", 14, active, r_active)
    swap("emb", 15, dpat, r_dpat)

    def arrived(name):
        for copy in core_copies[name]:
            copy.wait_recv()

    def store(piece, y, value):
        shape = piece.plan.shape
        if y is None:
            piece.buf[...] = value.astype(HALF).reshape(shape)
        else:
            piece.buf[y] = value.astype(HALF).reshape(shape[1:])

    def unit(name, left, r_left, right, r_right, parts):
        arrived(name)
        for piece, lo in parts:
            w = piece.plan.width
            for y in range(2):
                for at in range(0, w, 128):
                    wide = slice(lo + at, lo + at + 128)
                    value = dot_tn(left[...], right[2 * y + c, :, wide])
                    value += dot_tn(r_left[...], r_right[y, :, wide])
                    value = value.astype(HALF).reshape(piece.plan.shape[1:-1] + (128,))
                    lead = (y,) + (slice(None),) * (len(piece.plan.shape) - 2)
                    piece.buf[lead + (slice(at, at + 128),)] = value
            piece.start(0)

    def columns(values, width):
        total = values.shape[1]
        row = lax.broadcasted_iota(jnp.int32, (total, 2 * width), 0)
        col = lax.broadcasted_iota(jnp.int32, (total, 2 * width), 1)
        want = jnp.where(col < width, col + c * width, col + width + c * width)
        pick = jnp.where(row == want, 1.0, 0.0).astype(HALF)
        return jnp.dot(values, pick, preferred_element_type=FULL).astype(HALF)

    p_da, p_db, p_ua, p_ub, p_qa, p_qb, p_o, p_c, p_e = pieces
    half = p_da.plan.width
    unit("down", cot, r_cot, act, r_act, [(p_da, 0), (p_db, half)])
    unit("up", hid2, r_hid2, dpre, r_dpre, [(p_ua, 0), (p_ub, half)])
    unit("qkv", hid, r_hid, dqkv, r_dqkv, [(p_qa, 0), (p_qb, p_qa.plan.width)])
    unit("out", dattn, r_dattn, mixed, r_mixed, [(p_o, 0)])
    arrived("conv")
    mine, theirs = columns(dfeat[...], 64), columns(r_dfeat[...], 64)
    store(p_c, None, dot_tn(win[...], mine) + dot_tn(r_win[...], theirs))
    p_c.start(0)
    arrived("emb")
    mine, theirs = columns(dpat[...], 192), columns(r_dpat[...], 192)
    store(p_e, None, dot_tn(active[...], mine) + dot_tn(r_active[...], theirs))
    p_e.start(0)
    o_vec[...] = vec[...]
    vec_copies = []

    def vec_start(stage):
        copy = pltpu.make_async_remote_copy(
            src_ref=vec_recv[2 * stage], dst_ref=vec_recv[2 * stage + 1],
            send_sem=send_sem.at[slot + stage], recv_sem=recv_sem.at[slot + stage],
            device_id=partner(links[stage]), device_id_type=MESH_ID)
        copy.start()
        vec_copies.append(copy)

    vec_recv[0][...] = vec[...]
    vec_start(0)
    outs = {id(p_da): (o_down, 0), id(p_db): (o_down, half), id(p_ua): (o_up, 0), id(p_ub): (o_up, half),
            id(p_qa): (o_qkv, 0), id(p_qb): (o_qkv, p_qa.plan.width), id(p_o): (o_out, 0), id(p_c): (o_conv, 0), id(p_e): (o_emb, 0)}
    deepest = max(len(p.plan.order) for p in pieces)
    for stage in range(max(deepest, len(links))):
        for piece in pieces:
            if stage < len(piece.plan.order):
                last = stage == len(piece.plan.order) - 1
                ref, lo = outs[id(piece)]
                piece.finish(stage, ref.at[:, pl.ds(lo, piece.plan.width)] if last else None)
                if not last:
                    piece.start(stage + 1)
        if stage < len(links):
            vec_copies[stage].wait_recv()
            total = vec_recv[2 * stage][...] + vec_recv[2 * stage + 1][...]
            if stage == len(links) - 1:
                o_vec[...] = total
            else:
                vec_recv[2 * stage + 2][...] = total
                vec_start(stage + 1)
    for piece in pieces:
        piece.drain()
    for copy in vec_copies:
        copy.wait_send()
    for group in core_copies.values():
        for copy in group:
            copy.wait_send()


def reduce_grads(cot, act, hid2, dpre, dattn, mixed, hid, dqkv, win, dfeat, active, dpat, vec):
    n_img = lax.axis_size("img")
    y = ("band", 2)
    img_bits = [("img", k) for k in bits(n_img)]
    y_first = [y] + img_bits
    x_first = img_bits[:1] + [y] + img_bits[1:]
    tail = img_bits + [y]
    plans = [
        Plan(n_img, D, 384, y, y_first),
        Plan(n_img, D, 384, y, x_first),
        Plan(n_img, D, 384, y, y_first),
        Plan(n_img, D, 384, y, x_first),
        Plan(n_img, D, 384, y, y_first),
        Plan(n_img, D, 256, y, x_first),
        Plan(n_img, D, 256, y, y_first),
        Plan(n_img, win.shape[1], 128, None, tail),
        Plan(n_img, active.shape[1], 384, None, tail),
    ]
    outs = [(plans[0].rows, D), (plans[2].rows, D), (plans[6].rows, 256), (plans[4].rows, 640), (plans[7].rows, 128), (plans[8].rows, 384), vec.shape]
    half = lambda *s: pltpu.VMEM(s, HALF)
    scratch = [half(TOK, D), half(2, TOK, D), half(TOK, D), half(2, TOK, D), half(TOK, D), half(2, TOK, 256),
               half(TOK, D), half(2, TOK, 640), half(*win.shape), half(*dfeat.shape), half(*active.shape), half(*dpat.shape)]
    slots = 0
    for plan in plans:
        scratch += plan.scratch(HALF)
        slots += len(plan.order)
    n_links = 2 + len(img_bits)
    scratch += [pltpu.VMEM(vec.shape, FULL)] * (2 * n_links)
    slots += n_links
    scratch += [pltpu.SemaphoreType.DMA((16,)), pltpu.SemaphoreType.DMA((16,)), pltpu.SemaphoreType.DMA((slots,)), pltpu.SemaphoreType.DMA((slots,))]
    vm = pl.BlockSpec(memory_space=pltpu.VMEM)
    args = (cot, act, hid2, dpre, dattn, mixed, hid, dqkv, win, dfeat, active, dpat, vec)
    return pl.pallas_call(
        functools.partial(grads_kernel, plans, vec.shape[0]),
        out_shape=[jax.ShapeDtypeStruct(s, FULL) for s in outs],
        in_specs=[vm] * len(args),
        out_specs=[vm] * len(outs),
        scratch_shapes=scratch,
        compiler_params=pltpu.CompilerParams(collective_id=0, has_side_effects=True, vmem_limit_bytes=60 * 2**20),
    )(*args)


def padded(cells, sides, width):
    for axis, dim in sides:
        count = lax.axis_size(axis)
        ends = count - 1
        head = lax.slice_in_dim(cells, 0, width, axis=dim)
        tail = lax.slice_in_dim(cells, cells.shape[dim] - width, cells.shape[dim], axis=dim)
        cells = jnp.concatenate(
            [
                lax.ppermute(tail, axis, [(i, (i + 1) % count) for i in range(ends)]),
                cells,
                lax.ppermute(head, axis, [((i + 1) % count, i) for i in range(ends)]),
            ],
            axis=dim,
        )
    return cells


def matmul(left, right):
    return jnp.dot(left, right, preferred_element_type=jnp.float32)


def norm_forward(values, gain, shift):
    mean = jnp.mean(values, -1, keepdims=True)
    cent = values - mean
    rstd = lax.rsqrt(jnp.mean(cent * cent, -1, keepdims=True) + 1e-06)
    normed = cent * rstd
    return (normed * gain + shift, normed, rstd)


def norm_backward(grad, normed, rstd, gain):
    scaled = grad * gain
    inner = (
        scaled
        - jnp.mean(scaled, -1, keepdims=True)
        - normed * jnp.mean(scaled * normed, -1, keepdims=True)
    )
    return (inner * rstd, jnp.sum(grad * normed, 0), jnp.sum(grad, 0))


def conv_rows(rimmed, kernel):
    return lax.conv_general_dilated(
        rimmed,
        kernel,
        (1, 1),
        ((0, 0), (1, 1)),
        dimension_numbers=("NHWC", "HWIO", "NHWC"),
        preferred_element_type=jnp.float32,
    )


def exact_gelu(values):
    return jax.nn.gelu(values, approximate=False)


def body(
    image,
    conv_weight,
    gn_gain,
    gn_bias,
    embed_weight,
    embed_bias,
    ln1_gain,
    ln1_bias,
    qkv_weight,
    query_bias,
    value_bias,
    out_weight,
    out_bias,
    ln2_gain,
    ln2_bias,
    up_weight,
    up_bias,
    down_weight,
    down_bias,
    text_embed,
    text_len,
    cotangent,
):
    half_type = jnp.bfloat16
    full_type = jnp.float32
    channels = conv_weight.shape[1]
    pixels = image
    row_start = lax.axis_index("band") * image.shape[1]
    images_here = pixels.shape[0]
    rows = pixels.shape[1]
    row_live = (row_start + jnp.arange(rows) < GRID).astype(full_type)[None, :, None, None]
    pixels = pixels * row_live.astype(half_type)
    rimmed = padded(pixels, (("band", 1),), 1)
    wfull = conv_weight.astype(full_type)
    wcent = wfull - jnp.mean(wfull, 0)
    wscale = lax.rsqrt(jnp.mean(wcent * wcent, 0) + 1e-05)
    stand_full = wcent * wscale
    kernel = stand_full.astype(half_type).reshape(3, 3, channels, channels)
    feat = conv_rows(rimmed, kernel) * row_live
    per_group = channels // GROUPS
    entries = GRID * GRID * per_group
    grouped = feat.reshape(images_here, rows, GRID, GROUPS, per_group)
    sum_one = jnp.sum(grouped, (1, 2, 4))
    sum_two = jnp.sum(grouped * grouped, (1, 2, 4))
    sum_one, sum_two = lax.psum((sum_one, sum_two), "band")
    gmean = (sum_one / entries)[:, None, None, :, None]
    gvar = (sum_two / entries)[:, None, None, :, None] - gmean * gmean
    gscale = lax.rsqrt(gvar + 1e-05)
    zgroup = (grouped - gmean) * gscale
    zhat = zgroup.reshape(images_here, rows, GRID, channels)
    normed = zhat * gn_gain + gn_bias
    stem_out, stem_pull = jax.vjp(exact_gelu, normed)
    active = (stem_out * row_live).astype(half_type)
    embedded = (matmul(active.reshape(-1, channels), embed_weight) + embed_bias).astype(half_type)
    embedded = embedded.reshape(images_here, rows, GRID, D)
    embedded = lax.all_to_all(embedded, "band", split_axis=0, concat_axis=1, tiled=True)
    full_rows = embedded.shape[1]
    patches = embedded[:, :GRID].reshape(-1, PATCHES, D)
    seqs = patches.shape[0]
    seq_len = PATCHES + TEXT
    stream = jnp.concatenate([patches.astype(full_type), text_embed.astype(full_type)], 1).reshape(
        -1, D
    )
    hidden, nhat_one, rstd_one = norm_forward(stream, ln1_gain, ln1_bias)
    hidden = hidden.astype(half_type)
    projected = matmul(hidden, qkv_weight)
    query = (projected[:, :D] + query_bias).astype(half_type).reshape(seqs, seq_len, HEADS, HD)
    key = projected[:, D : 2 * D].astype(half_type).reshape(seqs, seq_len, HEADS, HD)
    value = (projected[:, 2 * D :] + value_bias).astype(half_type).reshape(seqs, seq_len, HEADS, HD)
    live_keys = jnp.arange(seq_len)[None, :] < (PATCHES + text_len)[:, None]
    scale = HD ** (-0.5)

    def scores_of(queries, keys):
        raw = jnp.einsum("bqhd,bkhd->bhqk", queries, keys, preferred_element_type=full_type) * scale
        return jnp.where(live_keys[:, None, None, :], raw, -1000000000.0)

    scores = scores_of(query, key)
    peak = jnp.max(scores, -1, keepdims=True)
    expd = jnp.exp(scores - peak)
    total = jnp.sum(expd, -1, keepdims=True)
    probs = expd / total
    log_total = peak + jnp.log(total)
    mixed = jnp.einsum(
        "bhqk,bkhd->bqhd", probs.astype(half_type), value, preferred_element_type=full_type
    )
    mixed = mixed.astype(half_type).reshape(-1, D)
    mid = stream + matmul(mixed, out_weight) + out_bias
    hidden2, nhat_two, rstd_two = norm_forward(mid, ln2_gain, ln2_bias)
    hidden2 = hidden2.astype(half_type)
    pre = matmul(hidden2, up_weight) + up_bias
    gelu_out, gelu_pull = jax.vjp(exact_gelu, pre)
    act = gelu_out.astype(half_type)
    final = mid + matmul(act, down_weight) + down_bias
    encoded = final.astype(half_type).reshape(seqs, seq_len, D)
    grad_out = cotangent.reshape(-1, D)
    grad_full = grad_out.astype(full_type)
    g_down_b = jnp.sum(grad_full, 0)
    d_pre = gelu_pull(matmul(grad_out, down_weight.T))[0].astype(half_type)
    g_up_b = jnp.sum(d_pre.astype(full_type), 0)
    d_mid_norm, g_ln2_g, g_ln2_b = norm_backward(
        matmul(d_pre, up_weight.T), nhat_two, rstd_two, ln2_gain
    )
    d_mid = grad_full + d_mid_norm
    d_attn = d_mid.astype(half_type)
    g_out_b = jnp.sum(d_attn.astype(full_type), 0)
    d_mixed = matmul(d_attn, out_weight.T).astype(half_type).reshape(seqs, seq_len, HEADS, HD)
    probs_again = jnp.exp(scores_of(query, key) - log_total)
    d_probs = jnp.einsum("bqhd,bkhd->bhqk", d_mixed, value, preferred_element_type=full_type)
    d_value = jnp.einsum(
        "bhqk,bqhd->bkhd", probs_again.astype(half_type), d_mixed, preferred_element_type=full_type
    )
    delta = jnp.sum(d_probs * probs_again, -1, keepdims=True)
    d_scores = (probs_again * (d_probs - delta)).astype(half_type)
    d_query = jnp.einsum("bhqk,bkhd->bqhd", d_scores, key, preferred_element_type=full_type) * scale
    d_key = jnp.einsum("bhqk,bqhd->bkhd", d_scores, query, preferred_element_type=full_type) * scale
    d_qkv = jnp.concatenate(
        [d_query.reshape(-1, D), d_key.reshape(-1, D), d_value.reshape(-1, D)], 1
    ).astype(half_type)
    g_q_b = jnp.sum(d_qkv[:, :D].astype(full_type), 0)
    g_v_b = jnp.sum(d_qkv[:, 2 * D :].astype(full_type), 0)
    d_stream_norm, g_ln1_g, g_ln1_b = norm_backward(
        matmul(d_qkv, qkv_weight.T), nhat_one, rstd_one, ln1_gain
    )
    d_stream = (d_mid + d_stream_norm).reshape(seqs, seq_len, D)
    text_grad = d_stream[:, PATCHES:]
    d_patches = d_stream[:, :PATCHES].astype(half_type).reshape(seqs, GRID, GRID, D)
    d_grid = jnp.pad(d_patches, ((0, 0), (0, full_rows - GRID), (0, 0), (0, 0)))
    d_grid = lax.all_to_all(d_grid, "band", split_axis=1, concat_axis=0, tiled=True)
    flat_grad = d_grid.reshape(-1, D)
    g_emb_b = jnp.sum(flat_grad.astype(full_type), 0)
    d_active = (
        matmul(flat_grad, embed_weight.T)
        .astype(half_type)
        .reshape(images_here, rows, GRID, channels)
    )
    d_norm = stem_pull(d_active.astype(full_type))[0] * row_live
    g_gn_g = jnp.sum(d_norm * zhat, (0, 1, 2))
    g_gn_b = jnp.sum(d_norm, (0, 1, 2))
    d_hat = (d_norm * gn_gain).reshape(images_here, rows, GRID, GROUPS, per_group)
    back_one = jnp.sum(d_hat, (1, 2, 4))
    back_two = jnp.sum(d_hat * zgroup, (1, 2, 4))
    back_one, back_two = lax.psum((back_one, back_two), "band")
    d_feat = gscale * (
        d_hat
        - (back_one / entries)[:, None, None, :, None]
        - zgroup * (back_two / entries)[:, None, None, :, None]
    )
    d_feat = (d_feat.reshape(images_here, rows, GRID, channels) * row_live).astype(half_type)
    widened = jnp.pad(rimmed, ((0, 0), (0, 0), (1, 1), (0, 0)))
    flat_feat = d_feat.reshape(-1, channels)
    windows = []
    for shift_r in range(3):
        for shift_c in range(3):
            window = widened[:, shift_r : shift_r + rows, shift_c : shift_c + GRID, :].reshape(
                -1, channels
            )
            windows.append(window)
    windows = jnp.concatenate(windows, 1)
    flipped = jnp.flip(kernel, (0, 1)).transpose(0, 1, 3, 2)
    d_rim = padded(d_feat, (("band", 1),), 1)
    image_grad = conv_rows(d_rim, flipped) * row_live
    def tall(v):
        return jnp.pad(v, ((0, TOK - v.shape[0]), (0, 0)))

    def banded(v, width):
        v = tall(v).reshape(TOK, 4, -1).transpose(1, 0, 2)
        return jnp.pad(v, ((0, 0), (0, 0), (0, width - v.shape[2])))

    stats = jnp.mean(windows.astype(full_type), 1)
    vectors = [g_gn_g, g_gn_b, g_emb_b, g_ln1_g, g_ln1_b, g_q_b, g_v_b, g_out_b, g_ln2_g, g_ln2_b, g_up_b, g_down_b]
    row_mean = jnp.sum(stats[:, None] * flat_feat.astype(full_type), 0)
    row_dot = jnp.sum(feat.reshape(-1, channels) * flat_feat.astype(full_type), 0) / conv_weight.shape[0]
    vec = jnp.concatenate(vectors + [row_mean, row_dot])
    vec = jnp.pad(vec, (0, -vec.shape[0] % 1024)).reshape(-1, 128)
    r_down, r_up, r_out, r_qkv, r_conv, r_emb, r_vec = reduce_grads(
        tall(grad_out), banded(act, D), tall(hidden2), banded(d_pre, D), tall(d_attn), banded(mixed, 256), tall(hidden),
        banded(d_qkv, 640), tall(windows), tall(flat_feat), tall(active.reshape(-1, channels)), tall(flat_grad), vec)
    img, band = lax.axis_index("img"), lax.axis_index("band")
    n_img, n_band = lax.axis_size("img"), lax.axis_size("band")
    flat = r_vec.reshape(-1)
    offset = 0
    vsum = []
    for v in vectors:
        size = v.shape[0] // n_img
        vsum.append(lax.dynamic_slice_in_dim(flat, offset + img * size, size))
        offset += v.shape[0]
    m_one, m_two = flat[offset : offset + channels], flat[offset + channels : offset + 2 * channels]

    def own(v, total):
        size = total // n_img
        return lax.dynamic_slice_in_dim(v, lax.rem(img, v.shape[0] // size) * size, size)

    def own_band(v, width):
        return lax.dynamic_slice_in_dim(v, lax.div(band, 2) * width, width, axis=1)

    cols = channels // n_band
    conv_rows_here = conv_weight.shape[0] // n_img
    g_conv = own_band(own(r_conv, conv_weight.shape[0]), cols)
    sl = lambda v: lax.dynamic_slice_in_dim(v, band * cols, cols)
    own_stand = lax.dynamic_slice(stand_full, (img * conv_rows_here, band * cols), (conv_rows_here, cols))
    s_conv = sl(wscale) * (g_conv - sl(m_one) - own_stand * sl(m_two))
    s_emb = own_band(own(r_emb, channels), D // n_band)
    s_qkv = own(r_qkv, D)[:, : 3 * D // n_band]
    s_out = own(r_out, D)[:, : D // n_band].T
    s_up = own(r_up, D)
    s_down = own(r_down, D).T
    summed = (
        s_conv, vsum[0], vsum[1], s_emb, vsum[2], vsum[3], vsum[4], s_qkv, vsum[5], vsum[6], s_out, vsum[7], vsum[8], vsum[9],
        s_up, vsum[10], s_down, vsum[11],
    )
    return (encoded, image_grad, text_grad) + summed


def solution(mesh):
    in_specs = (
        P("img", "band", None, None),
        P(),
        P(),
        P(),
        P(),
        P(),
        P(),
        P(),
        P(),
        P(),
        P(),
        P(),
        P(),
        P(),
        P(),
        P(),
        P(),
        P(),
        P(),
        P(("img", "band"), None, None),
        P(("img", "band")),
        P(("img", "band"), None, None),
    )
    out_specs = (
        P(("img", "band"), None, None),
        P("img", "band", None, None),
        P(("img", "band"), None, None),
        P("img", "band"),
        P("img"),
        P("img"),
        P("img", "band"),
        P("img"),
        P("img"),
        P("img"),
        P("img", "band"),
        P("img"),
        P("img"),
        P("band", "img"),
        P("img"),
        P("img"),
        P("img"),
        P("img", "band"),
        P("img"),
        P("band", "img"),
        P("img"),
    )
    return jax.shard_map(body, mesh=mesh, in_specs=in_specs, out_specs=out_specs, check_vma=False)
```

```python
import functools
import types

import jax
import jax.numpy as jnp
from jax import lax
from jax.experimental import pallas as pl
from jax.experimental.pallas import tpu as pltpu
from jax.sharding import PartitionSpec as P

D = 768
FF = 3072
HEADS = 12
GROUPS = 32
GRID = 14
TEXT = 32
PATCHES = 196
WIDE = 16
TOK = 256
CELLS = GRID * WIDE
HALF = jnp.bfloat16
FULL = jnp.float32
MESH_ID = pl.DeviceIdType.MESH
CORE = ("band", 1)
FAR = ("band", 2)


def bit_of(value, bit):
    return lax.rem(lax.div(value, bit), 2)


def flip(value, bit):
    return value + bit * (1 - 2 * bit_of(value, bit))


def partner(label):
    axis, bit = label
    img, band = lax.axis_index("img"), lax.axis_index("band")
    return (flip(img, bit), band) if axis == "img" else (img, flip(band, bit))


def my_bit(label):
    axis, bit = label
    return bit_of(lax.axis_index(axis), bit)


def bits(count):
    return [1 << k for k in range(count.bit_length() - 1)]


class Plan:
    def __init__(self, n_img, rows, width, lead, order):
        self.width = width
        split = [("img", k) for k in reversed(bits(n_img)) if (rows // n_img) * k % 16 == 0]
        self.rows = rows >> len(split)
        self.first = ([lead] if lead else []) + split
        rest = [("img", k) for k in bits(n_img) if ("img", k) not in split]
        ordered = [lab for lab in order if lab in self.first]
        self.order = ordered + rest + [lab for lab in order if lab not in self.first and lab[0] == "band"]
        self.shapes = []
        labels = list(self.first)
        for lab in self.order:
            if lab in labels:
                labels.remove(lab)
            self.shapes.append((2,) * len(labels) + (self.rows, width))
        self.shape = (2,) * len(self.first) + (self.rows, width)

    def scratch(self):
        return [self.shape] + self.shapes


class Piece:
    def __init__(self, plan, refs, sems, slot, out, at):
        self.plan, self.buf, self.recv = plan, refs[0], refs[1:]
        self.sems, self.slot = sems, slot
        self.labels, self.cur = list(plan.first), refs[0]
        self.sent = []
        self.out = out.at[:, pl.ds(at, plan.width)]
        self.stage = 0

    def _index(self, label, which):
        at = self.labels.index(label)
        return (slice(None),) * at + (which,)

    def start(self):
        label = self.plan.order[self.stage]
        src = self.cur
        if label in self.labels:
            src = src.at[self._index(label, 1 - my_bit(label))]
        send, recv = self.sems
        copy = pltpu.make_async_remote_copy(
            src_ref=src,
            dst_ref=self.recv[self.stage],
            send_sem=send.at[self.slot + self.stage],
            recv_sem=recv.at[self.slot + self.stage],
            device_id=partner(label),
            device_id_type=MESH_ID,
        )
        copy.start()
        self.sent.append(copy)

    def step(self):
        label = self.plan.order[self.stage]
        self.sent[self.stage].wait_recv()
        mine = self.cur
        if label in self.labels:
            mine = mine[self._index(label, my_bit(label))]
            self.labels.remove(label)
        else:
            mine = mine[...]
        got = self.recv[self.stage]
        self.stage += 1
        if self.stage == len(self.plan.order):
            self.out[...] = (got[...].astype(FULL) + mine.astype(FULL)).reshape(self.out.shape)
        else:
            got[...] = got[...] + mine
            self.cur = got
            self.start()

    def drain(self):
        for copy in self.sent:
            copy.wait_send()


def dot(left, right):
    return jnp.dot(left, right, preferred_element_type=FULL)


def dot_tn(left, right):
    return lax.dot_general(left, right, (((0,), (0,)), ((), ())), preferred_element_type=FULL)


def dot_nt(left, right):
    return lax.dot_general(left, right, (((1,), (1,)), ((), ())), preferred_element_type=FULL)


def exact_dot(left, right):
    return jnp.dot(left, right, precision=lax.Precision.HIGHEST, preferred_element_type=FULL)


def gelu_parts(x):
    cdf = 0.5 + 0.5 * lax.erf(x * 0.7071067811865476)
    pdf = jnp.exp(-0.5 * x * x) * 0.3989422804014327
    return x * cdf, cdf + x * pdf


def iota(shape, axis):
    return lax.broadcasted_iota(jnp.int32, shape, axis)


def row(ref):
    return ref[...].reshape(1, -1)


def column_sum(values):
    return jnp.sum(values, 0, keepdims=True)


def shifted(values):
    edge = jnp.zeros(values.shape[:2] + (1, values.shape[3]), FULL)
    left = jnp.concatenate([edge, values[:, :, : WIDE - 1]], 2)
    right = jnp.concatenate([values[:, :, 1:], edge], 2)
    return left, values, right


def layer_kernel(names, plans, *refs):
    r = types.SimpleNamespace(**dict(zip(names, refs)))
    img, band = lax.axis_index("img"), lax.axis_index("band")
    n_img, n_band = lax.axis_size("img"), lax.axis_size("band")
    images, rows = r.image.shape[:2]
    channels = r.conv_weight.shape[1]
    core = my_bit(CORE)
    others = [lax.rem(band + d, n_band) for d in range(n_band)]

    fetches = {}

    def fetch(name, at):
        copy = pltpu.make_async_copy(getattr(r, name), getattr(r, "v_" + name), r.fetch_sem.at[at])
        copy.start()
        fetches[name] = copy

    for at, name in enumerate(("conv_weight", "embed_weight", "qkv_weight", "cotangent", "text_embed", "out_weight", "up_weight", "down_weight")):
        fetch(name, at)

    links = [CORE, FAR] + [("img", k) for k in bits(n_img)]
    barrier = pltpu.get_barrier_semaphore()
    for d in range(1, n_band):
        pl.semaphore_signal(barrier, inc=1, device_id=(img, others[d]), device_id_type=MESH_ID)
    for label in links[2:]:
        pl.semaphore_signal(barrier, inc=1, device_id=partner(label), device_id_type=MESH_ID)
    pl.semaphore_wait(barrier, n_band - 1 + len(links) - 2)

    pending = []

    def send(src, dst, at, device):
        copy = pltpu.make_async_remote_copy(
            src_ref=src, dst_ref=dst, send_sem=r.send_sem.at[at], recv_sem=r.recv_sem.at[at],
            device_id=device, device_id_type=MESH_ID)
        copy.start()
        pending.append(copy)
        return copy

    def edge_rows(ref, at):
        up = send(ref.at[:, rows], ref.at[:, 0], at, (img, others[1]))
        down = send(ref.at[:, 1], ref.at[:, rows + 1], at + 1, (img, others[n_band - 1]))
        return up, down

    def edges_in(ref, copies):
        for copy in copies:
            copy.wait_recv()
        values = ref[...].astype(FULL)
        at = iota(values.shape, 1) + band * rows
        return jnp.where((at == 0) | (at > n_band * rows), 0.0, values)

    def exchange(values, slots, at):
        slots[0] = values
        copies = [send(slots.at[0], slots.at[d], at + d - 1, (img, others[d])) for d in range(1, n_band)]
        for d, copy in enumerate(copies, 1):
            copy.wait_recv()
            values = values + slots[d]
        return values

    def to_owners(src, dst, at):
        copies = [send(src.at[others[d]], dst.at[band], at + d - 1, (img, others[d])) for d in range(1, n_band)]
        dst[band] = src[band]
        for copy in copies:
            copy.wait_recv()

    r.pixels[:, 1 : rows + 1, GRID:, :] = jnp.zeros((images, rows, WIDE - GRID, channels), HALF)
    at_row = iota((images, rows, GRID, channels), 1) + band * rows
    r.pixels[:, 1 : rows + 1, :GRID, :] = jnp.where(at_row < GRID, r.image[...].astype(FULL), 0.0).astype(HALF)
    copies = edge_rows(r.pixels, 0)

    fetches["conv_weight"].wait()
    taps = r.conv_weight.shape[0]
    chunks = [slice(k, k + 256) for k in range(0, taps, 256)]
    wmean = sum(column_sum(r.v_conv_weight[s].astype(FULL)) for s in chunks) * (1.0 / taps)
    wvar = 0.0
    for s in chunks:
        cent = r.v_conv_weight[s].astype(FULL) - wmean
        wvar = wvar + column_sum(cent * cent)
    wscale = lax.rsqrt(wvar * (1.0 / taps) + 1e-05)
    for s in chunks:
        r.v_conv_weight[s] = ((r.v_conv_weight[s].astype(FULL) - wmean) * wscale).astype(HALF)
    r.o_wstat[0:1] = wmean
    r.o_wstat[1:2] = wscale

    pixels = edges_in(r.pixels, copies)
    for e, values in enumerate(shifted(pixels)):
        r.views[e] = values.astype(HALF)

    def window(views, a, e):
        return views[e, :, a : a + rows].reshape(TOK, channels)

    place = iota((TOK, channels), 0)
    live = (lax.rem(place, WIDE) < GRID) & (lax.rem(lax.div(place, WIDE), rows) + band * rows < GRID)
    feat = 0.0
    tap_sum = 0.0
    for a in range(3):
        for e in range(3):
            seen = window(r.views, a, e)
            feat = feat + dot(seen, r.v_conv_weight[(3 * a + e) * channels : (3 * a + e + 1) * channels])
            tap_sum = tap_sum + seen.astype(FULL)
    feat = jnp.where(live, feat, 0.0)
    r.feat[...] = feat
    r.tap_sum[...] = jnp.broadcast_to(jnp.sum(tap_sum, 1, keepdims=True), (TOK, 128))
    per_group = channels // GROUPS
    entries = 1.0 / (GRID * GRID * per_group)
    same = lax.div(iota((channels, channels), 0), per_group) == lax.div(iota((channels, channels), 1), per_group)
    same = jnp.where(same, 1.0, 0.0)
    cells = TOK // images

    def image_sums(one, two):
        one = jnp.sum(one.reshape(images, cells, channels), 1)
        two = jnp.sum(two.reshape(images, cells, channels), 1)
        return exact_dot(jnp.concatenate([one, two], 0), same)

    def per_image(sums, which):
        return sums[which * images : (which + 1) * images].reshape(images, 1, channels)

    sums = exchange(image_sums(feat, feat * feat), r.sums, 2) * entries
    gmean = per_image(sums, 0)
    gscale = lax.rsqrt(per_image(sums, 1) - gmean * gmean + 1e-05)
    zhat = ((feat.reshape(images, cells, channels) - gmean) * gscale).reshape(TOK, channels)
    r.zhat[...] = zhat
    stem, slope = gelu_parts(zhat * row(r.gn_gain) + row(r.gn_bias))
    r.active[...] = jnp.where(live, stem, 0.0).astype(HALF)
    r.slope[...] = jnp.where(live, slope, 0.0)
    fetches["embed_weight"].wait()
    embedded = dot(r.active[...], r.v_embed_weight[...]) + row(r.embed_bias)
    r.embedded[...] = embedded.astype(HALF).reshape(images, cells, D)
    to_owners(r.embedded, r.patches, 5)

    def norm(values):
        mean = jnp.mean(values, -1, keepdims=True)
        cent = values - mean
        rstd = lax.rsqrt(jnp.mean(cent * cent, -1, keepdims=True) + 1e-06)
        return cent * rstd, rstd

    def norm_back(grad, nhat, rstd, gain):
        s = grad * gain
        inner = s - jnp.mean(s, -1, keepdims=True) - nhat * jnp.mean(s * nhat, -1, keepdims=True)
        return inner * rstd

    fetches["text_embed"].wait()
    r.stream[...] = r.patches[...].reshape(TOK, D).astype(FULL)
    r.stream[CELLS:] = r.v_text_embed[0].astype(FULL)
    nhat, rstd_one = norm(r.stream[...])
    r.nhat_one[...] = nhat
    r.rstd_one[...] = rstd_one
    r.hidden[...] = (nhat * row(r.ln1_gain) + row(r.ln1_bias)).astype(HALF)
    fetches["qkv_weight"].wait()
    for k, bias in enumerate((r.query_bias, None, r.value_bias)):
        values = dot(r.hidden[...], r.v_qkv_weight[:, k * D : (k + 1) * D])
        if bias is not None:
            values = values + row(bias)
        values = values.astype(HALF)
        r.qkv[:, k * D : (k + 1) * D] = values * 0.125 if k == 0 else values

    key_at = iota((1, TOK), 1)
    key_live = ((key_at < CELLS) & (lax.rem(key_at, WIDE) < GRID)) | ((key_at >= CELLS) & (key_at - CELLS < r.text_len[0]))
    first = iota((TOK, 128), 1) < 64
    zero = jnp.zeros((TOK, 128), HALF)

    def pair_of(ref, k, p):
        return ref[:, pl.ds(pl.multiple_of(k * D + p * 128, 128), 128)]

    def only(values, h):
        return jnp.where(first, values, zero) if h == 0 else jnp.where(first, zero, values)

    def attend(p, carry):
        query, key, value = (pair_of(r.qkv, k, p) for k in range(3))
        sides = []
        for h in range(2):
            scores = jnp.where(key_live, dot_nt(only(query, h), key), -1000000000.0)
            expd = jnp.exp(scores - jnp.max(scores, -1, keepdims=True))
            probs = expd * (1.0 / jnp.sum(expd, -1, keepdims=True))
            r.probs[2 * p + h] = probs
            sides.append(dot(probs.astype(HALF), value))
        r.mixed[:, pl.ds(pl.multiple_of(p * 128, 128), 128)] = jnp.where(first, *sides).astype(HALF)
        return carry

    lax.fori_loop(0, HEADS // 2, attend, 0)
    fetches["out_weight"].wait()
    mid = r.stream[...] + dot(r.mixed[...], r.v_out_weight[...]) + row(r.out_bias)
    r.final[...] = mid + row(r.down_bias)
    nhat, rstd_two = norm(mid)
    r.nhat_two[...] = nhat
    r.rstd_two[...] = rstd_two
    r.hidden2[...] = (nhat * row(r.ln2_gain) + row(r.ln2_bias)).astype(HALF)

    fetches["cotangent"].wait()
    seq = r.cotangent.shape[1]

    def token_of(at):
        return jnp.where(at < CELLS, jnp.where(lax.rem(at, WIDE) < GRID, lax.div(at, WIDE) * GRID + lax.rem(at, WIDE), -1), at - CELLS + PATCHES)

    spread = jnp.where(token_of(iota((TOK, seq), 0)) == iota((TOK, seq), 1), 1.0, 0.0).astype(HALF)
    gather = jnp.where(token_of(iota((seq, TOK), 1)) == iota((seq, TOK), 0), 1.0, 0.0).astype(HALF)
    r.cot[...] = dot(spread, r.v_cotangent[0]).astype(HALF)

    fetches["up_weight"].wait()
    fetches["down_weight"].wait()
    step = 384
    r.grad_in[...] = jnp.zeros((TOK, D), FULL)

    def feed(t, carry):
        wide = pl.ds(pl.multiple_of(t * step, 128), step)
        here = (lax.div(t * step, D), slice(None), pl.ds(pl.multiple_of(lax.rem(t * step, D), 128), step))
        up, down = r.v_up_weight[:, wide], r.v_down_weight[wide, :]
        act, slope = gelu_parts(dot(r.hidden2[...], up) + r.up_bias[:, wide])
        act = act.astype(HALF)
        r.act[here] = act
        r.final[...] += dot(act, down)
        d_pre = (dot_nt(r.cot[...], down) * slope).astype(HALF)
        r.d_pre[here] = d_pre
        r.up_sum[:, wide] = column_sum(d_pre.astype(FULL))
        r.grad_in[...] += dot_nt(d_pre, up)
        return carry

    lax.fori_loop(0, FF // step, feed, 0)
    r.encoded[0] = dot(gather, r.final[...].astype(HALF)).astype(HALF)

    def put(at, values, lo=0):
        r.vec[at : at + 1, lo : lo + values.shape[1]] = values

    r.vec[...] = jnp.zeros(r.vec.shape, FULL)
    cot = r.cot[...].astype(FULL)
    put(8, column_sum(cot))
    for k in range(FF // D):
        put(9 + k, r.up_sum[:, k * D : (k + 1) * D])

    grad = r.grad_in[...]
    put(6, column_sum(grad * r.nhat_two[...]))
    put(7, column_sum(grad))
    d_mid = cot + norm_back(grad, r.nhat_two[...], r.rstd_two[...], row(r.ln2_gain))
    r.stream[...] = d_mid
    r.d_attn[...] = d_mid.astype(HALF)
    put(5, column_sum(r.d_attn[...].astype(FULL)))
    r.d_mixed[...] = dot_nt(r.d_attn[...], r.v_out_weight[...]).astype(HALF)

    def attend_back(p, carry):
        query, key, value = (pair_of(r.qkv, k, p) for k in range(3))
        d_mixed = pair_of(r.d_mixed, 0, p)
        sides = [[], [], []]
        for h in range(2):
            probs = r.probs[2 * p + h]
            d_probs = dot_nt(only(d_mixed, h), value)
            delta = jnp.sum(d_probs * probs, -1, keepdims=True)
            d_scores = (probs * (d_probs - delta)).astype(HALF)
            sides[0].append(dot(d_scores, key) * 0.125)
            sides[1].append(dot_tn(d_scores, query))
            sides[2].append(dot_tn(probs.astype(HALF), d_mixed))
        for k in range(3):
            r.d_qkv[:, pl.ds(pl.multiple_of(k * D + p * 128, 128), 128)] = jnp.where(first, *sides[k]).astype(HALF)
        return carry

    lax.fori_loop(0, HEADS // 2, attend_back, 0)
    put(3, column_sum(r.d_qkv[:, :D].astype(FULL)))
    put(4, column_sum(r.d_qkv[:, 2 * D :].astype(FULL)))
    grad = dot_nt(r.d_qkv[...], r.v_qkv_weight[...])
    put(1, column_sum(grad * r.nhat_one[...]))
    put(2, column_sum(grad))
    d_stream = r.stream[...] + norm_back(grad, r.nhat_one[...], r.rstd_one[...], row(r.ln1_gain))
    r.text_grad[0] = d_stream[CELLS:]
    at_cell = iota((TOK, D), 0) < CELLS
    r.d_patches[...] = jnp.where(at_cell, d_stream, 0.0).astype(HALF).reshape(r.d_patches.shape)
    to_owners(r.d_patches, r.d_cells, 8)

    d_cells = r.d_cells[...].reshape(TOK, D)
    put(0, column_sum(d_cells.astype(FULL)))
    d_active = dot_nt(d_cells, r.v_embed_weight[...]).astype(HALF).astype(FULL)
    d_norm = d_active * r.slope[...]
    zhat = r.zhat[...]
    put(13, column_sum(d_norm * zhat))
    put(13, column_sum(d_norm), channels)
    d_hat = d_norm * row(r.gn_gain)
    back = exchange(image_sums(d_hat, d_hat * zhat), r.sums_back, 11) * entries
    d_feat = d_hat.reshape(images, cells, channels) - per_image(back, 0)
    d_feat = (d_feat - zhat.reshape(images, cells, channels) * per_image(back, 1)) * gscale
    d_feat = jnp.where(live, d_feat.reshape(TOK, channels), 0.0).astype(HALF)
    r.d_feat[...] = d_feat
    r.d_rows[:, 1 : rows + 1] = d_feat.reshape(images, rows, WIDE, channels)
    copies = edge_rows(r.d_rows, 14)
    d_feat = d_feat.astype(FULL)
    put(13, column_sum(r.tap_sum[:, :1] * d_feat) * (1.0 / taps), 2 * channels)
    put(14, column_sum(r.feat[...] * d_feat) * (1.0 / taps))
    for e, values in enumerate(shifted(edges_in(r.d_rows, copies))):
        r.d_views[e] = values.astype(HALF)
    grad = 0.0
    for a in range(3):
        for e in range(3):
            seen = window(r.d_views, 2 - a, 2 - e)
            grad = grad + dot_nt(seen, r.v_conv_weight[(3 * a + e) * channels : (3 * a + e + 1) * channels])
    grad = jnp.where(live, grad, 0.0).reshape(images, rows, WIDE, channels)
    r.image_grad[...] = grad[:, :, :GRID]

    swaps = {}
    base = 16

    def swap(name, at, src, dst):
        swaps.setdefault(name, []).append(send(src, dst, base + at, partner(CORE)))

    def swap_bands(name, at, src, dst):
        for y in range(2):
            swap(name, at + y, src.at[2 * y + 1 - core], dst.at[y])

    def banded(ref, src, width):
        for k in range(4):
            ref[k, :, :width] = src[:, k * width : (k + 1) * width]
            ref[k, :, width:] = jnp.zeros((TOK, ref.shape[2] - width), HALF)

    banded(r.mixed_bands, r.mixed, D // 4)
    banded(r.d_qkv_bands, r.d_qkv, 3 * D // 4)
    swap("down", 0, r.cot, r.r_cot)
    swap_bands("down", 1, r.act, r.r_act)
    swap("up", 3, r.hidden2, r.r_hidden2)
    swap_bands("up", 4, r.d_pre, r.r_d_pre)
    swap("qkv", 6, r.hidden, r.r_hidden)
    swap_bands("qkv", 7, r.d_qkv_bands, r.r_d_qkv)
    swap("out", 9, r.d_attn, r.r_d_attn)
    swap_bands("out", 10, r.mixed_bands, r.r_mixed)
    swap("conv", 12, r.views, r.r_views)
    swap("conv", 13, r.d_feat, r.r_d_feat)
    swap("emb", 14, r.active, r.r_active)
    swap("emb", 15, r.d_cells, r.r_d_cells)

    def arrived(name):
        for copy in swaps[name]:
            copy.wait_recv()

    pieces = {}
    slot = base + 16
    for (name, (plan, out, at)) in plans.items():
        refs = [getattr(r, f"{name}{k}") for k in range(1 + len(plan.order))]
        pieces[name] = Piece(plan, refs, (r.send_sem, r.recv_sem), slot, getattr(r, out), at)
        slot += len(plan.order)

    def unit(name, left, r_left, right, r_right, parts):
        arrived(name)
        for piece, lo in parts:
            piece = pieces[piece]
            w = piece.plan.width
            for y in range(2):
                for at in range(0, w, 128):
                    wide = slice(lo + at, lo + at + 128)
                    value = dot_tn(left[...], right[2 * y + core, :, wide])
                    value += dot_tn(r_left[...], r_right[y, :, wide])
                    value = value.astype(HALF).reshape(piece.plan.shape[1:-1] + (128,))
                    lead = (y,) + (slice(None),) * (len(piece.plan.shape) - 2)
                    piece.buf[lead + (slice(at, at + 128),)] = value
            piece.start()

    def columns(values, width):
        total = values.shape[1]
        col = iota((total, 2 * width), 1)
        want = jnp.where(col < width, col, col + width) + core * width
        pick = jnp.where(iota((total, 2 * width), 0) == want, 1.0, 0.0).astype(HALF)
        return dot(values, pick).astype(HALF)

    unit("down", r.cot, r.r_cot, r.act, r.r_act, [("p_da", 0), ("p_db", 384)])
    unit("up", r.hidden2, r.r_hidden2, r.d_pre, r.r_d_pre, [("p_ua", 0), ("p_ub", 384)])
    unit("qkv", r.hidden, r.r_hidden, r.d_qkv_bands, r.r_d_qkv, [("p_qa", 0), ("p_qb", 384)])
    unit("out", r.d_attn, r.r_d_attn, r.mixed_bands, r.r_mixed, [("p_o", 0)])
    arrived("conv")
    mine, theirs = columns(r.d_feat[...], channels // 4), columns(r.r_d_feat[...], channels // 4)
    piece = pieces["p_c"]
    for a in range(3):
        for e in range(3):
            value = dot_tn(window(r.views, a, e), mine) + dot_tn(window(r.r_views, a, e), theirs)
            value = value.astype(HALF)
            at, end = (3 * a + e) * channels, (3 * a + e + 1) * channels
            while at < end:
                block, lo = divmod(at, piece.plan.rows)
                size = min(end - at, piece.plan.rows - lo)
                where = tuple(block >> k & 1 for k in reversed(range(len(piece.plan.first))))
                done = at - (3 * a + e) * channels
                piece.buf[where + (slice(lo, lo + size),)] = value[done : done + size]
                at += size
    piece.start()
    arrived("emb")
    mine, theirs = columns(d_cells, D // 4), columns(r.r_d_cells[...].reshape(TOK, D), D // 4)
    piece = pieces["p_e"]
    value = dot_tn(r.active[...], mine) + dot_tn(r.r_active[...], theirs)
    piece.buf[...] = value.astype(HALF).reshape(piece.plan.shape)
    piece.start()

    def vec_start(stage):
        return send(r.vec if stage == 0 else r.vec_sum.at[stage - 1], r.vec_in.at[stage], slot + stage, partner(links[stage]))

    total = r.vec[...]
    on_way = vec_start(0)
    for stage in range(max([len(p.plan.order) for p in pieces.values()] + [len(links)])):
        for piece in pieces.values():
            if piece.stage < len(piece.plan.order):
                piece.step()
        if stage < len(links):
            on_way.wait_recv()
            total = total + r.vec_in[stage]
            if stage == len(links) - 1:
                r.o_vec[...] = total
            else:
                r.vec_sum[stage] = total
                on_way = vec_start(stage + 1)
    for piece in pieces.values():
        piece.drain()
    for copy in pending:
        copy.wait_send()


def body(
    image,
    conv_weight,
    gn_gain,
    gn_bias,
    embed_weight,
    embed_bias,
    ln1_gain,
    ln1_bias,
    qkv_weight,
    query_bias,
    value_bias,
    out_weight,
    out_bias,
    ln2_gain,
    ln2_bias,
    up_weight,
    up_bias,
    down_weight,
    down_bias,
    text_embed,
    text_len,
    cotangent,
):
    n_img, n_band = lax.axis_size("img"), lax.axis_size("band")
    img, band = lax.axis_index("img"), lax.axis_index("band")
    images, rows = image.shape[:2]
    taps, channels = conv_weight.shape
    img_bits = [("img", k) for k in bits(n_img)]
    y_first = [FAR] + img_bits
    x_first = img_bits[:1] + [FAR] + img_bits[1:]
    tail = img_bits + [FAR]
    plans = {
        "p_da": (Plan(n_img, D, 384, FAR, y_first), "o_down", 0),
        "p_db": (Plan(n_img, D, 384, FAR, x_first), "o_down", 384),
        "p_ua": (Plan(n_img, D, 384, FAR, y_first), "o_up", 0),
        "p_ub": (Plan(n_img, D, 384, FAR, x_first), "o_up", 384),
        "p_qa": (Plan(n_img, D, 384, FAR, y_first), "o_qkv", 0),
        "p_qb": (Plan(n_img, D, 256, FAR, x_first), "o_qkv", 384),
        "p_o": (Plan(n_img, D, 256, FAR, y_first), "o_out", 0),
        "p_c": (Plan(n_img, taps, channels // 2, None, tail), "o_conv", 0),
        "p_e": (Plan(n_img, channels, D // 2, None, tail), "o_emb", 0),
    }
    vec_shape = (16, D)
    arguments = {
        "image": image, "conv_weight": conv_weight, "gn_gain": gn_gain, "gn_bias": gn_bias, "embed_weight": embed_weight,
        "embed_bias": embed_bias, "ln1_gain": ln1_gain, "ln1_bias": ln1_bias, "qkv_weight": qkv_weight, "query_bias": query_bias,
        "value_bias": value_bias, "out_weight": out_weight, "out_bias": out_bias, "ln2_gain": ln2_gain, "ln2_bias": ln2_bias,
        "up_weight": up_weight, "up_bias": up_bias.reshape(1, FF), "down_weight": down_weight, "down_bias": down_bias,
        "text_embed": text_embed, "text_len": text_len, "cotangent": cotangent,
    }
    fetched = ("conv_weight", "embed_weight", "qkv_weight", "cotangent", "text_embed", "out_weight", "up_weight", "down_weight")
    spaces = {name: pl.ANY for name in fetched}
    spaces["text_len"] = pltpu.SMEM
    results = {
        "encoded": (cotangent.shape, HALF),
        "image_grad": (image.shape, FULL),
        "text_grad": (text_embed.shape, FULL),
        "o_down": ((plans["p_da"][0].rows, D), FULL),
        "o_up": ((plans["p_ua"][0].rows, D), FULL),
        "o_out": ((plans["p_o"][0].rows, 256), FULL),
        "o_qkv": ((plans["p_qa"][0].rows, 640), FULL),
        "o_conv": ((plans["p_c"][0].rows, channels // 2), FULL),
        "o_emb": ((plans["p_e"][0].rows, D // 2), FULL),
        "o_vec": (vec_shape, FULL),
        "o_wstat": ((2, channels), FULL),
    }
    halo = (images, rows + 2, WIDE, channels)
    split = (images, TOK // images, D)
    scratch = {
        "v_" + name: (arguments[name].shape, HALF) for name in fetched
    }
    scratch.update({
        "pixels": (halo, HALF), "views": ((3,) + halo, HALF), "feat": ((TOK, channels), FULL),
        "tap_sum": ((TOK, 128), FULL), "sums": ((n_band, 2 * images, channels), FULL), "sums_back": ((n_band, 2 * images, channels), FULL),
        "zhat": ((TOK, channels), FULL), "active": ((TOK, channels), HALF), "slope": ((TOK, channels), FULL),
        "embedded": (split, HALF), "patches": (split, HALF), "stream": ((TOK, D), FULL), "nhat_one": ((TOK, D), FULL),
        "rstd_one": ((TOK, 1), FULL), "hidden": ((TOK, D), HALF), "qkv": ((TOK, 3 * D), HALF), "probs": ((HEADS, TOK, TOK), FULL),
        "mixed": ((TOK, D), HALF), "nhat_two": ((TOK, D), FULL), "rstd_two": ((TOK, 1), FULL),
        "hidden2": ((TOK, D), HALF), "cot": ((TOK, D), HALF), "final": ((TOK, D), FULL), "grad_in": ((TOK, D), FULL),
        "act": ((4, TOK, D), HALF), "d_pre": ((4, TOK, D), HALF), "up_sum": ((1, FF), FULL), "vec": (vec_shape, FULL),
        "d_attn": ((TOK, D), HALF), "d_mixed": ((TOK, D), HALF), "d_qkv": ((TOK, 3 * D), HALF),
        "d_patches": (split, HALF), "d_cells": (split, HALF), "d_feat": ((TOK, channels), HALF), "d_rows": (halo, HALF),
        "d_views": ((3,) + halo, HALF), "mixed_bands": ((4, TOK, 256), HALF), "d_qkv_bands": ((4, TOK, 640), HALF),
        "r_cot": ((TOK, D), HALF), "r_act": ((2, TOK, D), HALF), "r_hidden2": ((TOK, D), HALF), "r_d_pre": ((2, TOK, D), HALF),
        "r_hidden": ((TOK, D), HALF), "r_d_qkv": ((2, TOK, 640), HALF), "r_d_attn": ((TOK, D), HALF), "r_mixed": ((2, TOK, 256), HALF),
        "r_views": ((3,) + halo, HALF), "r_d_feat": ((TOK, channels), HALF), "r_active": ((TOK, channels), HALF), "r_d_cells": (split, HALF),
    })
    slots = 32
    for name, (plan, _, _) in plans.items():
        for k, shape in enumerate(plan.scratch()):
            scratch[f"{name}{k}"] = (shape, HALF)
        slots += len(plan.order)
    n_links = 2 + len(img_bits)
    scratch["vec_sum"] = ((n_links,) + vec_shape, FULL)
    scratch["vec_in"] = ((n_links,) + vec_shape, FULL)
    slots += n_links
    sems = {"fetch_sem": 8, "send_sem": slots, "recv_sem": slots}
    names = list(arguments) + list(results) + list(scratch) + list(sems)
    whole = lambda space: pl.BlockSpec(memory_space=space)
    outs = pl.pallas_call(
        functools.partial(layer_kernel, names, plans),
        out_shape=[jax.ShapeDtypeStruct(*v) for v in results.values()],
        in_specs=[whole(spaces.get(name, pltpu.VMEM)) for name in arguments],
        out_specs=[whole(pltpu.VMEM)] * len(results),
        scratch_shapes=[pltpu.VMEM(*v) for v in scratch.values()] + [pltpu.SemaphoreType.DMA((n,)) for n in sems.values()],
        compiler_params=pltpu.CompilerParams(collective_id=0, has_side_effects=True, vmem_limit_bytes=63 * 2**20),
    )(*arguments.values())
    res = dict(zip(results, outs))
    vec = res["o_vec"]

    def own(v, total, axis=0):
        size = total // n_img
        return lax.dynamic_slice_in_dim(v, lax.rem(img, v.shape[axis] // size) * size, size, axis)

    def own_band(v, width):
        return lax.dynamic_slice_in_dim(v, lax.div(band, 2) * width, width, axis=1)

    def own_vec(at, lo=0, total=D):
        return own(vec[at, lo : lo + total], total)

    cols = channels // n_band
    taps_here = taps // n_img
    m_one, m_two = vec[13, 2 * channels :], vec[14, :channels]
    mine = lambda v: lax.dynamic_slice_in_dim(v, band * cols, cols)
    own_weight = lax.dynamic_slice(conv_weight, (img * taps_here, band * cols), (taps_here, cols)).astype(FULL)
    wmean, wscale = mine(res["o_wstat"][0]), mine(res["o_wstat"][1])
    own_stand = (own_weight - wmean) * wscale
    g_conv = own_band(own(res["o_conv"], taps), cols)
    g_conv = wscale * (g_conv - mine(m_one) - own_stand * mine(m_two))
    return (
        res["encoded"],
        res["image_grad"],
        res["text_grad"],
        g_conv,
        own_vec(13, 0, channels),
        own_vec(13, channels, channels),
        own_band(own(res["o_emb"], channels), D // n_band),
        own_vec(0),
        own_vec(1),
        own_vec(2),
        own(res["o_qkv"], D)[:, : 3 * D // n_band],
        own_vec(3),
        own_vec(4),
        own(res["o_out"], D)[:, : D // n_band].T,
        own_vec(5),
        own_vec(6),
        own_vec(7),
        own(res["o_up"], D),
        own(vec[9:13].reshape(FF), FF),
        own(res["o_down"], D).T,
        own_vec(8),
    )


def solution(mesh):
    in_specs = (
        P("img", "band", None, None),
        P(),
        P(),
        P(),
        P(),
        P(),
        P(),
        P(),
        P(),
        P(),
        P(),
        P(),
        P(),
        P(),
        P(),
        P(),
        P(),
        P(),
        P(),
        P(("img", "band"), None, None),
        P(("img", "band")),
        P(("img", "band"), None, None),
    )
    out_specs = (
        P(("img", "band"), None, None),
        P("img", "band", None, None),
        P(("img", "band"), None, None),
        P("img", "band"),
        P("img"),
        P("img"),
        P("img", "band"),
        P("img"),
        P("img"),
        P("img"),
        P("img", "band"),
        P("img"),
        P("img"),
        P("band", "img"),
        P("img"),
        P("img"),
        P("img"),
        P("img", "band"),
        P("img"),
        P("band", "img"),
        P("img"),
    )
    return jax.shard_map(body, mesh=mesh, in_specs=in_specs, out_specs=out_specs, check_vma=False)
```

```python
import functools
import types

import jax
import jax.numpy as jnp
from jax import lax
from jax.experimental import pallas as pl
from jax.experimental.pallas import tpu as pltpu
from jax.sharding import PartitionSpec as P

D = 768
FF = 3072
HEADS = 12
GROUPS = 32
GRID = 14
TEXT = 32
PATCHES = 196
WIDE = 16
TOK = 256
CELLS = GRID * WIDE
HALF = jnp.bfloat16
FULL = jnp.float32
MESH_ID = pl.DeviceIdType.MESH
CORE = ("band", 1)
FAR = ("band", 2)


def bit_of(value, bit):
    return lax.rem(lax.div(value, bit), 2)


def flip(value, bit):
    return value + bit * (1 - 2 * bit_of(value, bit))


def partner(label):
    axis, bit = label
    img, band = lax.axis_index("img"), lax.axis_index("band")
    return (flip(img, bit), band) if axis == "img" else (img, flip(band, bit))


def my_bit(label):
    axis, bit = label
    return bit_of(lax.axis_index(axis), bit)


def bits(count):
    return [1 << k for k in range(count.bit_length() - 1)]


class Plan:
    def __init__(self, n_img, rows, width, lead, order, parts=1):
        self.width = width
        split = [("img", k) for k in reversed(bits(n_img)) if (rows // n_img) * k % 16 == 0]
        self.rows = (rows >> len(split)) // parts
        self.first = ([lead] if lead else []) + split
        rest = [("img", k) for k in bits(n_img) if ("img", k) not in split]
        ordered = [lab for lab in order if lab in self.first]
        self.order = ordered + rest + [lab for lab in order if lab not in self.first and lab[0] == "band"]
        self.shapes = []
        labels = list(self.first)
        for lab in self.order:
            if lab in labels:
                labels.remove(lab)
            self.shapes.append((2,) * len(labels) + (self.rows, width))
        self.shape = (2,) * len(self.first) + (self.rows, width)

    def scratch(self):
        return [self.shape] + self.shapes


class Once:
    def __init__(self, copy):
        self.copy, self.left = copy, {"wait", "wait_send", "wait_recv"}
        copy.start()

    def _wait(self, kind):
        if kind in self.left:
            self.left.remove(kind)
            getattr(self.copy, kind)()

    def wait(self):
        self._wait("wait")

    def wait_send(self):
        self._wait("wait_send")

    def wait_recv(self):
        self._wait("wait_recv")


class Piece:
    def __init__(self, plan, refs, sems, slot, out, at, pending):
        self.pending = pending
        self.plan, self.buf, self.recv = plan, refs[0], refs[1:]
        self.sems, self.slot = sems, slot
        self.labels, self.cur = list(plan.first), refs[0]
        self.sent = []
        self.out = out.at[pl.ds(at[0], plan.rows), pl.ds(at[1], plan.width)]
        self.stage = 0

    def _index(self, label, which):
        at = self.labels.index(label)
        return (slice(None),) * at + (which,)

    def start(self):
        label = self.plan.order[self.stage]
        src = self.cur
        if label in self.labels:
            src = src.at[self._index(label, 1 - my_bit(label))]
        send, recv = self.sems
        copy = pltpu.make_async_remote_copy(
            src_ref=src,
            dst_ref=self.recv[self.stage],
            send_sem=send.at[self.slot + self.stage],
            recv_sem=recv.at[self.slot + self.stage],
            device_id=partner(label),
            device_id_type=MESH_ID,
        )
        self.sent.append(Once(copy))
        self.pending.append(self.sent[-1])

    def step(self):
        label = self.plan.order[self.stage]
        self.sent[self.stage].wait_recv()
        mine = self.cur
        if label in self.labels:
            mine = mine[self._index(label, my_bit(label))]
            self.labels.remove(label)
        else:
            mine = mine[...]
        got = self.recv[self.stage]
        self.stage += 1
        if self.stage == len(self.plan.order):
            self.out[...] = (got[...].astype(FULL) + mine.astype(FULL)).reshape(self.out.shape)
        else:
            got[...] = got[...] + mine
            self.cur = got
            self.start()


def dot(left, right):
    return jnp.dot(left, right, preferred_element_type=FULL)


def dot_tn(left, right):
    return lax.dot_general(left, right, (((0,), (0,)), ((), ())), preferred_element_type=FULL)


def dot_nt(left, right):
    return lax.dot_general(left, right, (((1,), (1,)), ((), ())), preferred_element_type=FULL)


def exact_dot(left, right):
    return jnp.dot(left, right, precision=lax.Precision.HIGHEST, preferred_element_type=FULL)


def gelu_parts(x):
    cdf = 0.5 + 0.5 * lax.erf(x * 0.7071067811865476)
    pdf = jnp.exp(-0.5 * x * x) * 0.3989422804014327
    return x * cdf, cdf + x * pdf


def iota(shape, axis):
    return lax.broadcasted_iota(jnp.int32, shape, axis)


def row(ref):
    return ref[...].reshape(1, -1)


def column_sum(values):
    return jnp.sum(values, 0, keepdims=True)


def shifted(values):
    edge = jnp.zeros(values.shape[:2] + (1, values.shape[3]), FULL)
    left = jnp.concatenate([edge, values[:, :, : WIDE - 1]], 2)
    right = jnp.concatenate([values[:, :, 1:], edge], 2)
    return left, values, right


DOWN, UP, QKV, TAIL = ("p_d0", "p_d1", "p_d2"), ("p_u0", "p_u1", "p_u2"), ("p_q0", "p_q1", "p_q2"), ("p_c0", "p_c1", "p_c2", "p_e")
POLLS = {
    "back1": DOWN,
    "cells": ("qkv",) + UP + ("+p_q1", "+p_q2"),
    "sums": ("p_d1",),
    "edges": ("p_d0", "p_d2", "p_u1", "+p_q0"),
    "grad": ("p_u0", "p_u2"),
    "end": DOWN + ("p_q1", "p_q2", "p_q0") + TAIL + UP + DOWN + ("vec",) + QKV + TAIL + UP + ("vec",) + QKV + ("vec",) + TAIL + QKV + ("vec",) + TAIL + ("vec",),
}


def layer_kernel(names, plans, *refs):
    r = types.SimpleNamespace(**dict(zip(names, refs)))
    img, band = lax.axis_index("img"), lax.axis_index("band")
    n_img, n_band = lax.axis_size("img"), lax.axis_size("band")
    images, rows = r.image.shape[:2]
    channels = r.conv_weight.shape[1]
    core = my_bit(CORE)
    others = [lax.rem(band + d, n_band) for d in range(n_band)]

    fetches = {}

    def fetch(name, at):
        copy = pltpu.make_async_copy(getattr(r, name), getattr(r, "v_" + name), r.fetch_sem.at[at])
        fetches[name] = Once(copy)

    for at, name in enumerate(("conv_weight", "embed_weight", "qkv_weight", "cotangent", "text_embed", "out_weight", "up_weight", "down_weight")):
        fetch(name, at)

    links = [CORE, FAR] + [("img", k) for k in bits(n_img)]
    barrier = pltpu.get_barrier_semaphore()
    for d in range(1, n_band):
        pl.semaphore_signal(barrier, inc=1, device_id=(img, others[d]), device_id_type=MESH_ID)
    for label in links[2:]:
        pl.semaphore_signal(barrier, inc=1, device_id=partner(label), device_id_type=MESH_ID)
    pl.semaphore_wait(barrier, n_band - 1 + len(links) - 2)

    pending = []

    def send(src, dst, at, device):
        copy = pltpu.make_async_remote_copy(
            src_ref=src, dst_ref=dst, send_sem=r.send_sem.at[at], recv_sem=r.recv_sem.at[at],
            device_id=device, device_id_type=MESH_ID)
        pending.append(Once(copy))
        return pending[-1]

    def edge_rows(ref, at):
        up = send(ref.at[:, rows], ref.at[:, 0], at, (img, others[1]))
        down = send(ref.at[:, 1], ref.at[:, rows + 1], at + 1, (img, others[n_band - 1]))
        return up, down

    def edges_in(ref, copies):
        for copy in copies:
            copy.wait_recv()
        values = ref[...].astype(FULL)
        at = iota(values.shape, 1) + band * rows
        return jnp.where((at == 0) | (at > n_band * rows), 0.0, values)

    def exchange(values, slots, at, meanwhile=None):
        slots[0] = values
        copies = [send(slots.at[0], slots.at[d], at + d - 1, (img, others[d])) for d in range(1, n_band)]
        poll(meanwhile)
        for d, copy in enumerate(copies, 1):
            copy.wait_recv()
            values = values + slots[d]
        return values

    def to_owners(src, dst, at, meanwhile=None):
        copies = [send(src.at[others[d]], dst.at[band], at + d - 1, (img, others[d])) for d in range(1, n_band)]
        dst[band] = src[band]
        poll(meanwhile)
        for copy in copies:
            copy.wait_recv()

    swaps = {}
    base = 16

    def swap(name, at, src, dst):
        swaps.setdefault(name, []).append(send(src, dst, base + at, partner(CORE)))

    def swap_bands(name, at, src, dst):
        for y in range(2):
            swap(name, at + y, src.at[2 * y + 1 - core], dst.at[y])

    def swap_left(name, at, ref):
        swap(name, at, ref.at[:, pl.ds(0, TOK)], ref.at[:, pl.ds(TOK, TOK)])

    def arrived(name):
        for copy in swaps[name]:
            copy.wait_recv()

    pieces = {}
    slot = base + 16
    for name, (plan, out, at) in plans.items():
        refs = [getattr(r, f"{name}_{k}") for k in range(1 + len(plan.order))]
        pieces[name] = Piece(plan, refs, (r.send_sem, r.recv_sem), slot, getattr(r, out), at, pending)
        slot += len(plan.order)

    down, up, qkv = DOWN, UP, QKV

    def poll(point):
        for name in POLLS.get(point, ()):
            if name[0] == "+":
                pieces[name[1:]].start()
            elif name == "vec":
                vec_step()
            elif name == "qkv":
                qkv_unit()
            else:
                advance(name)

    def advance(*names):
        for name in names:
            if pieces[name].stage < len(pieces[name].plan.order):
                pieces[name].step()

    def unit(parts, terms, start=True):
        for j, name in enumerate(parts):
            piece = pieces[name]
            wide = slice(256 * j, 256 * (j + 1))
            for y in range(2):
                value = 0.0
                for left, right, got, at in terms:
                    if j >= at:
                        cut = slice(256 * (j - at), 256 * (j - at + 1))
                        both = jnp.concatenate([right[2 * y + core, :, cut], got[y, :, cut]], 0)
                        value = value + dot(left[...], both)
                piece.buf[y] = value.astype(HALF).reshape(piece.plan.shape[1:])
            if start:
                piece.start()

    r.pixels[:, 1 : rows + 1, GRID:, :] = jnp.zeros((images, rows, WIDE - GRID, channels), HALF)
    at_row = iota((images, rows, GRID, channels), 1) + band * rows
    r.pixels[:, 1 : rows + 1, :GRID, :] = jnp.where(at_row < GRID, r.image[...].astype(FULL), 0.0).astype(HALF)
    copies = edge_rows(r.pixels, 0)

    fetches["cotangent"].wait()
    seq = r.cotangent.shape[1]

    def token_of(at):
        return jnp.where(at < CELLS, jnp.where(lax.rem(at, WIDE) < GRID, lax.div(at, WIDE) * GRID + lax.rem(at, WIDE), -1), at - CELLS + PATCHES)

    spread = jnp.where(token_of(iota((TOK, seq), 0)) == iota((TOK, seq), 1), 1.0, 0.0).astype(HALF)
    gather = jnp.where(token_of(iota((seq, TOK), 1)) == iota((seq, TOK), 0), 1.0, 0.0).astype(HALF)
    r.cot[...] = dot(spread, r.v_cotangent[0]).astype(HALF)

    r.t_cot[:, :TOK] = r.cot[...].T
    swap_left("down", 0, r.t_cot)

    fetches["conv_weight"].wait()
    taps = r.conv_weight.shape[0]
    chunks = [slice(k, k + 256) for k in range(0, taps, 256)]
    wmean = sum(column_sum(r.v_conv_weight[s].astype(FULL)) for s in chunks) * (1.0 / taps)
    wvar = 0.0
    for s in chunks:
        cent = r.v_conv_weight[s].astype(FULL) - wmean
        wvar = wvar + column_sum(cent * cent)
    wscale = lax.rsqrt(wvar * (1.0 / taps) + 1e-05)
    taps_here = taps // n_img
    if taps_here % 16 == 0:
        own = r.v_conv_weight[pl.ds(pl.multiple_of(img * taps_here, 16), taps_here)]
    else:
        own = jnp.where(iota((taps_here, taps), 1) == iota((taps_here, taps), 0) + img * taps_here, 1.0, 0.0).astype(HALF)
        own = dot(own, r.v_conv_weight[...]).astype(HALF)
    own = ((own.astype(FULL) - wmean) * wscale, jnp.broadcast_to(wscale, (8, channels)))
    r.o_wstat[...] = jnp.concatenate(own, 0)
    for s in chunks:
        r.v_conv_weight[s] = ((r.v_conv_weight[s].astype(FULL) - wmean) * wscale).astype(HALF)
    pixels = edges_in(r.pixels, copies)
    for e, values in enumerate(shifted(pixels)):
        r.views[e] = values.astype(HALF)

    def window(views, a, e):
        return views[e, :, a : a + rows].reshape(TOK, channels)

    place = iota((TOK, channels), 0)
    live = (lax.rem(place, WIDE) < GRID) & (lax.rem(lax.div(place, WIDE), rows) + band * rows < GRID)
    feat = 0.0
    tap_sum = 0.0
    for a in range(3):
        for e in range(3):
            seen = window(r.views, a, e)
            feat = feat + dot(seen, r.v_conv_weight[(3 * a + e) * channels : (3 * a + e + 1) * channels])
            tap_sum = tap_sum + seen.astype(FULL)
    feat = jnp.where(live, feat, 0.0)
    r.feat[...] = feat
    r.tap_sum[...] = jnp.broadcast_to(jnp.sum(tap_sum, 1, keepdims=True), (TOK, 128))
    per_group = channels // GROUPS
    entries = 1.0 / (GRID * GRID * per_group)
    same = lax.div(iota((channels, channels), 0), per_group) == lax.div(iota((channels, channels), 1), per_group)
    same = jnp.where(same, 1.0, 0.0)
    cells = TOK // images

    def image_sums(one, two):
        one = jnp.sum(one.reshape(images, cells, channels), 1)
        two = jnp.sum(two.reshape(images, cells, channels), 1)
        return exact_dot(jnp.concatenate([one, two], 0), same)

    def per_image(sums, which):
        return sums[which * images : (which + 1) * images].reshape(images, 1, channels)
    sums = exchange(image_sums(feat, feat * feat), r.sums, 2) * entries
    gmean = per_image(sums, 0)
    gscale = lax.rsqrt(per_image(sums, 1) - gmean * gmean + 1e-05)
    zhat = ((feat.reshape(images, cells, channels) - gmean) * gscale).reshape(TOK, channels)
    r.zhat[...] = zhat
    stem, slope = gelu_parts(zhat * row(r.gn_gain) + row(r.gn_bias))
    r.active[...] = jnp.where(live, stem, 0.0).astype(HALF)
    r.slope[...] = jnp.where(live, slope, 0.0)
    fetches["embed_weight"].wait()
    embedded = dot(r.active[...], r.v_embed_weight[...]) + row(r.embed_bias)
    r.embedded[...] = embedded.astype(HALF).reshape(images, cells, D)
    to_owners(r.embedded, r.patches, 5)
    def norm(values):
        mean = jnp.mean(values, -1, keepdims=True)
        cent = values - mean
        rstd = lax.rsqrt(jnp.mean(cent * cent, -1, keepdims=True) + 1e-06)
        return cent * rstd, rstd

    def norm_back(grad, nhat, rstd, gain):
        s = grad * gain
        inner = s - jnp.mean(s, -1, keepdims=True) - nhat * jnp.mean(s * nhat, -1, keepdims=True)
        return inner * rstd

    fetches["text_embed"].wait()
    r.stream[...] = r.patches[...].reshape(TOK, D).astype(FULL)
    r.stream[CELLS:] = r.v_text_embed[0].astype(FULL)
    nhat, rstd_one = norm(r.stream[...])
    r.nhat_one[...] = nhat
    r.rstd_one[...] = rstd_one
    r.hidden[...] = (nhat * row(r.ln1_gain) + row(r.ln1_bias)).astype(HALF)
    r.t_hidden[:, :TOK] = r.hidden[...].T
    swap_left("qkv", 6, r.t_hidden)
    fetches["qkv_weight"].wait()
    for k, bias in enumerate((r.query_bias, None, r.value_bias)):
        values = dot(r.hidden[...], r.v_qkv_weight[:, k * D : (k + 1) * D])
        if bias is not None:
            values = values + row(bias)
        values = values.astype(HALF)
        r.qkv[:, k * D : (k + 1) * D] = values * 0.125 if k == 0 else values
    key_at = iota((1, TOK), 1)
    key_live = ((key_at < CELLS) & (lax.rem(key_at, WIDE) < GRID)) | ((key_at >= CELLS) & (key_at - CELLS < r.text_len[0]))
    first = iota((TOK, 128), 1) < 64
    zero = jnp.zeros((TOK, 128), HALF)

    def pair_of(ref, k, p):
        return ref[:, pl.ds(pl.multiple_of(k * D + p * 128, 128), 128)]

    def only(values, h):
        return jnp.where(first, values, zero) if h == 0 else jnp.where(first, zero, values)

    def attend(p, carry):
        query, key, value = (pair_of(r.qkv, k, p) for k in range(3))
        sides = []
        for h in range(2):
            scores = jnp.where(key_live, dot_nt(only(query, h), key), -1000000000.0)
            expd = jnp.exp(scores - jnp.max(scores, -1, keepdims=True))
            probs = expd * (1.0 / jnp.sum(expd, -1, keepdims=True))
            probs = probs.astype(HALF)
            r.probs[2 * p + h] = probs
            sides.append(dot(probs, value))
        r.mixed[:, pl.ds(pl.multiple_of(p * 128, 128), 128)] = jnp.where(first, *sides).astype(HALF)
        return carry

    lax.fori_loop(0, HEADS // 2, attend, 0)
    for k in range(4):
        width = D // 4
        r.mixed_bands[k] = jnp.concatenate([jnp.zeros((TOK, 256 - width), HALF), r.mixed[:, k * width : (k + 1) * width]], 1)
    swap_bands("out", 10, r.mixed_bands, r.r_mixed)
    fetches["out_weight"].wait()
    mid = r.stream[...] + dot(r.mixed[...], r.v_out_weight[...]) + row(r.out_bias)
    r.final[...] = mid + row(r.down_bias)
    nhat, rstd_two = norm(mid)
    r.nhat_two[...] = nhat
    r.rstd_two[...] = rstd_two
    r.hidden2[...] = (nhat * row(r.ln2_gain) + row(r.ln2_bias)).astype(HALF)
    fetches["up_weight"].wait()
    r.t_hidden2[:, :TOK] = r.hidden2[...].T
    swap_left("up", 3, r.t_hidden2)

    def feed(k, carry):
        wide = pl.ds(pl.multiple_of(k * D, 128), D)
        act, slope = gelu_parts(dot(r.hidden2[...], r.v_up_weight[:, wide]) + r.up_bias[:, wide])
        r.act[k] = act.astype(HALF)
        r.slopes[k] = slope.astype(HALF)
        return carry

    lax.fori_loop(0, FF // D, feed, 0)
    swap_bands("down", 1, r.act, r.r_act)
    fetches["down_weight"].wait()
    final = r.final[...]
    for k in range(FF // D):
        final = final + dot(r.act[k], r.v_down_weight[k * D : (k + 1) * D])
    r.encoded[0] = dot(gather, final.astype(HALF)).astype(HALF)
    arrived("down")
    unit(down, [(r.t_cot, r.act, r.r_act, 0)])

    def feed_back(k, carry):
        wide = pl.ds(pl.multiple_of(k * D, 128), D)
        d_pre = dot_nt(r.cot[...], r.v_down_weight[wide, :]) * r.slopes[k].astype(FULL)
        r.d_pre[k] = d_pre.astype(HALF)
        r.up_sum[k] = column_sum(r.d_pre[k].astype(FULL))
        return carry

    lax.fori_loop(0, FF // D, feed_back, 0)
    swap_bands("up", 4, r.d_pre, r.r_d_pre)
    grad = 0.0
    for k in range(FF // D):
        grad = grad + dot_nt(r.d_pre[k], r.v_up_weight[:, k * D : (k + 1) * D])
    r.final[...] = grad
    def put(at, values, lo=0):
        r.vec[at : at + 1, lo : lo + values.shape[1]] = values

    r.vec[...] = jnp.zeros(r.vec.shape, FULL)
    cot = r.cot[...].astype(FULL)
    put(8, column_sum(cot))
    for k in range(FF // D):
        put(9 + k, r.up_sum[k])

    grad = r.final[...]
    put(6, column_sum(grad * r.nhat_two[...]))
    put(7, column_sum(grad))
    d_mid = cot + norm_back(grad, r.nhat_two[...], r.rstd_two[...], row(r.ln2_gain))
    r.stream[...] = d_mid
    r.d_attn[...] = d_mid.astype(HALF)
    r.t_attn[:, :TOK] = r.d_attn[...].T
    swap_left("out", 9, r.t_attn)
    put(5, column_sum(r.d_attn[...].astype(FULL)))
    r.d_mixed[...] = dot_nt(r.d_attn[...], r.v_out_weight[...]).astype(HALF)

    arrived("up")
    unit(up, [(r.t_hidden2, r.d_pre, r.r_d_pre, 0)])
    def attend_back(p, carry):
        query, key, value = (pair_of(r.qkv, k, p) for k in range(3))
        d_mixed = pair_of(r.d_mixed, 0, p)
        sides = [[], [], []]
        for h in range(2):
            probs = r.probs[2 * p + h]
            d_probs = dot_nt(only(d_mixed, h), value)
            weight = probs.astype(FULL)
            delta = jnp.sum(d_probs * weight, -1, keepdims=True)
            d_scores = (weight * (d_probs - delta)).astype(HALF)
            sides[0].append(dot(d_scores, key) * 0.125)
            sides[1].append(dot_tn(d_scores, query))
            sides[2].append(dot_tn(probs, d_mixed))
        for k in range(3):
            r.d_qkv[:, pl.ds(pl.multiple_of(k * D + p * 128, 128), 128)] = jnp.where(first, *sides[k]).astype(HALF)
        return carry

    for part in range(3):
        lax.fori_loop(HEADS // 6 * part, HEADS // 6 * (part + 1), attend_back, 0)
        poll(f"back{part}")
    for k in range(4):
        width = 3 * D // 4
        r.d_qkv_bands[k] = jnp.concatenate([r.d_qkv[:, k * width : (k + 1) * width], jnp.zeros((TOK, D - width), HALF)], 1)
    swap_bands("qkv", 7, r.d_qkv_bands, r.r_d_qkv)
    put(3, column_sum(r.d_qkv[:, :D].astype(FULL)))
    put(4, column_sum(r.d_qkv[:, 2 * D :].astype(FULL)))
    grad = dot_nt(r.d_qkv[...], r.v_qkv_weight[...])
    put(1, column_sum(grad * r.nhat_one[...]))
    put(2, column_sum(grad))
    d_stream = r.stream[...] + norm_back(grad, r.nhat_one[...], r.rstd_one[...], row(r.ln1_gain))
    r.text_grad[0] = d_stream[CELLS:]
    at_cell = iota((TOK, D), 0) < CELLS
    r.d_patches[...] = jnp.where(at_cell, d_stream, 0.0).astype(HALF).reshape(r.d_patches.shape)
    def qkv_unit():
        arrived("qkv")
        arrived("out")
        unit(qkv, [(r.t_hidden, r.d_qkv_bands, r.r_d_qkv, 0), (r.t_attn, r.mixed_bands, r.r_mixed, 2)], False)
    to_owners(r.d_patches, r.d_cells, 8, "cells")
    d_cells = r.d_cells[...].reshape(TOK, D)
    put(0, column_sum(d_cells.astype(FULL)))
    d_active = dot_nt(d_cells, r.v_embed_weight[...]).astype(HALF).astype(FULL)
    d_norm = d_active * r.slope[...]
    zhat = r.zhat[...]
    put(13, column_sum(d_norm * zhat))
    put(13, column_sum(d_norm), channels)
    d_hat = d_norm * row(r.gn_gain)
    back = exchange(image_sums(d_hat, d_hat * zhat), r.sums_back, 11, "sums") * entries
    d_feat = d_hat.reshape(images, cells, channels) - per_image(back, 0)
    d_feat = (d_feat - zhat.reshape(images, cells, channels) * per_image(back, 1)) * gscale
    d_feat = jnp.where(live, d_feat.reshape(TOK, channels), 0.0).astype(HALF)
    r.d_feat[...] = d_feat
    r.d_rows[:, 1 : rows + 1] = d_feat.reshape(images, rows, WIDE, channels)
    copies = edge_rows(r.d_rows, 14)
    d_feat = d_feat.astype(FULL)
    put(13, column_sum(r.tap_sum[:, :1] * d_feat) * (1.0 / taps), 2 * channels)
    put(14, column_sum(r.feat[...] * d_feat) * (1.0 / taps))

    def vec_start(stage):
        return send(r.vec if stage == 0 else r.vec_sum.at[stage - 1], r.vec_in.at[stage], slot + stage, partner(links[stage]))

    vec_state = [r.vec[...], 0, vec_start(0)]

    def vec_step():
        total, stage, on_way = vec_state
        on_way.wait_recv()
        total = total + r.vec_in[stage]
        if stage == len(links) - 1:
            r.o_vec[...] = total
        else:
            r.vec_sum[stage] = total
            on_way = vec_start(stage + 1)
        vec_state[:] = [total, stage + 1, on_way]

    poll("edges")
    for e, values in enumerate(shifted(edges_in(r.d_rows, copies))):
        r.d_views[e] = values.astype(HALF)
    grad = 0.0
    for a in range(3):
        for e in range(3):
            seen = window(r.d_views, 2 - a, 2 - e)
            grad = grad + dot_nt(seen, r.v_conv_weight[(3 * a + e) * channels : (3 * a + e + 1) * channels])
    grad = jnp.where(live, grad, 0.0).reshape(images, rows, WIDE, channels)
    r.image_grad[...] = grad[:, :, :GRID]

    poll("grad")
    swap("conv", 12, r.views, r.r_views)
    swap("conv", 13, r.d_feat, r.r_d_feat)
    swap("emb", 14, r.active, r.r_active)
    swap("emb", 15, r.d_cells, r.r_d_cells)

    def columns(values, width):
        total = values.shape[1]
        col = iota((total, 2 * width), 1)
        want = jnp.where(col < width, col, col + width) + core * width
        pick = jnp.where(iota((total, 2 * width), 0) == want, 1.0, 0.0).astype(HALF)
        return dot(values, pick).astype(HALF)

    arrived("conv")
    mine, theirs = columns(r.d_feat[...], channels // 4), columns(r.r_d_feat[...], channels // 4)
    rows_here = pieces["p_c0"].plan.rows
    for a in range(3):
        for e in range(3):
            value = dot_tn(window(r.views, a, e), mine) + dot_tn(window(r.r_views, a, e), theirs)
            value = value.astype(HALF)
            begin = at = (3 * a + e) * channels
            while at < begin + channels:
                line, lo = divmod(at, rows_here)
                block, part = divmod(line, 3)
                size = min(begin + channels - at, rows_here - lo)
                piece = pieces[f"p_c{part}"]
                where = tuple(block >> k & 1 for k in reversed(range(len(piece.plan.first))))
                piece.buf[where + (slice(lo, lo + size),)] = value[at - begin : at - begin + size]
                at += size
    for part in range(3):
        pieces[f"p_c{part}"].start()
    arrived("emb")
    mine, theirs = columns(d_cells, D // 4), columns(r.r_d_cells[...].reshape(TOK, D), D // 4)
    piece = pieces["p_e"]
    value = dot_tn(r.active[...], mine) + dot_tn(r.r_active[...], theirs)
    piece.buf[...] = value.astype(HALF).reshape(piece.plan.shape)
    piece.start()
    poll("end")
    while vec_state[1] < len(links) or any(p.stage < len(p.plan.order) for p in pieces.values()):
        advance(*pieces)
        if vec_state[1] < len(links):
            vec_step()
    for copy in pending:
        copy.wait_send()


def finish_kernel(names, *refs):
    r = types.SimpleNamespace(**dict(zip(names, refs)))
    img, band = lax.axis_index("img"), lax.axis_index("band")
    n_img, n_band = lax.axis_size("img"), lax.axis_size("band")
    far = my_bit(FAR)
    for name in ("encoded", "image_grad", "text_grad"):
        getattr(r, name)[...] = getattr(r, "i_" + name)[...]

    def own(ref, rows):
        if ref.shape[0] == rows:
            return ref[...]
        at = lax.rem(img, ref.shape[0] // rows) * rows
        pick = jnp.where(iota((rows, ref.shape[0]), 1) == iota((rows, ref.shape[0]), 0) + at, 1.0, 0.0)
        return exact_dot(pick, ref[...])

    def lanes(values, at, count):
        width = values.shape[1]
        return exact_dot(values, jnp.where(iota((width, count), 0) == iota((width, count), 1) + at, 1.0, 0.0))

    def half(values):
        width = values.shape[1] // 2
        return jnp.where(far == 0, values[:, :width], values[:, width:])

    share = D // n_img
    r.down[...] = own(r.i_o_down, share)
    r.up[...] = own(r.i_o_up, share)
    both = own(r.i_o_qkv, share)
    r.qkv[...] = both[:, : 3 * D // n_band]
    r.out[...] = both[:, 3 * D // n_band :].T
    vec = r.i_o_vec[...]
    channels = r.i_o_wstat.shape[1]
    r.emb[...] = half(own(r.i_o_emb, channels // n_img))
    mine = lanes(vec, img * share, share)
    for at, name in enumerate(("embed_bias", "ln1_gain", "ln1_bias", "query_bias", "value_bias", "out_bias", "ln2_gain", "ln2_bias", "down_bias")):
        getattr(r, name)[...] = mine[at]
    share = channels // n_img
    r.gn_gain[...] = lanes(vec[8:], img * share, share)[5]
    r.gn_bias[...] = lanes(vec[8:], channels + img * share, share)[5]
    share = FF // n_img
    start = img * share
    line = jnp.sum(jnp.where(iota(vec.shape, 0) == 9 + lax.div(start, D), vec, 0.0), 0, keepdims=True)
    r.up_bias[...] = lanes(jnp.broadcast_to(line, (8, D)), lax.rem(start, D), share)[0]
    cols = channels // n_band
    taps = r.conv.shape[1]
    stats = jnp.concatenate([vec[13:14, 2 * channels :], vec[14:15, :channels], r.i_o_wstat[taps:][:6]], 0)
    stats = lanes(stats, band * cols, cols)
    stand = lanes(r.i_o_wstat[:taps], band * cols, cols)
    grad = half(own(r.i_o_conv, taps)) - stats[0:1] - stand * stats[1:2]
    r.conv[...] = (grad * stats[2:3]).T


def body(
    image,
    conv_weight,
    gn_gain,
    gn_bias,
    embed_weight,
    embed_bias,
    ln1_gain,
    ln1_bias,
    qkv_weight,
    query_bias,
    value_bias,
    out_weight,
    out_bias,
    ln2_gain,
    ln2_bias,
    up_weight,
    up_bias,
    down_weight,
    down_bias,
    text_embed,
    text_len,
    cotangent,
):
    n_img, n_band = lax.axis_size("img"), lax.axis_size("band")
    img, band = lax.axis_index("img"), lax.axis_index("band")
    images, rows = image.shape[:2]
    taps, channels = conv_weight.shape
    img_bits = [("img", k) for k in bits(n_img)]
    one, two, rest = img_bits[:1], img_bits[1:2], img_bits[2:]
    far = [FAR]
    orders = {
        "p_d": (far + one + two, one + two + far, two + one + far),
        "p_u": (far + two + one, one + two + far, two + one + far),
        "p_q": (far + one + two, one + far + two, two + far + one),
    }
    plans = {}
    for name, out in (("p_d", "o_down"), ("p_u", "o_up"), ("p_q", "o_qkv")):
        for k, order in enumerate(orders[name]):
            plans[f"{name}{k}"] = (Plan(n_img, D, 256, FAR, order + rest), out, (0, 256 * k))
    for k in range(3):
        order = (two + one if k == 1 else one + two) + rest + far
        plan = Plan(n_img, taps, channels // 2, None, order, 3)
        plans[f"p_c{k}"] = (plan, "o_conv", (k * plan.rows, 0))
    plans["p_e"] = (Plan(n_img, channels, D // 2, None, two + one + rest + far), "o_emb", (0, 0))
    vec_shape = (16, D)
    arguments = {
        "image": image, "conv_weight": conv_weight, "gn_gain": gn_gain, "gn_bias": gn_bias, "embed_weight": embed_weight,
        "embed_bias": embed_bias, "ln1_gain": ln1_gain, "ln1_bias": ln1_bias, "qkv_weight": qkv_weight, "query_bias": query_bias,
        "value_bias": value_bias, "out_weight": out_weight, "out_bias": out_bias, "ln2_gain": ln2_gain, "ln2_bias": ln2_bias,
        "up_weight": up_weight, "up_bias": up_bias.reshape(1, FF), "down_weight": down_weight, "down_bias": down_bias,
        "text_embed": text_embed, "text_len": text_len, "cotangent": cotangent,
    }
    fetched = ("conv_weight", "embed_weight", "qkv_weight", "cotangent", "text_embed", "out_weight", "up_weight", "down_weight")
    spaces = {name: pl.ANY for name in fetched}
    spaces["text_len"] = pltpu.SMEM
    results = {
        "encoded": (cotangent.shape, HALF),
        "image_grad": (image.shape, FULL),
        "text_grad": (text_embed.shape, FULL),
        "o_down": ((plans["p_d0"][0].rows, D), FULL),
        "o_up": ((plans["p_u0"][0].rows, D), FULL),
        "o_qkv": ((plans["p_q0"][0].rows, D), FULL),
        "o_conv": ((3 * plans["p_c0"][0].rows, channels // 2), FULL),
        "o_emb": ((plans["p_e"][0].rows, D // 2), FULL),
        "o_vec": (vec_shape, FULL),
        "o_wstat": ((taps // n_img + 8, channels), FULL),
    }
    halo = (images, rows + 2, WIDE, channels)
    split = (images, TOK // images, D)
    scratch = {
        "v_" + name: (arguments[name].shape, HALF) for name in fetched
    }
    scratch.update({
        "pixels": (halo, HALF), "views": ((3,) + halo, HALF), "feat": ((TOK, channels), FULL),
        "tap_sum": ((TOK, 128), FULL), "sums": ((n_band, 2 * images, channels), FULL), "sums_back": ((n_band, 2 * images, channels), FULL),
        "zhat": ((TOK, channels), FULL), "active": ((TOK, channels), HALF), "slope": ((TOK, channels), FULL),
        "embedded": (split, HALF), "patches": (split, HALF), "stream": ((TOK, D), FULL), "nhat_one": ((TOK, D), FULL),
        "rstd_one": ((TOK, 1), FULL), "hidden": ((TOK, D), HALF), "qkv": ((TOK, 3 * D), HALF), "probs": ((HEADS, TOK, TOK), HALF),
        "mixed": ((TOK, D), HALF), "nhat_two": ((TOK, D), FULL), "rstd_two": ((TOK, 1), FULL),
        "hidden2": ((TOK, D), HALF), "cot": ((TOK, D), HALF), "final": ((TOK, D), FULL),
        "act": ((4, TOK, D), HALF), "d_pre": ((4, TOK, D), HALF), "up_sum": ((FF // D, 1, D), FULL), "vec": (vec_shape, FULL),
        "d_attn": ((TOK, D), HALF), "d_mixed": ((TOK, D), HALF), "d_qkv": ((TOK, 3 * D), HALF),
        "d_patches": (split, HALF), "d_cells": (split, HALF), "d_feat": ((TOK, channels), HALF), "d_rows": (halo, HALF),
        "d_views": ((3,) + halo, HALF), "mixed_bands": ((4, TOK, 256), HALF), "d_qkv_bands": ((4, TOK, D), HALF), "t_cot": ((D, 2 * TOK), HALF), "t_hidden": ((D, 2 * TOK), HALF), "t_hidden2": ((D, 2 * TOK), HALF), "t_attn": ((D, 2 * TOK), HALF), "slopes": ((4, TOK, D), HALF),
        "r_act": ((2, TOK, D), HALF), "r_d_pre": ((2, TOK, D), HALF),
        "r_d_qkv": ((2, TOK, D), HALF), "r_mixed": ((2, TOK, 256), HALF),
        "r_views": ((3,) + halo, HALF), "r_d_feat": ((TOK, channels), HALF), "r_active": ((TOK, channels), HALF), "r_d_cells": (split, HALF),
    })
    slots = 32
    for name, (plan, _, _) in plans.items():
        for k, shape in enumerate(plan.scratch()):
            scratch[f"{name}_{k}"] = (shape, HALF)
        slots += len(plan.order)
    n_links = 2 + len(img_bits)
    scratch["vec_sum"] = ((n_links,) + vec_shape, FULL)
    scratch["vec_in"] = ((n_links,) + vec_shape, FULL)
    slots += n_links
    sems = {"fetch_sem": 8, "send_sem": slots, "recv_sem": slots}
    names = list(arguments) + list(results) + list(scratch) + list(sems)
    whole = lambda space: pl.BlockSpec(memory_space=space)
    outs = pl.pallas_call(
        functools.partial(layer_kernel, names, plans),
        out_shape=[jax.ShapeDtypeStruct(*v) for v in results.values()],
        in_specs=[whole(spaces.get(name, pltpu.VMEM)) for name in arguments],
        out_specs=[whole(pltpu.VMEM)] * len(results),
        scratch_shapes=[pltpu.VMEM(*v) for v in scratch.values()] + [pltpu.SemaphoreType.DMA((n,)) for n in sems.values()],
        compiler_params=pltpu.CompilerParams(collective_id=0, has_side_effects=True, vmem_limit_bytes=63 * 2**20),
    )(*arguments.values())
    finished = {
        "encoded": (cotangent.shape, HALF),
        "image_grad": (image.shape, FULL),
        "text_grad": (text_embed.shape, FULL),
        "conv": ((channels // n_band, taps // n_img), FULL),
        "gn_gain": ((channels // n_img,), FULL),
        "gn_bias": ((channels // n_img,), FULL),
        "emb": ((channels // n_img, D // n_band), FULL),
        "embed_bias": ((D // n_img,), FULL),
        "ln1_gain": ((D // n_img,), FULL),
        "ln1_bias": ((D // n_img,), FULL),
        "qkv": ((D // n_img, 3 * D // n_band), FULL),
        "query_bias": ((D // n_img,), FULL),
        "value_bias": ((D // n_img,), FULL),
        "out": ((D // n_band, D // n_img), FULL),
        "out_bias": ((D // n_img,), FULL),
        "ln2_gain": ((D // n_img,), FULL),
        "ln2_bias": ((D // n_img,), FULL),
        "up": ((D // n_img, FF // n_band), FULL),
        "up_bias": ((FF // n_img,), FULL),
        "down": ((D // n_img, FF // n_band), FULL),
        "down_bias": ((D // n_img,), FULL),
    }
    names = ["i_" + name for name in results] + list(finished)
    outs = pl.pallas_call(
        functools.partial(finish_kernel, names),
        out_shape=[jax.ShapeDtypeStruct(*v) for v in finished.values()],
        in_specs=[whole(pltpu.VMEM)] * len(results),
        out_specs=[whole(pltpu.VMEM)] * len(finished),
    )(*outs)
    res = dict(zip(finished, outs))
    res["conv"], res["down"] = res["conv"].T, res["down"].T
    return tuple(res.values())


def solution(mesh):
    in_specs = (
        P("img", "band", None, None),
        P(),
        P(),
        P(),
        P(),
        P(),
        P(),
        P(),
        P(),
        P(),
        P(),
        P(),
        P(),
        P(),
        P(),
        P(),
        P(),
        P(),
        P(),
        P(("img", "band"), None, None),
        P(("img", "band")),
        P(("img", "band"), None, None),
    )
    out_specs = (
        P(("img", "band"), None, None),
        P("img", "band", None, None),
        P(("img", "band"), None, None),
        P("img", "band"),
        P("img"),
        P("img"),
        P("img", "band"),
        P("img"),
        P("img"),
        P("img"),
        P("img", "band"),
        P("img"),
        P("img"),
        P("band", "img"),
        P("img"),
        P("img"),
        P("img"),
        P("img", "band"),
        P("img"),
        P("band", "img"),
        P("img"),
    )
    return jax.shard_map(body, mesh=mesh, in_specs=in_specs, out_specs=out_specs, check_vma=False)
```

```python
import functools
import types

import jax
import jax.numpy as jnp
from jax import lax
from jax.experimental import pallas as pl
from jax.experimental.pallas import tpu as pltpu
from jax.sharding import PartitionSpec as P

D = 768
FF = 3072
HEADS = 12
GROUPS = 32
GRID = 14
TEXT = 32
PATCHES = 196
WIDE = 16
TOK = 256
CELLS = GRID * WIDE
HALF = jnp.bfloat16
FULL = jnp.float32
MESH_ID = pl.DeviceIdType.MESH
CORE = ("band", 1)
FAR = ("band", 2)


def bit_of(value, bit):
    return lax.rem(lax.div(value, bit), 2)


def flip(value, bit):
    return value + bit * (1 - 2 * bit_of(value, bit))


def partner(label):
    axis, bit = label
    img, band = lax.axis_index("img"), lax.axis_index("band")
    return (flip(img, bit), band) if axis == "img" else (img, flip(band, bit))


def my_bit(label):
    axis, bit = label
    return bit_of(lax.axis_index(axis), bit)


def bits(count):
    return [1 << k for k in range(count.bit_length() - 1)]


def route(letters, n_img):
    near = [("img", k) for k in bits(n_img)]
    routes = {"c": [CORE], "y": [FAR], "Y": [FAR], "x": near[:1], "z": near[1:2], "w": near[2:]}
    return sum((routes[letter] for letter in letters), [])


class Plan:
    def __init__(self, n_img, rows, width, lead, order, parts=1):
        self.width = width
        split = [("img", k) for k in reversed(bits(n_img)) if (rows // n_img) * k % 16 == 0]
        self.rows = (rows >> len(split)) // parts
        self.first = ([lead] if lead else []) + split
        rest = [("img", k) for k in bits(n_img) if ("img", k) not in split]
        self.order = [lab for lab in order if lab not in rest] + rest
        self.shapes = []
        labels = list(self.first)
        for lab in self.order:
            if lab in labels:
                labels.remove(lab)
            self.shapes.append((2,) * len(labels) + (self.rows, width))
        self.shape = (2,) * len(self.first) + (self.rows, width)

    def scratch(self):
        return [self.shape] + self.shapes


class Once:
    def __init__(self, copy):
        self.copy, self.left = copy, {"wait", "wait_send", "wait_recv"}
        copy.start()

    def _wait(self, kind):
        if kind in self.left:
            self.left.remove(kind)
            getattr(self.copy, kind)()

    def wait(self):
        self._wait("wait")

    def wait_send(self):
        self._wait("wait_send")

    def wait_recv(self):
        self._wait("wait_recv")


class Piece:
    def __init__(self, plan, refs, sems, slot, out, at, pending):
        self.pending = pending
        self.plan, self.buf, self.recv = plan, refs[0], refs[1:]
        self.sems, self.slot = sems, slot
        self.labels, self.cur = list(plan.first), refs[0]
        self.sent = []
        self.out = out.at[pl.ds(at[0], plan.rows), pl.ds(at[1], plan.width)]
        self.stage = 0

    def _index(self, label, which):
        at = self.labels.index(label)
        return (slice(None),) * at + (which,)

    def start(self):
        label = self.plan.order[self.stage]
        src = self.cur
        if label in self.labels:
            src = src.at[self._index(label, 1 - my_bit(label))]
        send, recv = self.sems
        copy = pltpu.make_async_remote_copy(
            src_ref=src,
            dst_ref=self.recv[self.stage],
            send_sem=send.at[self.slot + self.stage],
            recv_sem=recv.at[self.slot + self.stage],
            device_id=partner(label),
            device_id_type=MESH_ID,
        )
        self.sent.append(Once(copy))
        self.pending.append(self.sent[-1])

    def step(self):
        label = self.plan.order[self.stage]
        self.sent[self.stage].wait_recv()
        mine = self.cur
        if label in self.labels:
            mine = mine[self._index(label, my_bit(label))]
            self.labels.remove(label)
        else:
            mine = mine[...]
        got = self.recv[self.stage]
        self.stage += 1
        if self.stage == len(self.plan.order):
            self.out[...] = (got[...].astype(FULL) + mine.astype(FULL)).reshape(self.out.shape)
        else:
            got[...] = got[...] + mine
            self.cur = got
            self.start()


def dot(left, right):
    return jnp.dot(left, right, preferred_element_type=FULL)


def dot_tn(left, right):
    return lax.dot_general(left, right, (((0,), (0,)), ((), ())), preferred_element_type=FULL)


def dot_nt(left, right):
    return lax.dot_general(left, right, (((1,), (1,)), ((), ())), preferred_element_type=FULL)


def exact_dot(left, right):
    return jnp.dot(left, right, precision=lax.Precision.HIGHEST, preferred_element_type=FULL)


def gelu_parts(x):
    cdf = 0.5 + 0.5 * lax.erf(x * 0.7071067811865476)
    pdf = jnp.exp(-0.5 * x * x) * 0.3989422804014327
    return x * cdf, cdf + x * pdf


def iota(shape, axis):
    return lax.broadcasted_iota(jnp.int32, shape, axis)


def row(ref):
    return ref[...].reshape(1, -1)


def column_sum(values):
    return jnp.sum(values, 0, keepdims=True)


def shifted(values):
    edge = jnp.zeros(values.shape[:2] + (1, values.shape[3]), FULL)
    left = jnp.concatenate([edge, values[:, :, : WIDE - 1]], 2)
    right = jnp.concatenate([values[:, :, 1:], edge], 2)
    return left, values, right


DOWN, UP, QKV = ("p_d0", "p_d1", "p_d2"), ("p_u0", "p_u1", "p_u2"), ("p_q0", "p_q1", "p_q2")
ORDERS = {
    "p_d0": "xzwy",
    "p_d1": "yzxw",
    "p_d2": "zxyw",
    "p_u0": "yxzw",
    "p_u1": "xyzw",
    "p_u2": "wyxz",
    "p_q0": "yxzw",
    "p_q1": "xzyw",
    "p_q2": "yxzw",
    "p_c0": "xzYw",
    "p_c1": "xwzY",
    "p_c2": "xzwY",
    "p_e": "zxwY",
    "vec": "zwycx",
}
POLLS = {
    "back1": (
        "p_d0",
        "p_d1",
        "p_d2",
    ),
    "cells": (
        "qkv",
        "+p_q1",
        "p_u1",
        "p_u0",
    ),
    "sums": (
        "p_d2",
        "p_d0",
    ),
    "edges": (
        "+p_q2",
        "+p_q0",
        "p_u1",
        "p_u2",
        "p_d1",
        "p_d2",
    ),
    "grad": (
        "p_q1",
        "vec",
        "p_d0",
    ),
    "end": (
        "p_u1",
        "p_u0",
        "p_d2",
        "p_d1",
        "p_q2",
        "p_q1",
        "p_c0",
        "vec",
        "p_c1",
        "p_e",
        "p_c2",
        "p_u1",
        "p_u0",
        "p_q0",
        "p_c0",
        "p_d1",
        "p_q2",
        "p_e",
        "p_c2",
        "p_c1",
        "p_u2",
        "p_u0",
        "p_d0",
        "p_q2",
        "p_q0",
        "p_e",
        "p_q1",
        "p_c2",
        "p_c1",
        "p_u2",
        "vec",
        "p_c0",
        "p_q2",
        "p_e",
        "vec",
        "p_c2",
        "p_q0",
        "p_c1",
        "p_u2",
        "p_q1",
        "vec",
        "p_c0",
        "p_q0",
    ),
}


def layer_kernel(names, plans, *refs):
    r = types.SimpleNamespace(**dict(zip(names, refs)))
    img, band = lax.axis_index("img"), lax.axis_index("band")
    n_img, n_band = lax.axis_size("img"), lax.axis_size("band")
    images, _, rows = r.image.shape[:3]
    channels = r.conv_weight.shape[1]
    core = my_bit(CORE)
    others = [lax.rem(band + d, n_band) for d in range(n_band)]

    fetches = {}

    def fetch(name, at):
        copy = pltpu.make_async_copy(getattr(r, name), getattr(r, "v_" + name), r.fetch_sem.at[at])
        fetches[name] = Once(copy)

    for at, name in enumerate(("cotangent", "conv_weight", "embed_weight", "qkv_weight", "text_embed", "out_weight", "up_weight", "down_weight")):
        fetch(name, at)

    links = [CORE, FAR] + [("img", k) for k in bits(n_img)]
    barrier = pltpu.get_barrier_semaphore()
    for d in range(1, n_band):
        pl.semaphore_signal(barrier, inc=1, device_id=(img, others[d]), device_id_type=MESH_ID)
    for label in links[2:]:
        pl.semaphore_signal(barrier, inc=1, device_id=partner(label), device_id_type=MESH_ID)

    pending = []

    def send(src, dst, at, device):
        copy = pltpu.make_async_remote_copy(
            src_ref=src, dst_ref=dst, send_sem=r.send_sem.at[at], recv_sem=r.recv_sem.at[at],
            device_id=device, device_id_type=MESH_ID)
        pending.append(Once(copy))
        return pending[-1]

    def edge_rows(ref, at):
        up = send(ref.at[:, rows], ref.at[:, 0], at, (img, others[1]))
        down = send(ref.at[:, 1], ref.at[:, rows + 1], at + 1, (img, others[n_band - 1]))
        return up, down

    def edges_in(ref, copies):
        for copy in copies:
            copy.wait_recv()
        values = ref[...].astype(FULL)
        at = iota(values.shape, 1) + band * rows
        return jnp.where((at == 0) | (at > n_band * rows), 0.0, values)

    def exchange(values, slots, at, meanwhile=None):
        slots[0] = values
        copies = [send(slots.at[0], slots.at[d], at + d - 1, (img, others[d])) for d in range(1, n_band)]
        poll(meanwhile)
        for d, copy in enumerate(copies, 1):
            copy.wait_recv()
            values = values + slots[d]
        return values

    def to_owners(src, dst, at, meanwhile=None):
        copies = [send(src.at[others[d]], dst.at[band], at + d - 1, (img, others[d])) for d in range(1, n_band)]
        dst[band] = src[band]
        poll(meanwhile)
        for copy in copies:
            copy.wait_recv()

    swaps = {}
    base = 16

    def swap(name, at, src, dst):
        swaps.setdefault(name, []).append(send(src, dst, base + at, partner(CORE)))

    def swap_bands(name, at, src, dst):
        for y in range(2):
            swap(name, at + y, src.at[2 * y + 1 - core], dst.at[y])

    def swap_left(name, at, ref):
        swap(name, at, ref.at[:, pl.ds(0, TOK)], ref.at[:, pl.ds(TOK, TOK)])

    def arrived(name):
        for copy in swaps[name]:
            copy.wait_recv()

    pieces = {}
    slot = base + 16
    for name, (plan, out, at) in plans.items():
        refs = [getattr(r, f"{name}_{k}") for k in range(1 + len(plan.order))]
        pieces[name] = Piece(plan, refs, (r.send_sem, r.recv_sem), slot, getattr(r, out), at, pending)
        slot += len(plan.order)

    down, up, qkv = DOWN, UP, QKV

    def poll(point):
        for name in POLLS.get(point, ()):
            if name[0] == "+":
                pieces[name[1:]].start()
            elif name == "vec":
                vec_step()
            elif name == "qkv":
                qkv_unit()
            else:
                advance(name)

    def advance(*names):
        for name in names:
            if pieces[name].stage < len(pieces[name].plan.order):
                pieces[name].step()

    def unit(parts, terms, start=True):
        for j, name in enumerate(parts):
            piece = pieces[name]
            wide = slice(256 * j, 256 * (j + 1))
            for y in range(2):
                value = 0.0
                for left, right, got, at in terms:
                    if j >= at:
                        cut = slice(256 * (j - at), 256 * (j - at + 1))
                        both = jnp.concatenate([right[2 * y + core, :, cut], got[y, :, cut]], 0)
                        value = value + dot(left[...], both)
                piece.buf[y] = value.astype(HALF).reshape(piece.plan.shape[1:])
            if start:
                piece.start()

    r.pixels[:, 1 : rows + 1, GRID:, :] = jnp.zeros((images, rows, WIDE - GRID, channels), HALF)
    for k in range(rows):
        line = r.image[:, :, k, :].astype(FULL)
        r.pixels[:, k + 1, :GRID, :] = jnp.where(band * rows + k < GRID, line, 0.0).astype(HALF)
    fetches["cotangent"].wait()
    seq = r.cotangent.shape[1]

    def token_of(at):
        return jnp.where(at < CELLS, jnp.where(lax.rem(at, WIDE) < GRID, lax.div(at, WIDE) * GRID + lax.rem(at, WIDE), -1), at - CELLS + PATCHES)

    spread = jnp.where(token_of(iota((TOK, seq), 0)) == iota((TOK, seq), 1), 1.0, 0.0).astype(HALF)
    gather = jnp.where(token_of(iota((seq, TOK), 1)) == iota((seq, TOK), 0), 1.0, 0.0).astype(HALF)
    r.cot[...] = dot(spread, r.v_cotangent[0]).astype(HALF)

    r.t_cot[:, :TOK] = r.cot[...].T
    pl.semaphore_wait(barrier, n_band - 1 + len(links) - 2)
    copies = edge_rows(r.pixels, 0)

    swap_left("down", 0, r.t_cot)

    fetches["conv_weight"].wait()
    taps = r.conv_weight.shape[0]
    chunks = [slice(k, k + 256) for k in range(0, taps, 256)]
    wmean = sum(column_sum(r.v_conv_weight[s].astype(FULL)) for s in chunks) * (1.0 / taps)
    wvar = 0.0
    for s in chunks:
        cent = r.v_conv_weight[s].astype(FULL) - wmean
        wvar = wvar + column_sum(cent * cent)
    wscale = lax.rsqrt(wvar * (1.0 / taps) + 1e-05)
    taps_here = taps // n_img
    if taps_here % 16 == 0:
        own = r.v_conv_weight[pl.ds(pl.multiple_of(img * taps_here, 16), taps_here)]
    else:
        own = jnp.where(iota((taps_here, taps), 1) == iota((taps_here, taps), 0) + img * taps_here, 1.0, 0.0).astype(HALF)
        own = dot(own, r.v_conv_weight[...]).astype(HALF)
    own = ((own.astype(FULL) - wmean) * wscale, jnp.broadcast_to(wscale, (8, channels)))
    r.o_wstat[...] = jnp.concatenate(own, 0)
    for s in chunks:
        r.v_conv_weight[s] = ((r.v_conv_weight[s].astype(FULL) - wmean) * wscale).astype(HALF)
    pixels = edges_in(r.pixels, copies)
    for e, values in enumerate(shifted(pixels)):
        r.views[e] = values.astype(HALF)
    swap("conv", 12, r.views, r.r_views)

    def window(views, a, e):
        return views[e, :, a : a + rows].reshape(TOK, channels)

    place = iota((TOK, channels), 0)
    live = (lax.rem(place, WIDE) < GRID) & (lax.rem(lax.div(place, WIDE), rows) + band * rows < GRID)
    feat = 0.0
    tap_sum = 0.0
    for a in range(3):
        for e in range(3):
            seen = window(r.views, a, e)
            feat = feat + dot(seen, r.v_conv_weight[(3 * a + e) * channels : (3 * a + e + 1) * channels])
            tap_sum = tap_sum + seen.astype(FULL)
    feat = jnp.where(live, feat, 0.0)
    r.feat[...] = feat
    r.tap_sum[...] = jnp.broadcast_to(jnp.sum(tap_sum, 1, keepdims=True), (TOK, 128))
    per_group = channels // GROUPS
    entries = 1.0 / (GRID * GRID * per_group)
    same = lax.div(iota((channels, channels), 0), per_group) == lax.div(iota((channels, channels), 1), per_group)
    same = jnp.where(same, 1.0, 0.0)
    cells = TOK // images

    def image_sums(one, two):
        one = jnp.sum(one.reshape(images, cells, channels), 1)
        two = jnp.sum(two.reshape(images, cells, channels), 1)
        return exact_dot(jnp.concatenate([one, two], 0), same)

    def per_image(sums, which):
        return sums[which * images : (which + 1) * images].reshape(images, 1, channels)
    sums = exchange(image_sums(feat, feat * feat), r.sums, 2) * entries
    gmean = per_image(sums, 0)
    gscale = lax.rsqrt(per_image(sums, 1) - gmean * gmean + 1e-05)
    zhat = ((feat.reshape(images, cells, channels) - gmean) * gscale).reshape(TOK, channels)
    r.zhat[...] = zhat
    stem, slope = gelu_parts(zhat * row(r.gn_gain) + row(r.gn_bias))
    r.active[...] = jnp.where(live, stem, 0.0).astype(HALF)
    r.slope[...] = jnp.where(live, slope, 0.0)
    swap("emb", 14, r.active, r.r_active)
    fetches["embed_weight"].wait()
    embedded = dot(r.active[...], r.v_embed_weight[...]) + row(r.embed_bias)
    r.embedded[...] = embedded.astype(HALF).reshape(images, cells, D)
    to_owners(r.embedded, r.patches, 5)
    def norm(values):
        mean = jnp.mean(values, -1, keepdims=True)
        cent = values - mean
        rstd = lax.rsqrt(jnp.mean(cent * cent, -1, keepdims=True) + 1e-06)
        return cent * rstd, rstd

    def norm_back(grad, nhat, rstd, gain):
        s = grad * gain
        inner = s - jnp.mean(s, -1, keepdims=True) - nhat * jnp.mean(s * nhat, -1, keepdims=True)
        return inner * rstd

    fetches["text_embed"].wait()
    r.stream[...] = r.patches[...].reshape(TOK, D).astype(FULL)
    r.stream[CELLS:] = r.v_text_embed[0].astype(FULL)
    nhat, rstd_one = norm(r.stream[...])
    r.nhat_one[...] = nhat
    r.rstd_one[...] = rstd_one
    r.hidden[...] = (nhat * row(r.ln1_gain) + row(r.ln1_bias)).astype(HALF)
    r.t_hidden[:, :TOK] = r.hidden[...].T
    swap_left("qkv", 6, r.t_hidden)
    fetches["qkv_weight"].wait()
    for k, bias in enumerate((r.query_bias, None, r.value_bias)):
        values = dot(r.hidden[...], r.v_qkv_weight[:, k * D : (k + 1) * D])
        if bias is not None:
            values = values + row(bias)
        values = values.astype(HALF)
        r.qkv[:, k * D : (k + 1) * D] = values * 0.125 if k == 0 else values
    key_at = iota((1, TOK), 1)
    key_live = ((key_at < CELLS) & (lax.rem(key_at, WIDE) < GRID)) | ((key_at >= CELLS) & (key_at - CELLS < r.text_len[0]))
    first = iota((TOK, 128), 1) < 64
    zero = jnp.zeros((TOK, 128), HALF)

    def pair_of(ref, k, p):
        return ref[:, k * D + p * 128 : k * D + (p + 1) * 128]

    def only(values, h):
        return jnp.where(first, values, zero) if h == 0 else jnp.where(first, zero, values)

    def attend(p):
        query, key, value = (pair_of(r.qkv, k, p) for k in range(3))
        sides = []
        for h in range(2):
            scores = jnp.where(key_live, dot_nt(only(query, h), key), -1000000000.0)
            expd = jnp.exp(scores - jnp.max(scores, -1, keepdims=True))
            probs = expd * (1.0 / jnp.sum(expd, -1, keepdims=True))
            probs = probs.astype(HALF)
            r.probs[2 * p + h] = probs
            sides.append(dot(probs, value))
        r.mixed[:, p * 128 : (p + 1) * 128] = jnp.where(first, *sides).astype(HALF)

    for p in range(HEADS // 2):
        attend(p)
    for k in range(4):
        width = D // 4
        r.mixed_bands[k] = jnp.concatenate([jnp.zeros((TOK, 256 - width), HALF), r.mixed[:, k * width : (k + 1) * width]], 1)
    swap_bands("out", 10, r.mixed_bands, r.r_mixed)
    fetches["out_weight"].wait()
    mid = r.stream[...] + dot(r.mixed[...], r.v_out_weight[...]) + row(r.out_bias)
    r.final[...] = mid + row(r.down_bias)
    nhat, rstd_two = norm(mid)
    r.nhat_two[...] = nhat
    r.rstd_two[...] = rstd_two
    r.hidden2[...] = (nhat * row(r.ln2_gain) + row(r.ln2_bias)).astype(HALF)
    fetches["up_weight"].wait()
    r.t_hidden2[:, :TOK] = r.hidden2[...].T
    swap_left("up", 3, r.t_hidden2)

    for k in range(FF // D):
        wide = slice(k * D, (k + 1) * D)
        act, slope = gelu_parts(dot(r.hidden2[...], r.v_up_weight[:, wide]) + r.up_bias[:, wide])
        r.act[k] = act.astype(HALF)
        r.slopes[k] = slope.astype(HALF)
    swap_bands("down", 1, r.act, r.r_act)
    fetches["down_weight"].wait()
    final = r.final[...]
    for k in range(FF // D):
        final = final + dot(r.act[k], r.v_down_weight[k * D : (k + 1) * D])
    r.encoded[0] = dot(gather, final.astype(HALF)).astype(HALF)
    arrived("down")
    unit(down, [(r.t_cot, r.act, r.r_act, 0)])

    for k in range(FF // D):
        wide = slice(k * D, (k + 1) * D)
        d_pre = dot_nt(r.cot[...], r.v_down_weight[wide, :]) * r.slopes[k].astype(FULL)
        r.d_pre[k] = d_pre.astype(HALF)
        r.up_sum[k] = column_sum(r.d_pre[k].astype(FULL))
    swap_bands("up", 4, r.d_pre, r.r_d_pre)
    grad = 0.0
    for k in range(FF // D):
        grad = grad + dot_nt(r.d_pre[k], r.v_up_weight[:, k * D : (k + 1) * D])
    r.final[...] = grad
    def put(at, values, lo=0):
        r.vec[at : at + 1, lo : lo + values.shape[1]] = values

    r.vec[...] = jnp.zeros(r.vec.shape, FULL)
    cot = r.cot[...].astype(FULL)
    put(8, column_sum(cot))
    for k in range(FF // D):
        put(9 + k, r.up_sum[k])

    grad = r.final[...]
    put(6, column_sum(grad * r.nhat_two[...]))
    put(7, column_sum(grad))
    d_mid = cot + norm_back(grad, r.nhat_two[...], r.rstd_two[...], row(r.ln2_gain))
    r.stream[...] = d_mid
    r.d_attn[...] = d_mid.astype(HALF)
    r.t_attn[:, :TOK] = r.d_attn[...].T
    swap_left("out", 9, r.t_attn)
    put(5, column_sum(r.d_attn[...].astype(FULL)))
    r.d_mixed[...] = dot_nt(r.d_attn[...], r.v_out_weight[...]).astype(HALF)

    arrived("up")
    unit(up, [(r.t_hidden2, r.d_pre, r.r_d_pre, 0)])
    def attend_back(p):
        query, key, value = (pair_of(r.qkv, k, p) for k in range(3))
        d_mixed = pair_of(r.d_mixed, 0, p)
        sides = [[], [], []]
        for h in range(2):
            probs = r.probs[2 * p + h]
            d_probs = dot_nt(only(d_mixed, h), value)
            weight = probs.astype(FULL)
            delta = jnp.sum(d_probs * weight, -1, keepdims=True)
            d_scores = (weight * (d_probs - delta)).astype(HALF)
            sides[0].append(dot(d_scores, key) * 0.125)
            sides[1].append(dot_tn(d_scores, query))
            sides[2].append(dot_tn(probs, d_mixed))
        for k in range(3):
            r.d_qkv[:, k * D + p * 128 : k * D + (p + 1) * 128] = jnp.where(first, *sides[k]).astype(HALF)

    for p in range(HEADS // 2):
        attend_back(p)
        poll(f"back{p}")
    for k in range(4):
        width = 3 * D // 4
        r.d_qkv_bands[k] = jnp.concatenate([r.d_qkv[:, k * width : (k + 1) * width], jnp.zeros((TOK, D - width), HALF)], 1)
    swap_bands("qkv", 7, r.d_qkv_bands, r.r_d_qkv)
    put(3, column_sum(r.d_qkv[:, :D].astype(FULL)))
    put(4, column_sum(r.d_qkv[:, 2 * D :].astype(FULL)))
    grad = dot_nt(r.d_qkv[...], r.v_qkv_weight[...])
    put(1, column_sum(grad * r.nhat_one[...]))
    put(2, column_sum(grad))
    d_stream = r.stream[...] + norm_back(grad, r.nhat_one[...], r.rstd_one[...], row(r.ln1_gain))
    r.text_grad[0] = d_stream[CELLS:]
    at_cell = iota((TOK, D), 0) < CELLS
    r.d_patches[...] = jnp.where(at_cell, d_stream, 0.0).astype(HALF).reshape(r.d_patches.shape)
    def qkv_unit():
        arrived("qkv")
        arrived("out")
        unit(qkv, [(r.t_hidden, r.d_qkv_bands, r.r_d_qkv, 0), (r.t_attn, r.mixed_bands, r.r_mixed, 2)], False)
    to_owners(r.d_patches, r.d_cells, 8, "cells")
    swap("emb", 15, r.d_cells, r.r_d_cells)
    d_cells = r.d_cells[...].reshape(TOK, D)
    put(0, column_sum(d_cells.astype(FULL)))
    d_active = dot_nt(d_cells, r.v_embed_weight[...]).astype(HALF).astype(FULL)
    d_norm = d_active * r.slope[...]
    zhat = r.zhat[...]
    put(13, column_sum(d_norm * zhat))
    put(13, column_sum(d_norm), channels)
    d_hat = d_norm * row(r.gn_gain)
    back = exchange(image_sums(d_hat, d_hat * zhat), r.sums_back, 11, "sums") * entries
    d_feat = d_hat.reshape(images, cells, channels) - per_image(back, 0)
    d_feat = (d_feat - zhat.reshape(images, cells, channels) * per_image(back, 1)) * gscale
    d_feat = jnp.where(live, d_feat.reshape(TOK, channels), 0.0).astype(HALF)
    r.d_feat[...] = d_feat
    r.d_rows[:, 1 : rows + 1] = d_feat.reshape(images, rows, WIDE, channels)
    copies = edge_rows(r.d_rows, 14)
    swap("conv", 13, r.d_feat, r.r_d_feat)
    d_feat = d_feat.astype(FULL)
    put(13, column_sum(r.tap_sum[:, :1] * d_feat) * (1.0 / taps), 2 * channels)
    put(14, column_sum(r.feat[...] * d_feat) * (1.0 / taps))

    vec_links = route(ORDERS["vec"], n_img)

    def vec_start(stage):
        return send(r.vec if stage == 0 else r.vec_sum.at[stage - 1], r.vec_in.at[stage], slot + stage, partner(vec_links[stage]))

    vec_state = [r.vec[...], 0, vec_start(0)]

    def vec_step():
        total, stage, on_way = vec_state
        on_way.wait_recv()
        total = total + r.vec_in[stage]
        if stage == len(links) - 1:
            r.o_vec[...] = total
        else:
            r.vec_sum[stage] = total
            on_way = vec_start(stage + 1)
        vec_state[:] = [total, stage + 1, on_way]

    poll("edges")
    for e, values in enumerate(shifted(edges_in(r.d_rows, copies))):
        r.d_views[e] = values.astype(HALF)
    grad = 0.0
    for a in range(3):
        for e in range(3):
            seen = window(r.d_views, 2 - a, 2 - e)
            grad = grad + dot_nt(seen, r.v_conv_weight[(3 * a + e) * channels : (3 * a + e + 1) * channels])
    grad = jnp.where(live, grad, 0.0).reshape(images, rows, WIDE, channels)
    r.image_grad[...] = grad[:, :, :GRID]

    poll("grad")

    def columns(values, width):
        total = values.shape[1]
        col = iota((total, 2 * width), 1)
        want = jnp.where(col < width, col, col + width) + core * width
        pick = jnp.where(iota((total, 2 * width), 0) == want, 1.0, 0.0).astype(HALF)
        return dot(values, pick).astype(HALF)

    arrived("conv")
    mine, theirs = columns(r.d_feat[...], channels // 4), columns(r.r_d_feat[...], channels // 4)
    rows_here = pieces["p_c0"].plan.rows
    for a in range(3):
        for e in range(3):
            value = dot_tn(window(r.views, a, e), mine) + dot_tn(window(r.r_views, a, e), theirs)
            value = value.astype(HALF)
            begin = at = (3 * a + e) * channels
            while at < begin + channels:
                line, lo = divmod(at, rows_here)
                block, part = divmod(line, 3)
                size = min(begin + channels - at, rows_here - lo)
                piece = pieces[f"p_c{part}"]
                where = tuple(block >> k & 1 for k in reversed(range(len(piece.plan.first))))
                piece.buf[where + (slice(lo, lo + size),)] = value[at - begin : at - begin + size]
                at += size
    for part in range(3):
        pieces[f"p_c{part}"].start()
    arrived("emb")
    mine, theirs = columns(d_cells, D // 4), columns(r.r_d_cells[...].reshape(TOK, D), D // 4)
    piece = pieces["p_e"]
    value = dot_tn(r.active[...], mine) + dot_tn(r.r_active[...], theirs)
    piece.buf[...] = value.astype(HALF).reshape(piece.plan.shape)
    piece.start()
    poll("end")
    while vec_state[1] < len(links) or any(p.stage < len(p.plan.order) for p in pieces.values()):
        advance(*pieces)
        if vec_state[1] < len(links):
            vec_step()
    for copy in pending:
        copy.wait_send()


def finish_kernel(names, *refs):
    r = types.SimpleNamespace(**dict(zip(names, refs)))
    img, band = lax.axis_index("img"), lax.axis_index("band")
    n_img, n_band = lax.axis_size("img"), lax.axis_size("band")
    far = my_bit(FAR)
    r.encoded[...] = r.i_encoded[...]
    r.text_grad[...] = r.i_text_grad[...]
    for k in range(r.image_grad.shape[2]):
        r.image_grad[:, :, k, :] = r.i_image_grad[:, k]

    def own(ref, rows):
        if ref.shape[0] == rows:
            return ref[...]
        at = lax.rem(img, ref.shape[0] // rows) * rows
        pick = jnp.where(iota((rows, ref.shape[0]), 1) == iota((rows, ref.shape[0]), 0) + at, 1.0, 0.0)
        return exact_dot(pick, ref[...])

    def lanes(values, at, count):
        width = values.shape[1]
        return exact_dot(values, jnp.where(iota((width, count), 0) == iota((width, count), 1) + at, 1.0, 0.0))

    def half(values):
        width = values.shape[1] // 2
        return jnp.where(far == 0, values[:, :width], values[:, width:])

    share = D // n_img
    r.down[...] = own(r.i_o_down, share)
    r.up[...] = own(r.i_o_up, share)
    both = own(r.i_o_qkv, share)
    r.qkv[...] = both[:, : 3 * D // n_band]
    r.out[...] = both[:, 3 * D // n_band :].T
    vec = r.i_o_vec[...]
    channels = r.i_o_wstat.shape[1]
    r.emb[...] = half(own(r.i_o_emb, channels // n_img))
    mine = lanes(vec, img * share, share)
    for at, name in enumerate(("embed_bias", "ln1_gain", "ln1_bias", "query_bias", "value_bias", "out_bias", "ln2_gain", "ln2_bias", "down_bias")):
        getattr(r, name)[...] = mine[at]
    share = channels // n_img
    r.gn_gain[...] = lanes(vec[8:], img * share, share)[5]
    r.gn_bias[...] = lanes(vec[8:], channels + img * share, share)[5]
    share = FF // n_img
    start = img * share
    line = jnp.sum(jnp.where(iota(vec.shape, 0) == 9 + lax.div(start, D), vec, 0.0), 0, keepdims=True)
    r.up_bias[...] = lanes(jnp.broadcast_to(line, (8, D)), lax.rem(start, D), share)[0]
    cols = channels // n_band
    taps = r.conv.shape[1]
    stats = jnp.concatenate([vec[13:14, 2 * channels :], vec[14:15, :channels], r.i_o_wstat[taps:][:6]], 0)
    stats = lanes(stats, band * cols, cols)
    stand = lanes(r.i_o_wstat[:taps], band * cols, cols)
    grad = half(own(r.i_o_conv, taps)) - stats[0:1] - stand * stats[1:2]
    r.conv[...] = (grad * stats[2:3]).T


def body(
    image,
    conv_weight,
    gn_gain,
    gn_bias,
    embed_weight,
    embed_bias,
    ln1_gain,
    ln1_bias,
    qkv_weight,
    query_bias,
    value_bias,
    out_weight,
    out_bias,
    ln2_gain,
    ln2_bias,
    up_weight,
    up_bias,
    down_weight,
    down_bias,
    text_embed,
    text_len,
    cotangent,
):
    n_img, n_band = lax.axis_size("img"), lax.axis_size("band")
    img, band = lax.axis_index("img"), lax.axis_index("band")
    images, rows = image.shape[:2]
    taps, channels = conv_weight.shape
    img_bits = [("img", k) for k in bits(n_img)]
    plans = {}
    for name, order in ORDERS.items():
        if name == "vec":
            continue
        order = route(order, n_img)
        k = int(name[3:] or 0)
        if name in DOWN + UP + QKV:
            out = {"d": "o_down", "u": "o_up", "q": "o_qkv"}[name[2]]
            plans[name] = (Plan(n_img, D, 256, FAR, order), out, (0, 256 * k))
        elif name == "p_e":
            plans[name] = (Plan(n_img, channels, D // 2, None, order), "o_emb", (0, 0))
        else:
            plan = Plan(n_img, taps, channels // 2, None, order, 3)
            plans[name] = (plan, "o_conv", (k * plan.rows, 0))
    vec_shape = (16, D)
    arguments = {
        "image": image.transpose(0, 2, 1, 3), "conv_weight": conv_weight, "gn_gain": gn_gain, "gn_bias": gn_bias, "embed_weight": embed_weight,
        "embed_bias": embed_bias, "ln1_gain": ln1_gain, "ln1_bias": ln1_bias, "qkv_weight": qkv_weight, "query_bias": query_bias,
        "value_bias": value_bias, "out_weight": out_weight, "out_bias": out_bias, "ln2_gain": ln2_gain, "ln2_bias": ln2_bias,
        "up_weight": up_weight, "up_bias": up_bias.reshape(1, FF), "down_weight": down_weight, "down_bias": down_bias,
        "text_embed": text_embed, "text_len": text_len, "cotangent": cotangent,
    }
    fetched = ("cotangent", "conv_weight", "embed_weight", "qkv_weight", "text_embed", "out_weight", "up_weight", "down_weight")
    spaces = {name: pl.ANY for name in fetched}
    spaces["text_len"] = pltpu.SMEM
    results = {
        "encoded": (cotangent.shape, HALF),
        "image_grad": (image.shape, FULL),
        "text_grad": (text_embed.shape, FULL),
        "o_down": ((plans["p_d0"][0].rows, D), FULL),
        "o_up": ((plans["p_u0"][0].rows, D), FULL),
        "o_qkv": ((plans["p_q0"][0].rows, D), FULL),
        "o_conv": ((3 * plans["p_c0"][0].rows, channels // 2), FULL),
        "o_emb": ((plans["p_e"][0].rows, D // 2), FULL),
        "o_vec": (vec_shape, FULL),
        "o_wstat": ((taps // n_img + 8, channels), FULL),
    }
    halo = (images, rows + 2, WIDE, channels)
    split = (images, TOK // images, D)
    scratch = {
        "v_" + name: (arguments[name].shape, HALF) for name in fetched
    }
    scratch.update({
        "pixels": (halo, HALF), "views": ((3,) + halo, HALF), "feat": ((TOK, channels), FULL),
        "tap_sum": ((TOK, 128), FULL), "sums": ((n_band, 2 * images, channels), FULL), "sums_back": ((n_band, 2 * images, channels), FULL),
        "zhat": ((TOK, channels), FULL), "active": ((TOK, channels), HALF), "slope": ((TOK, channels), FULL),
        "embedded": (split, HALF), "patches": (split, HALF), "stream": ((TOK, D), FULL), "nhat_one": ((TOK, D), FULL),
        "rstd_one": ((TOK, 1), FULL), "hidden": ((TOK, D), HALF), "qkv": ((TOK, 3 * D), HALF), "probs": ((HEADS, TOK, TOK), HALF),
        "mixed": ((TOK, D), HALF), "nhat_two": ((TOK, D), FULL), "rstd_two": ((TOK, 1), FULL),
        "hidden2": ((TOK, D), HALF), "cot": ((TOK, D), HALF), "final": ((TOK, D), FULL),
        "act": ((4, TOK, D), HALF), "d_pre": ((4, TOK, D), HALF), "up_sum": ((FF // D, 1, D), FULL), "vec": (vec_shape, FULL),
        "d_attn": ((TOK, D), HALF), "d_mixed": ((TOK, D), HALF), "d_qkv": ((TOK, 3 * D), HALF),
        "d_patches": (split, HALF), "d_cells": (split, HALF), "d_feat": ((TOK, channels), HALF), "d_rows": (halo, HALF),
        "d_views": ((3,) + halo, HALF), "mixed_bands": ((4, TOK, 256), HALF), "d_qkv_bands": ((4, TOK, D), HALF), "t_cot": ((D, 2 * TOK), HALF), "t_hidden": ((D, 2 * TOK), HALF), "t_hidden2": ((D, 2 * TOK), HALF), "t_attn": ((D, 2 * TOK), HALF), "slopes": ((4, TOK, D), HALF),
        "r_act": ((2, TOK, D), HALF), "r_d_pre": ((2, TOK, D), HALF),
        "r_d_qkv": ((2, TOK, D), HALF), "r_mixed": ((2, TOK, 256), HALF),
        "r_views": ((3,) + halo, HALF), "r_d_feat": ((TOK, channels), HALF), "r_active": ((TOK, channels), HALF), "r_d_cells": (split, HALF),
    })
    slots = 32
    for name, (plan, _, _) in plans.items():
        for k, shape in enumerate(plan.scratch()):
            scratch[f"{name}_{k}"] = (shape, HALF)
        slots += len(plan.order)
    n_links = 2 + len(img_bits)
    scratch["vec_sum"] = ((n_links,) + vec_shape, FULL)
    scratch["vec_in"] = ((n_links,) + vec_shape, FULL)
    slots += n_links
    sems = {"fetch_sem": 8, "send_sem": slots, "recv_sem": slots}
    names = list(arguments) + list(results) + list(scratch) + list(sems)
    whole = lambda space: pl.BlockSpec(memory_space=space)
    outs = pl.pallas_call(
        functools.partial(layer_kernel, names, plans),
        out_shape=[jax.ShapeDtypeStruct(*v) for v in results.values()],
        in_specs=[whole(spaces.get(name, pltpu.VMEM)) for name in arguments],
        out_specs=[whole(pltpu.VMEM)] * len(results),
        scratch_shapes=[pltpu.VMEM(*v) for v in scratch.values()] + [pltpu.SemaphoreType.DMA((n,)) for n in sems.values()],
        compiler_params=pltpu.CompilerParams(collective_id=0, has_side_effects=True, vmem_limit_bytes=63 * 2**20),
    )(*arguments.values())
    finished = {
        "encoded": (cotangent.shape, HALF),
        "image_grad": (arguments["image"].shape, FULL),
        "text_grad": (text_embed.shape, FULL),
        "conv": ((channels // n_band, taps // n_img), FULL),
        "gn_gain": ((channels // n_img,), FULL),
        "gn_bias": ((channels // n_img,), FULL),
        "emb": ((channels // n_img, D // n_band), FULL),
        "embed_bias": ((D // n_img,), FULL),
        "ln1_gain": ((D // n_img,), FULL),
        "ln1_bias": ((D // n_img,), FULL),
        "qkv": ((D // n_img, 3 * D // n_band), FULL),
        "query_bias": ((D // n_img,), FULL),
        "value_bias": ((D // n_img,), FULL),
        "out": ((D // n_band, D // n_img), FULL),
        "out_bias": ((D // n_img,), FULL),
        "ln2_gain": ((D // n_img,), FULL),
        "ln2_bias": ((D // n_img,), FULL),
        "up": ((D // n_img, FF // n_band), FULL),
        "up_bias": ((FF // n_img,), FULL),
        "down": ((D // n_img, FF // n_band), FULL),
        "down_bias": ((D // n_img,), FULL),
    }
    names = ["i_" + name for name in results] + list(finished)
    outs = pl.pallas_call(
        functools.partial(finish_kernel, names),
        out_shape=[jax.ShapeDtypeStruct(*v) for v in finished.values()],
        in_specs=[whole(pltpu.VMEM)] * len(results),
        out_specs=[whole(pltpu.VMEM)] * len(finished),
    )(*outs)
    res = dict(zip(finished, outs))
    res["conv"], res["down"] = res["conv"].T, res["down"].T
    res["image_grad"] = res["image_grad"].transpose(0, 2, 1, 3)
    return tuple(res.values())


def solution(mesh):
    in_specs = (
        P("img", "band", None, None),
        P(),
        P(),
        P(),
        P(),
        P(),
        P(),
        P(),
        P(),
        P(),
        P(),
        P(),
        P(),
        P(),
        P(),
        P(),
        P(),
        P(),
        P(),
        P(("img", "band"), None, None),
        P(("img", "band")),
        P(("img", "band"), None, None),
    )
    out_specs = (
        P(("img", "band"), None, None),
        P("img", "band", None, None),
        P(("img", "band"), None, None),
        P("img", "band"),
        P("img"),
        P("img"),
        P("img", "band"),
        P("img"),
        P("img"),
        P("img"),
        P("img", "band"),
        P("img"),
        P("img"),
        P("band", "img"),
        P("img"),
        P("img"),
        P("img"),
        P("img", "band"),
        P("img"),
        P("band", "img"),
        P("img"),
    )
    return jax.shard_map(body, mesh=mesh, in_specs=in_specs, out_specs=out_specs, check_vma=False)
```

```python
import functools
import types

import jax
import jax.numpy as jnp
from jax import lax
from jax.experimental import pallas as pl
from jax.experimental.pallas import tpu as pltpu
from jax.sharding import PartitionSpec as P

D = 768
FF = 3072
HEADS = 12
GROUPS = 32
GRID = 14
TEXT = 32
PATCHES = 196
WIDE = 16
TOK = 256
CELLS = GRID * WIDE
HALF = jnp.bfloat16
FULL = jnp.float32
MESH_ID = pl.DeviceIdType.MESH
CORE = ("band", 1)
FAR = ("band", 2)


def bit_of(value, bit):
    return lax.rem(lax.div(value, bit), 2)


def flip(value, bit):
    return value + bit * (1 - 2 * bit_of(value, bit))


def partner(label):
    axis, bit = label
    img, band = lax.axis_index("img"), lax.axis_index("band")
    return (flip(img, bit), band) if axis == "img" else (img, flip(band, bit))


def my_bit(label):
    axis, bit = label
    return bit_of(lax.axis_index(axis), bit)


def bits(count):
    return [1 << k for k in range(count.bit_length() - 1)]


def route(letters, n_img):
    near = [("img", k) for k in bits(n_img)]
    routes = {"c": [CORE], "y": [FAR], "Y": [FAR], "x": near[:1], "z": near[1:2], "w": near[2:]}
    return sum((routes[letter] for letter in letters), [])


class Plan:
    def __init__(self, n_img, rows, width, lead, order, parts=1):
        self.width = width
        split = [("img", k) for k in reversed(bits(n_img)) if (rows // n_img) * k % 16 == 0]
        self.rows = (rows >> len(split)) // parts
        self.first = ([lead] if lead else []) + split
        rest = [("img", k) for k in bits(n_img) if ("img", k) not in split]
        self.order = [lab for lab in order if lab not in rest] + rest
        self.shapes = []
        labels = list(self.first)
        for lab in self.order:
            if lab in labels:
                labels.remove(lab)
            self.shapes.append((2,) * len(labels) + (self.rows, width))
        self.shape = (2,) * len(self.first) + (self.rows, width)

    def scratch(self):
        return [self.shape] + self.shapes


class Once:
    def __init__(self, copy):
        self.copy, self.left = copy, {"wait", "wait_send", "wait_recv"}
        copy.start()

    def _wait(self, kind):
        if kind in self.left:
            self.left.remove(kind)
            getattr(self.copy, kind)()

    def wait(self):
        self._wait("wait")

    def wait_send(self):
        self._wait("wait_send")

    def wait_recv(self):
        self._wait("wait_recv")


class Piece:
    def __init__(self, plan, refs, sems, slot, out, at, pending):
        self.pending = pending
        self.plan, self.buf, self.recv = plan, refs[0], refs[1:]
        self.sems, self.slot = sems, slot
        self.labels, self.cur = list(plan.first), refs[0]
        self.sent = []
        self.out = out.at[pl.ds(at[0], plan.rows), pl.ds(at[1], plan.width)]
        self.stage = 0

    def _index(self, label, which):
        at = self.labels.index(label)
        return (slice(None),) * at + (which,)

    def start(self):
        label = self.plan.order[self.stage]
        src = self.cur
        if label in self.labels:
            src = src.at[self._index(label, 1 - my_bit(label))]
        send, recv = self.sems
        copy = pltpu.make_async_remote_copy(
            src_ref=src,
            dst_ref=self.recv[self.stage],
            send_sem=send.at[self.slot + self.stage],
            recv_sem=recv.at[self.slot + self.stage],
            device_id=partner(label),
            device_id_type=MESH_ID,
        )
        self.sent.append(Once(copy))
        self.pending.append(self.sent[-1])

    def step(self):
        label = self.plan.order[self.stage]
        self.sent[self.stage].wait_recv()
        mine = self.cur
        if label in self.labels:
            mine = mine[self._index(label, my_bit(label))]
            self.labels.remove(label)
        else:
            mine = mine[...]
        got = self.recv[self.stage]
        self.stage += 1
        if self.stage == len(self.plan.order):
            self.out[...] = (got[...].astype(FULL) + mine.astype(FULL)).reshape(self.out.shape)
        else:
            got[...] = got[...] + mine
            self.cur = got
            self.start()


def dot(left, right):
    return jnp.dot(left, right, preferred_element_type=FULL)


def dot_tn(left, right):
    return lax.dot_general(left, right, (((0,), (0,)), ((), ())), preferred_element_type=FULL)


def dot_nt(left, right):
    return lax.dot_general(left, right, (((1,), (1,)), ((), ())), preferred_element_type=FULL)


def exact_dot(left, right):
    return jnp.dot(left, right, precision=lax.Precision.HIGHEST, preferred_element_type=FULL)


def gelu_parts(x):
    cdf = 0.5 + 0.5 * lax.erf(x * 0.7071067811865476)
    pdf = jnp.exp(-0.5 * x * x) * 0.3989422804014327
    return x * cdf, cdf + x * pdf


def iota(shape, axis):
    return lax.broadcasted_iota(jnp.int32, shape, axis)


def row(ref):
    return ref[...].reshape(1, -1)


def column_sum(values):
    return jnp.sum(values, 0, keepdims=True)


def shifted(values):
    edge = jnp.zeros(values.shape[:2] + (1, values.shape[3]), FULL)
    left = jnp.concatenate([edge, values[:, :, : WIDE - 1]], 2)
    right = jnp.concatenate([values[:, :, 1:], edge], 2)
    return left, values, right


DOWN, UP, QKV = (tuple(f"p_{unit}{k}" for k in range(3)) for unit in "duq")
ORDERS = {
    "p_d0": "xzwy",
    "p_d1": "yzxw",
    "p_d2": "zxyw",
    "p_u0": "yxzw",
    "p_u1": "xyzw",
    "p_u2": "wyxz",
    "p_q0": "yxzw",
    "p_q1": "xzyw",
    "p_q2": "yxzw",
    "p_c0": "xzYw",
    "p_c1": "xwzY",
    "p_c2": "xzwY",
    "p_e": "zxwY",
    "vec": "zwycx",
}
POLLS = {
    "back1": (
        "p_d0",
        "p_d1",
        "p_d2",
    ),
    "cells": (
        "qkv",
        "+p_q1",
        "p_u1",
        "p_u0",
    ),
    "sums": (
        "p_d2",
        "p_d0",
    ),
    "edges": (
        "+p_q2",
        "+p_q0",
        "p_u1",
        "p_u2",
        "p_d1",
        "p_d2",
    ),
    "grad": (
        "p_q1",
        "vec",
        "p_d0",
    ),
    "end": (
        "p_u1",
        "p_u0",
        "p_d2",
        "p_d1",
        "p_q2",
        "p_q1",
        "p_c0",
        "vec",
        "p_c1",
        "p_e",
        "p_c2",
        "p_u1",
        "p_u0",
        "p_q0",
        "p_c0",
        "p_d1",
        "p_q2",
        "p_e",
        "p_c2",
        "p_c1",
        "p_u2",
        "p_u0",
        "p_d0",
        "p_q2",
        "p_q0",
        "p_e",
        "p_q1",
        "p_c2",
        "p_c1",
        "p_u2",
        "vec",
        "p_c0",
        "p_q2",
        "p_e",
        "vec",
        "p_c2",
        "p_q0",
        "p_c1",
        "p_u2",
        "p_q1",
        "vec",
        "p_c0",
        "p_q0",
    ),
}


def layer_kernel(names, plans, *refs):
    r = types.SimpleNamespace(**dict(zip(names, refs)))
    img, band = lax.axis_index("img"), lax.axis_index("band")
    n_img, n_band = lax.axis_size("img"), lax.axis_size("band")
    images, _, rows = r.image.shape[:3]
    channels = r.conv_weight.shape[1]
    core = my_bit(CORE)
    others = [lax.rem(band + d, n_band) for d in range(n_band)]

    fetches = {}

    def fetch(name, at):
        copy = pltpu.make_async_copy(getattr(r, name), getattr(r, "v_" + name), r.fetch_sem.at[at])
        fetches[name] = Once(copy)

    for at, name in enumerate(("cotangent", "conv_weight", "embed_weight", "qkv_weight", "text_embed", "out_weight", "up_weight", "down_weight")):
        fetch(name, at)

    links = [CORE, FAR] + [("img", k) for k in bits(n_img)]
    barrier = pltpu.get_barrier_semaphore()
    for d in range(1, n_band):
        pl.semaphore_signal(barrier, inc=1, device_id=(img, others[d]), device_id_type=MESH_ID)
    for label in links[2:]:
        pl.semaphore_signal(barrier, inc=1, device_id=partner(label), device_id_type=MESH_ID)

    pending = []

    def send(src, dst, at, device):
        copy = pltpu.make_async_remote_copy(
            src_ref=src, dst_ref=dst, send_sem=r.send_sem.at[at], recv_sem=r.recv_sem.at[at],
            device_id=device, device_id_type=MESH_ID)
        pending.append(Once(copy))
        return pending[-1]

    def edge_rows(ref, at):
        up = send(ref.at[:, rows], ref.at[:, 0], at, (img, others[1]))
        down = send(ref.at[:, 1], ref.at[:, rows + 1], at + 1, (img, others[n_band - 1]))
        return up, down

    def edges_in(ref, copies):
        for copy in copies:
            copy.wait_recv()
        values = ref[...].astype(FULL)
        at = iota(values.shape, 1) + band * rows
        return jnp.where((at == 0) | (at > n_band * rows), 0.0, values)

    def exchange(values, slots, at, meanwhile=None):
        slots[0] = values
        copies = [send(slots.at[0], slots.at[d], at + d - 1, (img, others[d])) for d in range(1, n_band)]
        poll(meanwhile)
        for d, copy in enumerate(copies, 1):
            copy.wait_recv()
            values = values + slots[d]
        return values

    def to_owners(src, dst, at, meanwhile=None):
        copies = [send(src.at[others[d]], dst.at[band], at + d - 1, (img, others[d])) for d in range(1, n_band)]
        dst[band] = src[band]
        poll(meanwhile)
        for copy in copies:
            copy.wait_recv()

    swaps = {}
    base = 16

    def swap(name, at, src, dst):
        swaps.setdefault(name, []).append(send(src, dst, base + at, partner(CORE)))

    def swap_bands(name, at, src, dst):
        for y in range(2):
            swap(name, at + y, src.at[2 * y + 1 - core], dst.at[y])

    def swap_left(name, at, ref):
        swap(name, at, ref.at[:, pl.ds(0, TOK)], ref.at[:, pl.ds(TOK, TOK)])

    def arrived(name):
        for copy in swaps[name]:
            copy.wait_recv()

    pieces = {}
    slot = base + 16
    for name, (plan, out, at) in plans.items():
        refs = [getattr(r, f"{name}_{k}") for k in range(1 + len(plan.order))]
        pieces[name] = Piece(plan, refs, (r.send_sem, r.recv_sem), slot, getattr(r, out), at, pending)
        slot += len(plan.order)

    down, up, qkv = DOWN, UP, QKV

    def poll(point):
        for name in POLLS.get(point, ()):
            if name[0] == "+":
                pieces[name[1:]].start()
            elif name == "vec":
                vec_step()
            elif name == "qkv":
                qkv_unit()
            else:
                advance(name)

    def advance(*names):
        for name in names:
            if pieces[name].stage < len(pieces[name].plan.order):
                pieces[name].step()

    def unit(parts, terms, start=True):
        for j, name in enumerate(parts):
            piece = pieces[name]
            wide = slice(256 * j, 256 * (j + 1))
            for y in range(2):
                value = 0.0
                for left, right, got, at in terms:
                    if j >= at:
                        cut = slice(256 * (j - at), 256 * (j - at + 1))
                        both = jnp.concatenate([right[2 * y + core, :, cut], got[y, :, cut]], 0)
                        value = value + dot(left[...], both)
                piece.buf[y] = value.astype(HALF).reshape(piece.plan.shape[1:])
            if start:
                piece.start()

    r.pixels[:, 1 : rows + 1, GRID:, :] = jnp.zeros((images, rows, WIDE - GRID, channels), HALF)
    for k in range(rows):
        line = r.image[:, :, k, :].astype(FULL)
        r.pixels[:, k + 1, :GRID, :] = jnp.where(band * rows + k < GRID, line, 0.0).astype(HALF)
    fetches["cotangent"].wait()
    seq = r.cotangent.shape[1]

    def token_of(at):
        return jnp.where(at < CELLS, jnp.where(lax.rem(at, WIDE) < GRID, lax.div(at, WIDE) * GRID + lax.rem(at, WIDE), -1), at - CELLS + PATCHES)

    spread = jnp.where(token_of(iota((TOK, seq), 0)) == iota((TOK, seq), 1), 1.0, 0.0).astype(HALF)
    gather = jnp.where(token_of(iota((seq, TOK), 1)) == iota((seq, TOK), 0), 1.0, 0.0).astype(HALF)
    r.cot[...] = dot(spread, r.v_cotangent[0]).astype(HALF)

    r.t_cot[:, :TOK] = r.cot[...].T
    pl.semaphore_wait(barrier, n_band - 1 + len(links) - 2)
    copies = edge_rows(r.pixels, 0)

    swap_left("down", 0, r.t_cot)

    fetches["conv_weight"].wait()
    taps = r.conv_weight.shape[0]
    chunks = [slice(k, k + 256) for k in range(0, taps, 256)]
    wmean = sum(column_sum(r.v_conv_weight[s].astype(FULL)) for s in chunks) * (1.0 / taps)
    wvar = 0.0
    for s in chunks:
        cent = r.v_conv_weight[s].astype(FULL) - wmean
        wvar = wvar + column_sum(cent * cent)
    wscale = lax.rsqrt(wvar * (1.0 / taps) + 1e-05)
    taps_here = taps // n_img
    if taps_here % 16 == 0:
        own = r.v_conv_weight[pl.ds(pl.multiple_of(img * taps_here, 16), taps_here)]
    else:
        own = jnp.where(iota((taps_here, taps), 1) == iota((taps_here, taps), 0) + img * taps_here, 1.0, 0.0).astype(HALF)
        own = dot(own, r.v_conv_weight[...]).astype(HALF)
    own = ((own.astype(FULL) - wmean) * wscale, jnp.broadcast_to(wscale, (8, channels)))
    r.o_wstat[...] = jnp.concatenate(own, 0)
    for s in chunks:
        r.v_conv_weight[s] = ((r.v_conv_weight[s].astype(FULL) - wmean) * wscale).astype(HALF)
    pixels = edges_in(r.pixels, copies)
    for e, values in enumerate(shifted(pixels)):
        r.views[e] = values.astype(HALF)

    def window(views, a, e):
        return views[e, :, a : a + rows].reshape(TOK, channels)

    place = iota((TOK, channels), 0)
    live = (lax.rem(place, WIDE) < GRID) & (lax.rem(lax.div(place, WIDE), rows) + band * rows < GRID)
    feat = 0.0
    tap_sum = 0.0
    for a in range(3):
        for e in range(3):
            seen = window(r.views, a, e)
            feat = feat + dot(seen, r.v_conv_weight[(3 * a + e) * channels : (3 * a + e + 1) * channels])
            tap_sum = tap_sum + seen.astype(FULL)
    feat = jnp.where(live, feat, 0.0)
    r.feat[...] = feat
    r.tap_sum[...] = jnp.broadcast_to(jnp.sum(tap_sum, 1, keepdims=True), (TOK, 128))
    per_group = channels // GROUPS
    entries = 1.0 / (GRID * GRID * per_group)
    same = lax.div(iota((channels, channels), 0), per_group) == lax.div(iota((channels, channels), 1), per_group)
    same = jnp.where(same, 1.0, 0.0)
    cells = TOK // images

    def image_sums(one, two):
        one = jnp.sum(one.reshape(images, cells, channels), 1)
        two = jnp.sum(two.reshape(images, cells, channels), 1)
        return exact_dot(jnp.concatenate([one, two], 0), same)

    def per_image(sums, which):
        return sums[which * images : (which + 1) * images].reshape(images, 1, channels)
    sums = exchange(image_sums(feat, feat * feat), r.sums, 2) * entries
    gmean = per_image(sums, 0)
    gscale = lax.rsqrt(per_image(sums, 1) - gmean * gmean + 1e-05)
    zhat = ((feat.reshape(images, cells, channels) - gmean) * gscale).reshape(TOK, channels)
    r.zhat[...] = zhat
    stem, slope = gelu_parts(zhat * row(r.gn_gain) + row(r.gn_bias))
    r.active[...] = jnp.where(live, stem, 0.0).astype(HALF)
    r.slope[...] = jnp.where(live, slope, 0.0)
    fetches["embed_weight"].wait()
    embedded = dot(r.active[...], r.v_embed_weight[...]) + row(r.embed_bias)
    r.embedded[...] = embedded.astype(HALF).reshape(images, cells, D)
    to_owners(r.embedded, r.patches, 5)
    swap("conv", 12, r.views, r.r_views)
    swap("emb", 14, r.active, r.r_active)
    def norm(values):
        mean = jnp.mean(values, -1, keepdims=True)
        cent = values - mean
        rstd = lax.rsqrt(jnp.mean(cent * cent, -1, keepdims=True) + 1e-06)
        return cent * rstd, rstd

    def norm_back(grad, nhat, rstd, gain):
        s = grad * gain
        inner = s - jnp.mean(s, -1, keepdims=True) - nhat * jnp.mean(s * nhat, -1, keepdims=True)
        return inner * rstd

    fetches["text_embed"].wait()
    r.stream[...] = r.patches[...].reshape(TOK, D).astype(FULL)
    r.stream[CELLS:] = r.v_text_embed[0].astype(FULL)
    nhat, rstd_one = norm(r.stream[...])
    r.nhat_one[...] = nhat
    r.rstd_one[...] = rstd_one
    r.hidden[...] = (nhat * row(r.ln1_gain) + row(r.ln1_bias)).astype(HALF)
    r.t_hidden[:, :TOK] = r.hidden[...].T
    swap_left("qkv", 6, r.t_hidden)
    fetches["qkv_weight"].wait()
    for k, bias in enumerate((r.query_bias, None, r.value_bias)):
        values = dot(r.hidden[...], r.v_qkv_weight[:, k * D : (k + 1) * D])
        if bias is not None:
            values = values + row(bias)
        values = values.astype(HALF)
        r.qkv[:, k * D : (k + 1) * D] = values * 0.125 if k == 0 else values
    key_at = iota((1, TOK), 1)
    key_live = ((key_at < CELLS) & (lax.rem(key_at, WIDE) < GRID)) | ((key_at >= CELLS) & (key_at - CELLS < r.text_len[0]))
    first = iota((TOK, 128), 1) < 64
    zero = jnp.zeros((TOK, 128), HALF)

    def pair_of(ref, k, p):
        return ref[:, k * D + p * 128 : k * D + (p + 1) * 128]

    def only(values, h):
        return jnp.where(first, values, zero) if h == 0 else jnp.where(first, zero, values)

    def attend(p):
        query, key, value = (pair_of(r.qkv, k, p) for k in range(3))
        sides = []
        for h in range(2):
            scores = jnp.where(key_live, dot_nt(only(query, h), key), -1000000000.0)
            expd = jnp.exp(scores - jnp.max(scores, -1, keepdims=True))
            probs = expd * (1.0 / jnp.sum(expd, -1, keepdims=True))
            probs = probs.astype(HALF)
            r.probs[2 * p + h] = probs
            sides.append(dot(probs, value))
        r.mixed[:, p * 128 : (p + 1) * 128] = jnp.where(first, *sides).astype(HALF)

    for p in range(HEADS // 2):
        attend(p)
    for k in range(4):
        width = D // 4
        r.mixed_bands[k] = jnp.concatenate([jnp.zeros((TOK, 256 - width), HALF), r.mixed[:, k * width : (k + 1) * width]], 1)
    swap_bands("out", 10, r.mixed_bands, r.r_mixed)
    fetches["out_weight"].wait()
    mid = r.stream[...] + dot(r.mixed[...], r.v_out_weight[...]) + row(r.out_bias)
    r.final[...] = mid + row(r.down_bias)
    nhat, rstd_two = norm(mid)
    r.nhat_two[...] = nhat
    r.rstd_two[...] = rstd_two
    r.hidden2[...] = (nhat * row(r.ln2_gain) + row(r.ln2_bias)).astype(HALF)
    fetches["up_weight"].wait()
    r.t_hidden2[:, :TOK] = r.hidden2[...].T
    swap_left("up", 3, r.t_hidden2)

    for k in range(FF // D):
        wide = slice(k * D, (k + 1) * D)
        act, slope = gelu_parts(dot(r.hidden2[...], r.v_up_weight[:, wide]) + r.up_bias[:, wide])
        r.act[k] = act.astype(HALF)
        r.slopes[k] = slope.astype(HALF)
    swap_bands("down", 1, r.act, r.r_act)
    fetches["down_weight"].wait()
    final = r.final[...]
    for k in range(FF // D):
        final = final + dot(r.act[k], r.v_down_weight[k * D : (k + 1) * D])
    arrived("down")
    unit(down, [(r.t_cot, r.act, r.r_act, 0)])
    r.encoded[0] = dot(gather, final.astype(HALF)).astype(HALF)

    for k in range(FF // D):
        wide = slice(k * D, (k + 1) * D)
        d_pre = dot_nt(r.cot[...], r.v_down_weight[wide, :]) * r.slopes[k].astype(FULL)
        r.d_pre[k] = d_pre.astype(HALF)
        r.up_sum[k] = column_sum(r.d_pre[k].astype(FULL))
    swap_bands("up", 4, r.d_pre, r.r_d_pre)
    grad = 0.0
    for k in range(FF // D):
        grad = grad + dot_nt(r.d_pre[k], r.v_up_weight[:, k * D : (k + 1) * D])
    r.final[...] = grad
    def put(at, values, lo=0):
        r.vec[at : at + 1, lo : lo + values.shape[1]] = values

    r.vec[...] = jnp.zeros(r.vec.shape, FULL)
    cot = r.cot[...].astype(FULL)
    put(8, column_sum(cot))
    for k in range(FF // D):
        put(9 + k, r.up_sum[k])

    grad = r.final[...]
    put(6, column_sum(grad * r.nhat_two[...]))
    put(7, column_sum(grad))
    d_mid = cot + norm_back(grad, r.nhat_two[...], r.rstd_two[...], row(r.ln2_gain))
    r.stream[...] = d_mid
    r.d_attn[...] = d_mid.astype(HALF)
    r.t_attn[:, :TOK] = r.d_attn[...].T
    swap_left("out", 9, r.t_attn)
    put(5, column_sum(r.d_attn[...].astype(FULL)))
    r.d_mixed[...] = dot_nt(r.d_attn[...], r.v_out_weight[...]).astype(HALF)

    arrived("up")
    unit(up, [(r.t_hidden2, r.d_pre, r.r_d_pre, 0)])
    def attend_back(p):
        query, key, value = (pair_of(r.qkv, k, p) for k in range(3))
        d_mixed = pair_of(r.d_mixed, 0, p)
        sides = [[], [], []]
        for h in range(2):
            probs = r.probs[2 * p + h]
            d_probs = dot_nt(only(d_mixed, h), value)
            weight = probs.astype(FULL)
            delta = jnp.sum(d_probs * weight, -1, keepdims=True)
            d_scores = (weight * (d_probs - delta)).astype(HALF)
            sides[0].append(dot(d_scores, key) * 0.125)
            sides[1].append(dot_tn(d_scores, query))
            sides[2].append(dot_tn(probs, d_mixed))
        for k in range(3):
            r.d_qkv[:, k * D + p * 128 : k * D + (p + 1) * 128] = jnp.where(first, *sides[k]).astype(HALF)

    for p in range(HEADS // 2):
        attend_back(p)
        poll(f"back{p}")
    for k in range(4):
        width = 3 * D // 4
        r.d_qkv_bands[k] = jnp.concatenate([r.d_qkv[:, k * width : (k + 1) * width], jnp.zeros((TOK, D - width), HALF)], 1)
    swap_bands("qkv", 7, r.d_qkv_bands, r.r_d_qkv)
    put(3, column_sum(r.d_qkv[:, :D].astype(FULL)))
    put(4, column_sum(r.d_qkv[:, 2 * D :].astype(FULL)))
    grad = dot_nt(r.d_qkv[...], r.v_qkv_weight[...])
    put(1, column_sum(grad * r.nhat_one[...]))
    put(2, column_sum(grad))
    d_stream = r.stream[...] + norm_back(grad, r.nhat_one[...], r.rstd_one[...], row(r.ln1_gain))
    r.text_grad[0] = d_stream[CELLS:]
    at_cell = iota((TOK, D), 0) < CELLS
    r.d_patches[...] = jnp.where(at_cell, d_stream, 0.0).astype(HALF).reshape(r.d_patches.shape)
    def qkv_unit():
        arrived("qkv")
        arrived("out")
        unit(qkv, [(r.t_hidden, r.d_qkv_bands, r.r_d_qkv, 0), (r.t_attn, r.mixed_bands, r.r_mixed, 2)], False)
    to_owners(r.d_patches, r.d_cells, 8, "cells")
    swap("emb", 15, r.d_cells, r.r_d_cells)
    d_cells = r.d_cells[...].reshape(TOK, D)
    put(0, column_sum(d_cells.astype(FULL)))
    d_active = dot_nt(d_cells, r.v_embed_weight[...]).astype(HALF).astype(FULL)
    d_norm = d_active * r.slope[...]
    zhat = r.zhat[...]
    put(13, column_sum(d_norm * zhat))
    put(13, column_sum(d_norm), channels)
    d_hat = d_norm * row(r.gn_gain)
    back = exchange(image_sums(d_hat, d_hat * zhat), r.sums_back, 11, "sums") * entries
    d_feat = d_hat.reshape(images, cells, channels) - per_image(back, 0)
    d_feat = (d_feat - zhat.reshape(images, cells, channels) * per_image(back, 1)) * gscale
    d_feat = jnp.where(live, d_feat.reshape(TOK, channels), 0.0).astype(HALF)
    r.d_feat[...] = d_feat
    r.d_rows[:, 1 : rows + 1] = d_feat.reshape(images, rows, WIDE, channels)
    copies = edge_rows(r.d_rows, 14)
    swap("conv", 13, r.d_feat, r.r_d_feat)
    d_feat = d_feat.astype(FULL)
    put(13, column_sum(r.tap_sum[:, :1] * d_feat) * (1.0 / taps), 2 * channels)
    put(14, column_sum(r.feat[...] * d_feat) * (1.0 / taps))

    vec_links = route(ORDERS["vec"], n_img)

    def vec_start(stage):
        return send(r.vec if stage == 0 else r.vec_sum.at[stage - 1], r.vec_in.at[stage], slot + stage, partner(vec_links[stage]))

    vec_state = [r.vec[...], 0, vec_start(0)]

    def vec_step():
        total, stage, on_way = vec_state
        on_way.wait_recv()
        total = total + r.vec_in[stage]
        if stage == len(links) - 1:
            r.o_vec[...] = total
        else:
            r.vec_sum[stage] = total
            on_way = vec_start(stage + 1)
        vec_state[:] = [total, stage + 1, on_way]

    poll("edges")
    for e, values in enumerate(shifted(edges_in(r.d_rows, copies))):
        r.d_views[e] = values.astype(HALF)
    grad = 0.0
    for a in range(3):
        for e in range(3):
            seen = window(r.d_views, 2 - a, 2 - e)
            grad = grad + dot_nt(seen, r.v_conv_weight[(3 * a + e) * channels : (3 * a + e + 1) * channels])
    grad = jnp.where(live, grad, 0.0).reshape(images, rows, WIDE, channels)
    r.image_grad[...] = grad[:, :, :GRID]

    poll("grad")

    def columns(values, width):
        total = values.shape[1]
        col = iota((total, 2 * width), 1)
        want = jnp.where(col < width, col, col + width) + core * width
        pick = jnp.where(iota((total, 2 * width), 0) == want, 1.0, 0.0).astype(HALF)
        return dot(values, pick).astype(HALF)

    arrived("conv")
    mine, theirs = columns(r.d_feat[...], channels // 4), columns(r.r_d_feat[...], channels // 4)
    rows_here = pieces["p_c0"].plan.rows
    for a in range(3):
        for e in range(3):
            value = dot_tn(window(r.views, a, e), mine) + dot_tn(window(r.r_views, a, e), theirs)
            value = value.astype(HALF)
            begin = at = (3 * a + e) * channels
            while at < begin + channels:
                line, lo = divmod(at, rows_here)
                block, part = divmod(line, 3)
                size = min(begin + channels - at, rows_here - lo)
                piece = pieces[f"p_c{part}"]
                where = tuple(block >> k & 1 for k in reversed(range(len(piece.plan.first))))
                piece.buf[where + (slice(lo, lo + size),)] = value[at - begin : at - begin + size]
                at += size
    for part in range(3):
        pieces[f"p_c{part}"].start()
    arrived("emb")
    mine, theirs = columns(d_cells, D // 4), columns(r.r_d_cells[...].reshape(TOK, D), D // 4)
    piece = pieces["p_e"]
    value = dot_tn(r.active[...], mine) + dot_tn(r.r_active[...], theirs)
    piece.buf[...] = value.astype(HALF).reshape(piece.plan.shape)
    piece.start()
    poll("end")
    while vec_state[1] < len(links) or any(p.stage < len(p.plan.order) for p in pieces.values()):
        advance(*pieces)
        if vec_state[1] < len(links):
            vec_step()
    for copy in pending:
        copy.wait_send()


def finish_kernel(names, *refs):
    r = types.SimpleNamespace(**dict(zip(names, refs)))
    img, band = lax.axis_index("img"), lax.axis_index("band")
    n_img, n_band = lax.axis_size("img"), lax.axis_size("band")
    far = my_bit(FAR)
    r.encoded[...] = r.i_encoded[...]
    r.text_grad[...] = r.i_text_grad[...]
    for k in range(r.image_grad.shape[2]):
        r.image_grad[:, :, k, :] = r.i_image_grad[:, k]

    def own(ref, rows):
        if ref.shape[0] == rows:
            return ref[...]
        at = lax.rem(img, ref.shape[0] // rows) * rows
        pick = jnp.where(iota((rows, ref.shape[0]), 1) == iota((rows, ref.shape[0]), 0) + at, 1.0, 0.0)
        return exact_dot(pick, ref[...])

    def lanes(values, at, count):
        width = values.shape[1]
        return exact_dot(values, jnp.where(iota((width, count), 0) == iota((width, count), 1) + at, 1.0, 0.0))

    def half(values):
        width = values.shape[1] // 2
        return jnp.where(far == 0, values[:, :width], values[:, width:])

    share = D // n_img
    r.down[...] = own(r.i_o_down, share)
    r.up[...] = own(r.i_o_up, share)
    both = own(r.i_o_qkv, share)
    r.qkv[...] = both[:, : 3 * D // n_band]
    r.out[...] = both[:, 3 * D // n_band :].T
    vec = r.i_o_vec[...]
    channels = r.i_o_wstat.shape[1]
    r.emb[...] = half(own(r.i_o_emb, channels // n_img))
    mine = lanes(vec, img * share, share)
    for at, name in enumerate(("embed_bias", "ln1_gain", "ln1_bias", "query_bias", "value_bias", "out_bias", "ln2_gain", "ln2_bias", "down_bias")):
        getattr(r, name)[...] = mine[at]
    share = channels // n_img
    r.gn_gain[...] = lanes(vec[8:], img * share, share)[5]
    r.gn_bias[...] = lanes(vec[8:], channels + img * share, share)[5]
    share = FF // n_img
    start = img * share
    line = jnp.sum(jnp.where(iota(vec.shape, 0) == 9 + lax.div(start, D), vec, 0.0), 0, keepdims=True)
    r.up_bias[...] = lanes(jnp.broadcast_to(line, (8, D)), lax.rem(start, D), share)[0]
    cols = channels // n_band
    taps = r.conv.shape[1]
    stats = jnp.concatenate([vec[13:14, 2 * channels :], vec[14:15, :channels], r.i_o_wstat[taps:][:6]], 0)
    stats = lanes(stats, band * cols, cols)
    stand = lanes(r.i_o_wstat[:taps], band * cols, cols)
    grad = half(own(r.i_o_conv, taps)) - stats[0:1] - stand * stats[1:2]
    r.conv[...] = (grad * stats[2:3]).T


def body(
    image,
    conv_weight,
    gn_gain,
    gn_bias,
    embed_weight,
    embed_bias,
    ln1_gain,
    ln1_bias,
    qkv_weight,
    query_bias,
    value_bias,
    out_weight,
    out_bias,
    ln2_gain,
    ln2_bias,
    up_weight,
    up_bias,
    down_weight,
    down_bias,
    text_embed,
    text_len,
    cotangent,
):
    n_img, n_band = lax.axis_size("img"), lax.axis_size("band")
    img, band = lax.axis_index("img"), lax.axis_index("band")
    images, rows = image.shape[:2]
    taps, channels = conv_weight.shape
    img_bits = [("img", k) for k in bits(n_img)]
    plans = {}
    for name, order in ORDERS.items():
        if name == "vec":
            continue
        order = route(order, n_img)
        k = int(name[3:] or 0)
        if name in DOWN + UP + QKV:
            out = {"d": "o_down", "u": "o_up", "q": "o_qkv"}[name[2]]
            plans[name] = (Plan(n_img, D, 256, FAR, order), out, (0, 256 * k))
        elif name == "p_e":
            plans[name] = (Plan(n_img, channels, D // 2, None, order), "o_emb", (0, 0))
        else:
            plan = Plan(n_img, taps, channels // 2, None, order, 3)
            plans[name] = (plan, "o_conv", (k * plan.rows, 0))
    vec_shape = (16, D)
    arguments = {
        "image": image.transpose(0, 2, 1, 3), "conv_weight": conv_weight, "gn_gain": gn_gain, "gn_bias": gn_bias, "embed_weight": embed_weight,
        "embed_bias": embed_bias, "ln1_gain": ln1_gain, "ln1_bias": ln1_bias, "qkv_weight": qkv_weight, "query_bias": query_bias,
        "value_bias": value_bias, "out_weight": out_weight, "out_bias": out_bias, "ln2_gain": ln2_gain, "ln2_bias": ln2_bias,
        "up_weight": up_weight, "up_bias": up_bias.reshape(1, FF), "down_weight": down_weight, "down_bias": down_bias,
        "text_embed": text_embed, "text_len": text_len, "cotangent": cotangent,
    }
    fetched = ("cotangent", "conv_weight", "embed_weight", "qkv_weight", "text_embed", "out_weight", "up_weight", "down_weight")
    spaces = {name: pl.ANY for name in fetched}
    spaces["text_len"] = pltpu.SMEM
    results = {
        "encoded": (cotangent.shape, HALF),
        "image_grad": (image.shape, FULL),
        "text_grad": (text_embed.shape, FULL),
        "o_down": ((plans["p_d0"][0].rows, D), FULL),
        "o_up": ((plans["p_u0"][0].rows, D), FULL),
        "o_qkv": ((plans["p_q0"][0].rows, D), FULL),
        "o_conv": ((3 * plans["p_c0"][0].rows, channels // 2), FULL),
        "o_emb": ((plans["p_e"][0].rows, D // 2), FULL),
        "o_vec": (vec_shape, FULL),
        "o_wstat": ((taps // n_img + 8, channels), FULL),
    }
    halo = (images, rows + 2, WIDE, channels)
    split = (images, TOK // images, D)
    scratch = {
        "v_" + name: (arguments[name].shape, HALF) for name in fetched
    }
    scratch.update({
        "pixels": (halo, HALF), "views": ((3,) + halo, HALF), "feat": ((TOK, channels), FULL),
        "tap_sum": ((TOK, 128), FULL), "sums": ((n_band, 2 * images, channels), FULL), "sums_back": ((n_band, 2 * images, channels), FULL),
        "zhat": ((TOK, channels), FULL), "active": ((TOK, channels), HALF), "slope": ((TOK, channels), FULL),
        "embedded": (split, HALF), "patches": (split, HALF), "stream": ((TOK, D), FULL), "nhat_one": ((TOK, D), FULL),
        "rstd_one": ((TOK, 1), FULL), "hidden": ((TOK, D), HALF), "qkv": ((TOK, 3 * D), HALF), "probs": ((HEADS, TOK, TOK), HALF),
        "mixed": ((TOK, D), HALF), "nhat_two": ((TOK, D), FULL), "rstd_two": ((TOK, 1), FULL),
        "hidden2": ((TOK, D), HALF), "cot": ((TOK, D), HALF), "final": ((TOK, D), FULL),
        "act": ((4, TOK, D), HALF), "d_pre": ((4, TOK, D), HALF), "up_sum": ((FF // D, 1, D), FULL), "vec": (vec_shape, FULL),
        "d_attn": ((TOK, D), HALF), "d_mixed": ((TOK, D), HALF), "d_qkv": ((TOK, 3 * D), HALF),
        "d_patches": (split, HALF), "d_cells": (split, HALF), "d_feat": ((TOK, channels), HALF), "d_rows": (halo, HALF),
        "d_views": ((3,) + halo, HALF), "mixed_bands": ((4, TOK, 256), HALF), "d_qkv_bands": ((4, TOK, D), HALF), "t_cot": ((D, 2 * TOK), HALF), "t_hidden": ((D, 2 * TOK), HALF), "t_hidden2": ((D, 2 * TOK), HALF), "t_attn": ((D, 2 * TOK), HALF), "slopes": ((4, TOK, D), HALF),
        "r_act": ((2, TOK, D), HALF), "r_d_pre": ((2, TOK, D), HALF),
        "r_d_qkv": ((2, TOK, D), HALF), "r_mixed": ((2, TOK, 256), HALF),
        "r_views": ((3,) + halo, HALF), "r_d_feat": ((TOK, channels), HALF), "r_active": ((TOK, channels), HALF), "r_d_cells": (split, HALF),
    })
    slots = 32
    for name, (plan, _, _) in plans.items():
        for k, shape in enumerate(plan.scratch()):
            scratch[f"{name}_{k}"] = (shape, HALF)
        slots += len(plan.order)
    n_links = 2 + len(img_bits)
    scratch["vec_sum"] = ((n_links,) + vec_shape, FULL)
    scratch["vec_in"] = ((n_links,) + vec_shape, FULL)
    slots += n_links
    sems = {"fetch_sem": 8, "send_sem": slots, "recv_sem": slots}
    names = list(arguments) + list(results) + list(scratch) + list(sems)
    whole = lambda space: pl.BlockSpec(memory_space=space)
    outs = pl.pallas_call(
        functools.partial(layer_kernel, names, plans),
        out_shape=[jax.ShapeDtypeStruct(*v) for v in results.values()],
        in_specs=[whole(spaces.get(name, pltpu.VMEM)) for name in arguments],
        out_specs=[whole(pltpu.VMEM)] * len(results),
        scratch_shapes=[pltpu.VMEM(*v) for v in scratch.values()] + [pltpu.SemaphoreType.DMA((n,)) for n in sems.values()],
        compiler_params=pltpu.CompilerParams(collective_id=0, has_side_effects=True, vmem_limit_bytes=63 * 2**20),
    )(*arguments.values())
    finished = {
        "encoded": (cotangent.shape, HALF),
        "image_grad": (arguments["image"].shape, FULL),
        "text_grad": (text_embed.shape, FULL),
        "conv": ((channels // n_band, taps // n_img), FULL),
        "gn_gain": ((channels // n_img,), FULL),
        "gn_bias": ((channels // n_img,), FULL),
        "emb": ((channels // n_img, D // n_band), FULL),
        "embed_bias": ((D // n_img,), FULL),
        "ln1_gain": ((D // n_img,), FULL),
        "ln1_bias": ((D // n_img,), FULL),
        "qkv": ((D // n_img, 3 * D // n_band), FULL),
        "query_bias": ((D // n_img,), FULL),
        "value_bias": ((D // n_img,), FULL),
        "out": ((D // n_band, D // n_img), FULL),
        "out_bias": ((D // n_img,), FULL),
        "ln2_gain": ((D // n_img,), FULL),
        "ln2_bias": ((D // n_img,), FULL),
        "up": ((D // n_img, FF // n_band), FULL),
        "up_bias": ((FF // n_img,), FULL),
        "down": ((D // n_img, FF // n_band), FULL),
        "down_bias": ((D // n_img,), FULL),
    }
    names = ["i_" + name for name in results] + list(finished)
    outs = pl.pallas_call(
        functools.partial(finish_kernel, names),
        out_shape=[jax.ShapeDtypeStruct(*v) for v in finished.values()],
        in_specs=[whole(pltpu.VMEM)] * len(results),
        out_specs=[whole(pltpu.VMEM)] * len(finished),
    )(*outs)
    res = dict(zip(finished, outs))
    res["conv"], res["down"] = res["conv"].T, res["down"].T
    res["image_grad"] = res["image_grad"].transpose(0, 2, 1, 3)
    return tuple(res.values())


def solution(mesh):
    in_specs = (
        P("img", "band", None, None),
        P(),
        P(),
        P(),
        P(),
        P(),
        P(),
        P(),
        P(),
        P(),
        P(),
        P(),
        P(),
        P(),
        P(),
        P(),
        P(),
        P(),
        P(),
        P(("img", "band"), None, None),
        P(("img", "band")),
        P(("img", "band"), None, None),
    )
    out_specs = (
        P(("img", "band"), None, None),
        P("img", "band", None, None),
        P(("img", "band"), None, None),
        P("img", "band"),
        P("img"),
        P("img"),
        P("img", "band"),
        P("img"),
        P("img"),
        P("img"),
        P("img", "band"),
        P("img"),
        P("img"),
        P("band", "img"),
        P("img"),
        P("img"),
        P("img"),
        P("img", "band"),
        P("img"),
        P("band", "img"),
        P("img"),
    )
    return jax.shard_map(body, mesh=mesh, in_specs=in_specs, out_specs=out_specs, check_vma=False)
```

```python
import functools
import types

import jax
import jax.numpy as jnp
from jax import lax
from jax.experimental import pallas as pl
from jax.experimental.pallas import tpu as pltpu
from jax.sharding import PartitionSpec as P

D = 768
FF = 3072
HEADS = 12
GROUPS = 32
GRID = 14
TEXT = 32
PATCHES = 196
WIDE = 16
TOK = 256
CELLS = GRID * WIDE
HALF = jnp.bfloat16
FULL = jnp.float32
MESH_ID = pl.DeviceIdType.MESH
CORE = ("band", 1)
FAR = ("band", 2)


def bit_of(value, bit):
    return lax.rem(lax.div(value, bit), 2)


def flip(value, bit):
    return value + bit * (1 - 2 * bit_of(value, bit))


def partner(label):
    axis, bit = label
    img, band = lax.axis_index("img"), lax.axis_index("band")
    return (flip(img, bit), band) if axis == "img" else (img, flip(band, bit))


def my_bit(label):
    axis, bit = label
    return bit_of(lax.axis_index(axis), bit)


def bits(count):
    return [1 << k for k in range(count.bit_length() - 1)]


def route(letters, n_img):
    near = [("img", k) for k in bits(n_img)]
    routes = {"c": [CORE], "y": [FAR], "Y": [FAR], "x": near[:1], "z": near[1:2], "w": near[2:]}
    return sum((routes[letter] for letter in letters), [])


class Plan:
    def __init__(self, n_img, rows, width, lead, order, parts=1):
        self.width = width
        split = [("img", k) for k in reversed(bits(n_img)) if (rows // n_img) * k % 16 == 0]
        self.rows = (rows >> len(split)) // parts
        self.first = ([lead] if lead else []) + split
        rest = [("img", k) for k in bits(n_img) if ("img", k) not in split]
        self.order = [lab for lab in order if lab not in rest] + rest
        self.shapes = []
        labels = list(self.first)
        for lab in self.order:
            if lab in labels:
                labels.remove(lab)
            self.shapes.append((2,) * len(labels) + (self.rows, width))
        self.shape = (2,) * len(self.first) + (self.rows, width)

    def scratch(self):
        return [self.shape] + self.shapes


class Once:
    def __init__(self, copy):
        self.copy, self.left = copy, {"wait", "wait_send", "wait_recv"}
        copy.start()

    def _wait(self, kind):
        if kind in self.left:
            self.left.remove(kind)
            getattr(self.copy, kind)()

    def wait(self):
        self._wait("wait")

    def wait_send(self):
        self._wait("wait_send")

    def wait_recv(self):
        self._wait("wait_recv")


class Piece:
    def __init__(self, plan, refs, sems, slot, out, at, pending):
        self.pending = pending
        self.plan, self.buf, self.recv = plan, refs[0], refs[1:]
        self.sems, self.slot = sems, slot
        self.labels, self.cur = list(plan.first), refs[0]
        self.sent = []
        self.out = out.at[pl.ds(at[0], plan.rows), pl.ds(at[1], plan.width)]
        self.stage = 0

    def _index(self, label, which):
        at = self.labels.index(label)
        return (slice(None),) * at + (which,)

    def start(self):
        label = self.plan.order[self.stage]
        src = self.cur
        if label in self.labels:
            src = src.at[self._index(label, 1 - my_bit(label))]
        send, recv = self.sems
        copy = pltpu.make_async_remote_copy(
            src_ref=src,
            dst_ref=self.recv[self.stage],
            send_sem=send.at[self.slot + self.stage],
            recv_sem=recv.at[self.slot + self.stage],
            device_id=partner(label),
            device_id_type=MESH_ID,
        )
        self.sent.append(Once(copy))
        self.pending.append(self.sent[-1])

    def step(self):
        label = self.plan.order[self.stage]
        self.sent[self.stage].wait_recv()
        mine = self.cur
        if label in self.labels:
            mine = mine[self._index(label, my_bit(label))]
            self.labels.remove(label)
        else:
            mine = mine[...]
        got = self.recv[self.stage]
        self.stage += 1
        if self.stage == len(self.plan.order):
            self.out[...] = (got[...].astype(FULL) + mine.astype(FULL)).reshape(self.out.shape)
        else:
            got[...] = got[...] + mine
            self.cur = got
            self.start()


def dot(left, right):
    return jnp.dot(left, right, preferred_element_type=FULL)


def dot_tn(left, right):
    return lax.dot_general(left, right, (((0,), (0,)), ((), ())), preferred_element_type=FULL)


def dot_nt(left, right):
    return lax.dot_general(left, right, (((1,), (1,)), ((), ())), preferred_element_type=FULL)


def exact_dot(left, right):
    return jnp.dot(left, right, precision=lax.Precision.HIGHEST, preferred_element_type=FULL)


def gelu_parts(x):
    cdf = 0.5 + 0.5 * lax.erf(x * 0.7071067811865476)
    pdf = jnp.exp(-0.5 * x * x) * 0.3989422804014327
    return x * cdf, cdf + x * pdf


def iota(shape, axis):
    return lax.broadcasted_iota(jnp.int32, shape, axis)


def row(ref):
    return ref[...].reshape(1, -1)


def column_sum(values):
    return jnp.sum(values, 0, keepdims=True)


def shifted(values):
    edge = jnp.zeros(values.shape[:2] + (1, values.shape[3]), FULL)
    left = jnp.concatenate([edge, values[:, :, : WIDE - 1]], 2)
    right = jnp.concatenate([values[:, :, 1:], edge], 2)
    return left, values, right


DOWN, UP, QKV = (tuple(f"p_{unit}{k}" for k in range(3)) for unit in "duq")
ORDERS = {
    "p_d0": "xzwy",
    "p_d1": "yzxw",
    "p_d2": "zxyw",
    "p_u0": "yxzw",
    "p_u1": "xyzw",
    "p_u2": "wyxz",
    "p_q0": "yxzw",
    "p_q1": "xzyw",
    "p_q2": "yxzw",
    "p_c0": "xzYw",
    "p_c1": "xwzY",
    "p_c2": "xzwY",
    "p_e": "zxwY",
    "vec": "zwycx",
}
POLLS = {
    "back1": (
        "p_d0",
        "p_d1",
        "p_d2",
    ),
    "cells": (
        "qkv",
        "+p_q1",
        "p_u1",
        "p_u0",
    ),
    "sums": (
        "p_d2",
        "p_d0",
    ),
    "edges": (
        "+p_q2",
        "+p_q0",
        "p_u1",
        "p_u2",
        "p_d1",
        "p_d2",
    ),
    "grad": (
        "p_q1",
        "vec",
        "p_d0",
    ),
    "end": (
        "p_u1",
        "p_u0",
        "p_d2",
        "p_d1",
        "p_q2",
        "p_q1",
        "p_c0",
        "vec",
        "p_c1",
        "p_e",
        "p_c2",
        "p_u1",
        "p_u0",
        "p_q0",
        "p_c0",
        "p_d1",
        "p_q2",
        "p_e",
        "p_c2",
        "p_c1",
        "p_u2",
        "p_u0",
        "p_d0",
        "p_q2",
        "p_q0",
        "p_e",
        "p_q1",
        "p_c2",
        "p_c1",
        "p_u2",
        "vec",
        "p_c0",
        "p_q2",
        "p_e",
        "vec",
        "p_c2",
        "p_q0",
        "p_c1",
        "p_u2",
        "p_q1",
        "vec",
        "p_c0",
        "p_q0",
    ),
}


def layer_kernel(names, plans, *refs):
    r = types.SimpleNamespace(**dict(zip(names, refs)))
    img, band = lax.axis_index("img"), lax.axis_index("band")
    n_img, n_band = lax.axis_size("img"), lax.axis_size("band")
    images, _, rows = r.image.shape[:3]
    channels = r.conv_weight.shape[1]
    core = my_bit(CORE)
    others = [lax.rem(band + d, n_band) for d in range(n_band)]

    fetches = {}

    def fetch(name, at):
        copy = pltpu.make_async_copy(getattr(r, name), getattr(r, "v_" + name), r.fetch_sem.at[at])
        fetches[name] = Once(copy)

    for at, name in enumerate(("cotangent", "conv_weight", "embed_weight", "qkv_weight", "text_embed", "out_weight", "up_weight", "down_weight")):
        fetch(name, at)

    links = [CORE, FAR] + [("img", k) for k in bits(n_img)]
    barrier = pltpu.get_barrier_semaphore()
    for d in range(1, n_band):
        pl.semaphore_signal(barrier, inc=1, device_id=(img, others[d]), device_id_type=MESH_ID)
    for label in links[2:]:
        pl.semaphore_signal(barrier, inc=1, device_id=partner(label), device_id_type=MESH_ID)

    pending = []

    def send(src, dst, at, device):
        copy = pltpu.make_async_remote_copy(
            src_ref=src, dst_ref=dst, send_sem=r.send_sem.at[at], recv_sem=r.recv_sem.at[at],
            device_id=device, device_id_type=MESH_ID)
        pending.append(Once(copy))
        return pending[-1]

    def edge_rows(ref, at):
        up = send(ref.at[:, rows], ref.at[:, 0], at, (img, others[1]))
        down = send(ref.at[:, 1], ref.at[:, rows + 1], at + 1, (img, others[n_band - 1]))
        return up, down

    def edges_in(ref, copies):
        for copy in copies:
            copy.wait_recv()
        values = ref[...].astype(FULL)
        at = iota(values.shape, 1) + band * rows
        return jnp.where((at == 0) | (at > n_band * rows), 0.0, values)

    def exchange(values, slots, at, meanwhile=None):
        slots[0] = values
        copies = [send(slots.at[0], slots.at[d], at + d - 1, (img, others[d])) for d in range(1, n_band)]
        poll(meanwhile)
        for d, copy in enumerate(copies, 1):
            copy.wait_recv()
            values = values + slots[d]
        return values

    def to_owners(src, dst, at, meanwhile=None):
        copies = [send(src.at[others[d]], dst.at[band], at + d - 1, (img, others[d])) for d in range(1, n_band)]
        dst[band] = src[band]
        poll(meanwhile)
        for copy in copies:
            copy.wait_recv()

    swaps = {}
    base = 16

    def swap(name, at, src, dst):
        swaps.setdefault(name, []).append(send(src, dst, base + at, partner(CORE)))

    def swap_bands(name, at, src, dst):
        for y in range(2):
            swap(name, at + y, src.at[2 * y + 1 - core], dst.at[y])

    def swap_left(name, at, ref):
        swap(name, at, ref.at[:, pl.ds(0, TOK)], ref.at[:, pl.ds(TOK, TOK)])

    def arrived(name):
        for copy in swaps[name]:
            copy.wait_recv()

    pieces = {}
    slot = base + 16
    for name, (plan, out, at) in plans.items():
        refs = [getattr(r, f"{name}_{k}") for k in range(1 + len(plan.order))]
        pieces[name] = Piece(plan, refs, (r.send_sem, r.recv_sem), slot, getattr(r, out), at, pending)
        slot += len(plan.order)

    down, up, qkv = DOWN, UP, QKV

    def poll(point):
        for name in POLLS.get(point, ()):
            if name[0] == "+":
                pieces[name[1:]].start()
            elif name == "vec":
                vec_step()
            elif name == "qkv":
                qkv_unit()
            else:
                advance(name)

    def advance(*names):
        for name in names:
            if pieces[name].stage < len(pieces[name].plan.order):
                pieces[name].step()

    def unit(parts, terms, start=True):
        for j, name in enumerate(parts):
            piece = pieces[name]
            wide = slice(256 * j, 256 * (j + 1))
            for y in range(2):
                value = 0.0
                for left, right, got, at in terms:
                    if j >= at:
                        cut = slice(256 * (j - at), 256 * (j - at + 1))
                        both = jnp.concatenate([right[2 * y + core, :, cut], got[y, :, cut]], 0)
                        value = value + dot(left[...], both)
                piece.buf[y] = value.astype(HALF).reshape(piece.plan.shape[1:])
            if start:
                piece.start()

    r.pixels[:, 1 : rows + 1, GRID:, :] = jnp.zeros((images, rows, WIDE - GRID, channels), HALF)
    for k in range(rows):
        line = r.image[:, :, k, :].astype(FULL)
        r.pixels[:, k + 1, :GRID, :] = jnp.where(band * rows + k < GRID, line, 0.0).astype(HALF)
    fetches["cotangent"].wait()
    seq = r.cotangent.shape[1]

    def token_of(at):
        return jnp.where(at < CELLS, jnp.where(lax.rem(at, WIDE) < GRID, lax.div(at, WIDE) * GRID + lax.rem(at, WIDE), -1), at - CELLS + PATCHES)

    spread = jnp.where(token_of(iota((TOK, seq), 0)) == iota((TOK, seq), 1), 1.0, 0.0).astype(HALF)
    gather = jnp.where(token_of(iota((seq, TOK), 1)) == iota((seq, TOK), 0), 1.0, 0.0).astype(HALF)
    r.cot[...] = dot(spread, r.v_cotangent[0]).astype(HALF)

    r.t_cot[:, :TOK] = r.cot[...].T
    pl.semaphore_wait(barrier, n_band - 1 + len(links) - 2)
    copies = edge_rows(r.pixels, 0)

    swap_left("down", 0, r.t_cot)

    fetches["conv_weight"].wait()
    taps = r.conv_weight.shape[0]
    chunks = [slice(k, k + 256) for k in range(0, taps, 256)]
    wmean = sum(column_sum(r.v_conv_weight[s].astype(FULL)) for s in chunks) * (1.0 / taps)
    wvar = 0.0
    for s in chunks:
        cent = r.v_conv_weight[s].astype(FULL) - wmean
        wvar = wvar + column_sum(cent * cent)
    wscale = lax.rsqrt(wvar * (1.0 / taps) + 1e-05)
    taps_here = taps // n_img
    if taps_here % 16 == 0:
        own = r.v_conv_weight[pl.ds(pl.multiple_of(img * taps_here, 16), taps_here)]
    else:
        own = jnp.where(iota((taps_here, taps), 1) == iota((taps_here, taps), 0) + img * taps_here, 1.0, 0.0).astype(HALF)
        own = dot(own, r.v_conv_weight[...]).astype(HALF)
    own = ((own.astype(FULL) - wmean) * wscale, jnp.broadcast_to(wscale, (8, channels)))
    r.o_wstat[...] = jnp.concatenate(own, 0)
    for s in chunks:
        r.v_conv_weight[s] = ((r.v_conv_weight[s].astype(FULL) - wmean) * wscale).astype(HALF)
    pixels = edges_in(r.pixels, copies)
    for e, values in enumerate(shifted(pixels)):
        r.views[e] = values.astype(HALF)

    def window(views, a, e):
        return views[e, :, a : a + rows].reshape(TOK, channels)

    place = iota((TOK, channels), 0)
    live = (lax.rem(place, WIDE) < GRID) & (lax.rem(lax.div(place, WIDE), rows) + band * rows < GRID)
    feat = 0.0
    tap_sum = 0.0
    for a in range(3):
        for e in range(3):
            seen = window(r.views, a, e)
            feat = feat + dot(seen, r.v_conv_weight[(3 * a + e) * channels : (3 * a + e + 1) * channels])
            tap_sum = tap_sum + seen.astype(FULL)
    feat = jnp.where(live, feat, 0.0)
    r.feat[...] = feat
    r.tap_sum[...] = jnp.broadcast_to(jnp.sum(tap_sum, 1, keepdims=True), (TOK, 128))
    per_group = channels // GROUPS
    entries = 1.0 / (GRID * GRID * per_group)
    same = lax.div(iota((channels, channels), 0), per_group) == lax.div(iota((channels, channels), 1), per_group)
    same = jnp.where(same, 1.0, 0.0)
    cells = TOK // images

    def image_sums(one, two):
        one = jnp.sum(one.reshape(images, cells, channels), 1)
        two = jnp.sum(two.reshape(images, cells, channels), 1)
        return exact_dot(jnp.concatenate([one, two], 0), same)

    def per_image(sums, which):
        return sums[which * images : (which + 1) * images].reshape(images, 1, channels)
    sums = exchange(image_sums(feat, feat * feat), r.sums, 2) * entries
    gmean = per_image(sums, 0)
    gscale = lax.rsqrt(per_image(sums, 1) - gmean * gmean + 1e-05)
    zhat = ((feat.reshape(images, cells, channels) - gmean) * gscale).reshape(TOK, channels)
    r.zhat[...] = zhat
    stem, slope = gelu_parts(zhat * row(r.gn_gain) + row(r.gn_bias))
    r.active[...] = jnp.where(live, stem, 0.0).astype(HALF)
    r.slope[...] = jnp.where(live, slope, 0.0)
    fetches["embed_weight"].wait()
    embedded = dot(r.active[...], r.v_embed_weight[...]) + row(r.embed_bias)
    r.embedded[...] = embedded.astype(HALF).reshape(images, cells, D)
    to_owners(r.embedded, r.patches, 5)
    swap("conv", 12, r.views, r.r_views)
    swap("emb", 14, r.active, r.r_active)
    def norm(values):
        mean = jnp.mean(values, -1, keepdims=True)
        cent = values - mean
        rstd = lax.rsqrt(jnp.mean(cent * cent, -1, keepdims=True) + 1e-06)
        return cent * rstd, rstd

    def norm_back(grad, nhat, rstd, gain):
        s = grad * gain
        inner = s - jnp.mean(s, -1, keepdims=True) - nhat * jnp.mean(s * nhat, -1, keepdims=True)
        return inner * rstd

    fetches["text_embed"].wait()
    r.stream[...] = r.patches[...].reshape(TOK, D).astype(FULL)
    r.stream[CELLS:] = r.v_text_embed[0].astype(FULL)
    nhat, rstd_one = norm(r.stream[...])
    r.nhat_one[...] = nhat
    r.rstd_one[...] = rstd_one
    r.hidden[...] = (nhat * row(r.ln1_gain) + row(r.ln1_bias)).astype(HALF)
    fetches["qkv_weight"].wait()
    for k, bias in enumerate((r.query_bias, None, r.value_bias)):
        values = dot(r.hidden[...], r.v_qkv_weight[:, k * D : (k + 1) * D])
        if bias is not None:
            values = values + row(bias)
        values = values.astype(HALF)
        r.qkv[:, k * D : (k + 1) * D] = values * 0.125 if k == 0 else values
    key_at = iota((1, TOK), 1)
    key_live = ((key_at < CELLS) & (lax.rem(key_at, WIDE) < GRID)) | ((key_at >= CELLS) & (key_at - CELLS < r.text_len[0]))
    first = iota((TOK, 128), 1) < 64
    zero = jnp.zeros((TOK, 128), HALF)

    def pair_of(ref, k, p):
        return ref[:, k * D + p * 128 : k * D + (p + 1) * 128]

    def only(values, h):
        return jnp.where(first, values, zero) if h == 0 else jnp.where(first, zero, values)

    def attend(p):
        query, key, value = (pair_of(r.qkv, k, p) for k in range(3))
        sides = []
        for h in range(2):
            scores = jnp.where(key_live, dot_nt(only(query, h), key), -1000000000.0)
            expd = jnp.exp(scores - jnp.max(scores, -1, keepdims=True))
            probs = expd * (1.0 / jnp.sum(expd, -1, keepdims=True))
            probs = probs.astype(HALF)
            r.probs[2 * p + h] = probs
            sides.append(dot(probs, value))
        r.mixed[:, p * 128 : (p + 1) * 128] = jnp.where(first, *sides).astype(HALF)

    for p in range(HEADS // 2):
        attend(p)
    fetches["out_weight"].wait()
    mid = r.stream[...] + dot(r.mixed[...], r.v_out_weight[...]) + row(r.out_bias)
    r.final[...] = mid + row(r.down_bias)
    nhat, rstd_two = norm(mid)
    r.nhat_two[...] = nhat
    r.rstd_two[...] = rstd_two
    r.hidden2[...] = (nhat * row(r.ln2_gain) + row(r.ln2_bias)).astype(HALF)
    fetches["up_weight"].wait()

    for k in range(FF // D):
        wide = slice(k * D, (k + 1) * D)
        act, slope = gelu_parts(dot(r.hidden2[...], r.v_up_weight[:, wide]) + r.up_bias[:, wide])
        r.act[k] = act.astype(HALF)
        r.slopes[k] = slope.astype(HALF)
    swap_bands("down", 1, r.act, r.r_act)
    fetches["down_weight"].wait()
    final = r.final[...]
    for k in range(FF // D):
        final = final + dot(r.act[k], r.v_down_weight[k * D : (k + 1) * D])
    arrived("down")
    unit(down, [(r.t_cot, r.act, r.r_act, 0)])
    r.t_hidden2[:, :TOK] = r.hidden2[...].T
    swap_left("up", 3, r.t_hidden2)
    r.encoded[0] = dot(gather, final.astype(HALF)).astype(HALF)

    for k in range(FF // D):
        wide = slice(k * D, (k + 1) * D)
        d_pre = dot_nt(r.cot[...], r.v_down_weight[wide, :]) * r.slopes[k].astype(FULL)
        r.d_pre[k] = d_pre.astype(HALF)
        r.up_sum[k] = column_sum(r.d_pre[k].astype(FULL))
    swap_bands("up", 4, r.d_pre, r.r_d_pre)
    grad = 0.0
    for k in range(FF // D):
        grad = grad + dot_nt(r.d_pre[k], r.v_up_weight[:, k * D : (k + 1) * D])
    r.final[...] = grad
    def put(at, values, lo=0):
        r.vec[at : at + 1, lo : lo + values.shape[1]] = values

    r.vec[...] = jnp.zeros(r.vec.shape, FULL)
    cot = r.cot[...].astype(FULL)
    put(8, column_sum(cot))
    for k in range(FF // D):
        put(9 + k, r.up_sum[k])

    grad = r.final[...]
    put(6, column_sum(grad * r.nhat_two[...]))
    put(7, column_sum(grad))
    d_mid = cot + norm_back(grad, r.nhat_two[...], r.rstd_two[...], row(r.ln2_gain))
    r.stream[...] = d_mid
    r.d_attn[...] = d_mid.astype(HALF)
    r.t_attn[:, :TOK] = r.d_attn[...].T
    swap_left("out", 9, r.t_attn)
    put(5, column_sum(r.d_attn[...].astype(FULL)))
    r.d_mixed[...] = dot_nt(r.d_attn[...], r.v_out_weight[...]).astype(HALF)

    arrived("up")
    unit(up, [(r.t_hidden2, r.d_pre, r.r_d_pre, 0)])
    r.t_hidden[:, :TOK] = r.hidden[...].T
    swap_left("qkv", 6, r.t_hidden)
    for k in range(4):
        width = D // 4
        r.mixed_bands[k] = jnp.concatenate([jnp.zeros((TOK, 256 - width), HALF), r.mixed[:, k * width : (k + 1) * width]], 1)
    swap_bands("out", 10, r.mixed_bands, r.r_mixed)
    def attend_back(p):
        query, key, value = (pair_of(r.qkv, k, p) for k in range(3))
        d_mixed = pair_of(r.d_mixed, 0, p)
        sides = [[], [], []]
        for h in range(2):
            probs = r.probs[2 * p + h]
            d_probs = dot_nt(only(d_mixed, h), value)
            weight = probs.astype(FULL)
            delta = jnp.sum(d_probs * weight, -1, keepdims=True)
            d_scores = (weight * (d_probs - delta)).astype(HALF)
            sides[0].append(dot(d_scores, key) * 0.125)
            sides[1].append(dot_tn(d_scores, query))
            sides[2].append(dot_tn(probs, d_mixed))
        for k in range(3):
            r.d_qkv[:, k * D + p * 128 : k * D + (p + 1) * 128] = jnp.where(first, *sides[k]).astype(HALF)

    for p in range(HEADS // 2):
        attend_back(p)
        poll(f"back{p}")
    for k in range(4):
        width = 3 * D // 4
        r.d_qkv_bands[k] = jnp.concatenate([r.d_qkv[:, k * width : (k + 1) * width], jnp.zeros((TOK, D - width), HALF)], 1)
    swap_bands("qkv", 7, r.d_qkv_bands, r.r_d_qkv)
    put(3, column_sum(r.d_qkv[:, :D].astype(FULL)))
    put(4, column_sum(r.d_qkv[:, 2 * D :].astype(FULL)))
    grad = dot_nt(r.d_qkv[...], r.v_qkv_weight[...])
    put(1, column_sum(grad * r.nhat_one[...]))
    put(2, column_sum(grad))
    d_stream = r.stream[...] + norm_back(grad, r.nhat_one[...], r.rstd_one[...], row(r.ln1_gain))
    r.text_grad[0] = d_stream[CELLS:]
    at_cell = iota((TOK, D), 0) < CELLS
    r.d_patches[...] = jnp.where(at_cell, d_stream, 0.0).astype(HALF).reshape(r.d_patches.shape)
    def qkv_unit():
        arrived("qkv")
        arrived("out")
        unit(qkv, [(r.t_hidden, r.d_qkv_bands, r.r_d_qkv, 0), (r.t_attn, r.mixed_bands, r.r_mixed, 2)], False)
    to_owners(r.d_patches, r.d_cells, 8, "cells")
    swap("emb", 15, r.d_cells, r.r_d_cells)
    d_cells = r.d_cells[...].reshape(TOK, D)
    put(0, column_sum(d_cells.astype(FULL)))
    d_active = dot_nt(d_cells, r.v_embed_weight[...]).astype(HALF).astype(FULL)
    d_norm = d_active * r.slope[...]
    zhat = r.zhat[...]
    put(13, column_sum(d_norm * zhat))
    put(13, column_sum(d_norm), channels)
    d_hat = d_norm * row(r.gn_gain)
    back = exchange(image_sums(d_hat, d_hat * zhat), r.sums_back, 11, "sums") * entries
    d_feat = d_hat.reshape(images, cells, channels) - per_image(back, 0)
    d_feat = (d_feat - zhat.reshape(images, cells, channels) * per_image(back, 1)) * gscale
    d_feat = jnp.where(live, d_feat.reshape(TOK, channels), 0.0).astype(HALF)
    r.d_feat[...] = d_feat
    r.d_rows[:, 1 : rows + 1] = d_feat.reshape(images, rows, WIDE, channels)
    copies = edge_rows(r.d_rows, 14)
    swap("conv", 13, r.d_feat, r.r_d_feat)
    d_feat = d_feat.astype(FULL)
    put(13, column_sum(r.tap_sum[:, :1] * d_feat) * (1.0 / taps), 2 * channels)
    put(14, column_sum(r.feat[...] * d_feat) * (1.0 / taps))

    vec_links = route(ORDERS["vec"], n_img)

    def vec_start(stage):
        return send(r.vec if stage == 0 else r.vec_sum.at[stage - 1], r.vec_in.at[stage], slot + stage, partner(vec_links[stage]))

    vec_state = [r.vec[...], 0, vec_start(0)]

    def vec_step():
        total, stage, on_way = vec_state
        on_way.wait_recv()
        total = total + r.vec_in[stage]
        if stage == len(links) - 1:
            r.o_vec[...] = total
        else:
            r.vec_sum[stage] = total
            on_way = vec_start(stage + 1)
        vec_state[:] = [total, stage + 1, on_way]

    poll("edges")
    for e, values in enumerate(shifted(edges_in(r.d_rows, copies))):
        r.d_views[e] = values.astype(HALF)
    grad = 0.0
    for a in range(3):
        for e in range(3):
            seen = window(r.d_views, 2 - a, 2 - e)
            grad = grad + dot_nt(seen, r.v_conv_weight[(3 * a + e) * channels : (3 * a + e + 1) * channels])
    grad = jnp.where(live, grad, 0.0).reshape(images, rows, WIDE, channels)
    r.image_grad[...] = grad[:, :, :GRID]

    poll("grad")

    def columns(values, width):
        total = values.shape[1]
        col = iota((total, 2 * width), 1)
        want = jnp.where(col < width, col, col + width) + core * width
        pick = jnp.where(iota((total, 2 * width), 0) == want, 1.0, 0.0).astype(HALF)
        return dot(values, pick).astype(HALF)

    arrived("conv")
    mine, theirs = columns(r.d_feat[...], channels // 4), columns(r.r_d_feat[...], channels // 4)
    rows_here = pieces["p_c0"].plan.rows
    for a in range(3):
        for e in range(3):
            value = dot_tn(window(r.views, a, e), mine) + dot_tn(window(r.r_views, a, e), theirs)
            value = value.astype(HALF)
            begin = at = (3 * a + e) * channels
            while at < begin + channels:
                line, lo = divmod(at, rows_here)
                block, part = divmod(line, 3)
                size = min(begin + channels - at, rows_here - lo)
                piece = pieces[f"p_c{part}"]
                where = tuple(block >> k & 1 for k in reversed(range(len(piece.plan.first))))
                piece.buf[where + (slice(lo, lo + size),)] = value[at - begin : at - begin + size]
                at += size
    for part in range(3):
        pieces[f"p_c{part}"].start()
    arrived("emb")
    mine, theirs = columns(d_cells, D // 4), columns(r.r_d_cells[...].reshape(TOK, D), D // 4)
    piece = pieces["p_e"]
    value = dot_tn(r.active[...], mine) + dot_tn(r.r_active[...], theirs)
    piece.buf[...] = value.astype(HALF).reshape(piece.plan.shape)
    piece.start()
    poll("end")
    while vec_state[1] < len(links) or any(p.stage < len(p.plan.order) for p in pieces.values()):
        advance(*pieces)
        if vec_state[1] < len(links):
            vec_step()
    for copy in pending:
        copy.wait_send()


def finish_kernel(names, *refs):
    r = types.SimpleNamespace(**dict(zip(names, refs)))
    img, band = lax.axis_index("img"), lax.axis_index("band")
    n_img, n_band = lax.axis_size("img"), lax.axis_size("band")
    far = my_bit(FAR)
    r.encoded[...] = r.i_encoded[...]
    r.text_grad[...] = r.i_text_grad[...]
    for k in range(r.image_grad.shape[2]):
        r.image_grad[:, :, k, :] = r.i_image_grad[:, k]

    def own(ref, rows):
        if ref.shape[0] == rows:
            return ref[...]
        at = lax.rem(img, ref.shape[0] // rows) * rows
        pick = jnp.where(iota((rows, ref.shape[0]), 1) == iota((rows, ref.shape[0]), 0) + at, 1.0, 0.0)
        return exact_dot(pick, ref[...])

    def lanes(values, at, count):
        width = values.shape[1]
        return exact_dot(values, jnp.where(iota((width, count), 0) == iota((width, count), 1) + at, 1.0, 0.0))

    def half(values):
        width = values.shape[1] // 2
        return jnp.where(far == 0, values[:, :width], values[:, width:])

    share = D // n_img
    r.down[...] = own(r.i_o_down, share)
    r.up[...] = own(r.i_o_up, share)
    both = own(r.i_o_qkv, share)
    r.qkv[...] = both[:, : 3 * D // n_band]
    r.out[...] = both[:, 3 * D // n_band :].T
    vec = r.i_o_vec[...]
    channels = r.i_o_wstat.shape[1]
    r.emb[...] = half(own(r.i_o_emb, channels // n_img))
    mine = lanes(vec, img * share, share)
    for at, name in enumerate(("embed_bias", "ln1_gain", "ln1_bias", "query_bias", "value_bias", "out_bias", "ln2_gain", "ln2_bias", "down_bias")):
        getattr(r, name)[...] = mine[at]
    share = channels // n_img
    r.gn_gain[...] = lanes(vec[8:], img * share, share)[5]
    r.gn_bias[...] = lanes(vec[8:], channels + img * share, share)[5]
    share = FF // n_img
    start = img * share
    line = jnp.sum(jnp.where(iota(vec.shape, 0) == 9 + lax.div(start, D), vec, 0.0), 0, keepdims=True)
    r.up_bias[...] = lanes(jnp.broadcast_to(line, (8, D)), lax.rem(start, D), share)[0]
    cols = channels // n_band
    taps = r.conv.shape[1]
    stats = jnp.concatenate([vec[13:14, 2 * channels :], vec[14:15, :channels], r.i_o_wstat[taps:][:6]], 0)
    stats = lanes(stats, band * cols, cols)
    stand = lanes(r.i_o_wstat[:taps], band * cols, cols)
    grad = half(own(r.i_o_conv, taps)) - stats[0:1] - stand * stats[1:2]
    r.conv[...] = (grad * stats[2:3]).T


def body(
    image,
    conv_weight,
    gn_gain,
    gn_bias,
    embed_weight,
    embed_bias,
    ln1_gain,
    ln1_bias,
    qkv_weight,
    query_bias,
    value_bias,
    out_weight,
    out_bias,
    ln2_gain,
    ln2_bias,
    up_weight,
    up_bias,
    down_weight,
    down_bias,
    text_embed,
    text_len,
    cotangent,
):
    n_img, n_band = lax.axis_size("img"), lax.axis_size("band")
    img, band = lax.axis_index("img"), lax.axis_index("band")
    images, rows = image.shape[:2]
    taps, channels = conv_weight.shape
    img_bits = [("img", k) for k in bits(n_img)]
    plans = {}
    for name, order in ORDERS.items():
        if name == "vec":
            continue
        order = route(order, n_img)
        k = int(name[3:] or 0)
        if name in DOWN + UP + QKV:
            out = {"d": "o_down", "u": "o_up", "q": "o_qkv"}[name[2]]
            plans[name] = (Plan(n_img, D, 256, FAR, order), out, (0, 256 * k))
        elif name == "p_e":
            plans[name] = (Plan(n_img, channels, D // 2, None, order), "o_emb", (0, 0))
        else:
            plan = Plan(n_img, taps, channels // 2, None, order, 3)
            plans[name] = (plan, "o_conv", (k * plan.rows, 0))
    vec_shape = (16, D)
    arguments = {
        "image": image.transpose(0, 2, 1, 3), "conv_weight": conv_weight, "gn_gain": gn_gain, "gn_bias": gn_bias, "embed_weight": embed_weight,
        "embed_bias": embed_bias, "ln1_gain": ln1_gain, "ln1_bias": ln1_bias, "qkv_weight": qkv_weight, "query_bias": query_bias,
        "value_bias": value_bias, "out_weight": out_weight, "out_bias": out_bias, "ln2_gain": ln2_gain, "ln2_bias": ln2_bias,
        "up_weight": up_weight, "up_bias": up_bias.reshape(1, FF), "down_weight": down_weight, "down_bias": down_bias,
        "text_embed": text_embed, "text_len": text_len, "cotangent": cotangent,
    }
    fetched = ("cotangent", "conv_weight", "embed_weight", "qkv_weight", "text_embed", "out_weight", "up_weight", "down_weight")
    spaces = {name: pl.ANY for name in fetched}
    spaces["text_len"] = pltpu.SMEM
    results = {
        "encoded": (cotangent.shape, HALF),
        "image_grad": (image.shape, FULL),
        "text_grad": (text_embed.shape, FULL),
        "o_down": ((plans["p_d0"][0].rows, D), FULL),
        "o_up": ((plans["p_u0"][0].rows, D), FULL),
        "o_qkv": ((plans["p_q0"][0].rows, D), FULL),
        "o_conv": ((3 * plans["p_c0"][0].rows, channels // 2), FULL),
        "o_emb": ((plans["p_e"][0].rows, D // 2), FULL),
        "o_vec": (vec_shape, FULL),
        "o_wstat": ((taps // n_img + 8, channels), FULL),
    }
    halo = (images, rows + 2, WIDE, channels)
    split = (images, TOK // images, D)
    scratch = {
        "v_" + name: (arguments[name].shape, HALF) for name in fetched
    }
    scratch.update({
        "pixels": (halo, HALF), "views": ((3,) + halo, HALF), "feat": ((TOK, channels), FULL),
        "tap_sum": ((TOK, 128), FULL), "sums": ((n_band, 2 * images, channels), FULL), "sums_back": ((n_band, 2 * images, channels), FULL),
        "zhat": ((TOK, channels), FULL), "active": ((TOK, channels), HALF), "slope": ((TOK, channels), FULL),
        "embedded": (split, HALF), "patches": (split, HALF), "stream": ((TOK, D), FULL), "nhat_one": ((TOK, D), FULL),
        "rstd_one": ((TOK, 1), FULL), "hidden": ((TOK, D), HALF), "qkv": ((TOK, 3 * D), HALF), "probs": ((HEADS, TOK, TOK), HALF),
        "mixed": ((TOK, D), HALF), "nhat_two": ((TOK, D), FULL), "rstd_two": ((TOK, 1), FULL),
        "hidden2": ((TOK, D), HALF), "cot": ((TOK, D), HALF), "final": ((TOK, D), FULL),
        "act": ((4, TOK, D), HALF), "d_pre": ((4, TOK, D), HALF), "up_sum": ((FF // D, 1, D), FULL), "vec": (vec_shape, FULL),
        "d_attn": ((TOK, D), HALF), "d_mixed": ((TOK, D), HALF), "d_qkv": ((TOK, 3 * D), HALF),
        "d_patches": (split, HALF), "d_cells": (split, HALF), "d_feat": ((TOK, channels), HALF), "d_rows": (halo, HALF),
        "d_views": ((3,) + halo, HALF), "mixed_bands": ((4, TOK, 256), HALF), "d_qkv_bands": ((4, TOK, D), HALF), "t_cot": ((D, 2 * TOK), HALF), "t_hidden": ((D, 2 * TOK), HALF), "t_hidden2": ((D, 2 * TOK), HALF), "t_attn": ((D, 2 * TOK), HALF), "slopes": ((4, TOK, D), HALF),
        "r_act": ((2, TOK, D), HALF), "r_d_pre": ((2, TOK, D), HALF),
        "r_d_qkv": ((2, TOK, D), HALF), "r_mixed": ((2, TOK, 256), HALF),
        "r_views": ((3,) + halo, HALF), "r_d_feat": ((TOK, channels), HALF), "r_active": ((TOK, channels), HALF), "r_d_cells": (split, HALF),
    })
    slots = 32
    for name, (plan, _, _) in plans.items():
        for k, shape in enumerate(plan.scratch()):
            scratch[f"{name}_{k}"] = (shape, HALF)
        slots += len(plan.order)
    n_links = 2 + len(img_bits)
    scratch["vec_sum"] = ((n_links,) + vec_shape, FULL)
    scratch["vec_in"] = ((n_links,) + vec_shape, FULL)
    slots += n_links
    sems = {"fetch_sem": 8, "send_sem": slots, "recv_sem": slots}
    names = list(arguments) + list(results) + list(scratch) + list(sems)
    whole = lambda space: pl.BlockSpec(memory_space=space)
    outs = pl.pallas_call(
        functools.partial(layer_kernel, names, plans),
        out_shape=[jax.ShapeDtypeStruct(*v) for v in results.values()],
        in_specs=[whole(spaces.get(name, pltpu.VMEM)) for name in arguments],
        out_specs=[whole(pltpu.VMEM)] * len(results),
        scratch_shapes=[pltpu.VMEM(*v) for v in scratch.values()] + [pltpu.SemaphoreType.DMA((n,)) for n in sems.values()],
        compiler_params=pltpu.CompilerParams(collective_id=0, has_side_effects=True, vmem_limit_bytes=63 * 2**20),
    )(*arguments.values())
    finished = {
        "encoded": (cotangent.shape, HALF),
        "image_grad": (arguments["image"].shape, FULL),
        "text_grad": (text_embed.shape, FULL),
        "conv": ((channels // n_band, taps // n_img), FULL),
        "gn_gain": ((channels // n_img,), FULL),
        "gn_bias": ((channels // n_img,), FULL),
        "emb": ((channels // n_img, D // n_band), FULL),
        "embed_bias": ((D // n_img,), FULL),
        "ln1_gain": ((D // n_img,), FULL),
        "ln1_bias": ((D // n_img,), FULL),
        "qkv": ((D // n_img, 3 * D // n_band), FULL),
        "query_bias": ((D // n_img,), FULL),
        "value_bias": ((D // n_img,), FULL),
        "out": ((D // n_band, D // n_img), FULL),
        "out_bias": ((D // n_img,), FULL),
        "ln2_gain": ((D // n_img,), FULL),
        "ln2_bias": ((D // n_img,), FULL),
        "up": ((D // n_img, FF // n_band), FULL),
        "up_bias": ((FF // n_img,), FULL),
        "down": ((D // n_img, FF // n_band), FULL),
        "down_bias": ((D // n_img,), FULL),
    }
    names = ["i_" + name for name in results] + list(finished)
    outs = pl.pallas_call(
        functools.partial(finish_kernel, names),
        out_shape=[jax.ShapeDtypeStruct(*v) for v in finished.values()],
        in_specs=[whole(pltpu.VMEM)] * len(results),
        out_specs=[whole(pltpu.VMEM)] * len(finished),
    )(*outs)
    res = dict(zip(finished, outs))
    res["conv"], res["down"] = res["conv"].T, res["down"].T
    res["image_grad"] = res["image_grad"].transpose(0, 2, 1, 3)
    return tuple(res.values())


def solution(mesh):
    in_specs = (
        P("img", "band", None, None),
        P(),
        P(),
        P(),
        P(),
        P(),
        P(),
        P(),
        P(),
        P(),
        P(),
        P(),
        P(),
        P(),
        P(),
        P(),
        P(),
        P(),
        P(),
        P(("img", "band"), None, None),
        P(("img", "band")),
        P(("img", "band"), None, None),
    )
    out_specs = (
        P(("img", "band"), None, None),
        P("img", "band", None, None),
        P(("img", "band"), None, None),
        P("img", "band"),
        P("img"),
        P("img"),
        P("img", "band"),
        P("img"),
        P("img"),
        P("img"),
        P("img", "band"),
        P("img"),
        P("img"),
        P("band", "img"),
        P("img"),
        P("img"),
        P("img"),
        P("img", "band"),
        P("img"),
        P("band", "img"),
        P("img"),
    )
    return jax.shard_map(body, mesh=mesh, in_specs=in_specs, out_specs=out_specs, check_vma=False)
```
